32 devices in a mesh: dp: 16 (over z, y, x), mp: 2 (over core).
Axes of the slice: x: 2, y: 2, z: 4, core: 2. Of those that a mesh axis runs over, the one named last changes fastest.
Arguments:
- tokens: bfloat16 [32, 512, 1024], P('dp'), may hold values from -6 to 6
- text_states: bfloat16 [32, 256, 768], P('dp', 'mp'), may hold values from -6 to 6
- text_len: int32 [32], P('dp'), may hold values from 1 to 256, as said below
- frame_valid: int32 [32], P('dp'), may hold values from 256 to 512, as said below
- ln1_gain: bfloat16 [1024], replicated, may hold values from 0.5 to 1.5
- ln1_bias: bfloat16 [1024], replicated, may hold values from -1 to 1
- ln2_gain: bfloat16 [1024], replicated, may hold values from 0.5 to 1.5
- ln2_bias: bfloat16 [1024], replicated, may hold values from -1 to 1
- ln3_gain: bfloat16 [1024], replicated, may hold values from 0.5 to 1.5
- ln3_bias: bfloat16 [1024], replicated, may hold values from -1 to 1
- w_query: bfloat16 [1024, 1024], P(None, 'mp'), may hold values from -0.1875 to 0.1875
- w_key: bfloat16 [1024, 1024], P(None, 'mp'), may hold values from -0.1875 to 0.1875
- w_value: bfloat16 [1024, 1024], P(None, 'mp'), may hold values from -0.1875 to 0.1875
- w_out: bfloat16 [1024, 1024], P('mp'), may hold values from -0.75 to 0.75
- c_query: bfloat16 [1024, 1024], P(None, 'mp'), may hold values from -0.1875 to 0.1875
- c_key: bfloat16 [768, 1024], P(None, 'mp'), may hold values from -0.21875 to 0.21875
- c_value: bfloat16 [768, 1024], P(None, 'mp'), may hold values from -0.21875 to 0.21875
- c_out: bfloat16 [1024, 1024], P('mp'), may hold values from -0.5 to 0.5
- w_up: bfloat16 [1024, 4096], P(None, 'mp'), may hold values from -0.1875 to 0.1875
- w_down: bfloat16 [4096, 1024], P('mp'), may hold values from -0.09375 to 0.09375
- grad_out: bfloat16 [32, 512, 1024], P('dp', 'mp'), may hold values from -6 to 6
Outputs:
- out: bfloat16 [32, 512, 1024], P('dp', 'mp')
- d_tokens: float32 [32, 512, 1024], P('dp', 'mp')
- d_text_states: float32 [32, 256, 768], P('dp', 'mp')
- d_ln1_gain: float32 [1024], replicated
- d_ln1_bias: float32 [1024], replicated
- d_ln2_gain: float32 [1024], replicated
- d_ln2_bias: float32 [1024], replicated
- d_ln3_gain: float32 [1024], replicated
- d_ln3_bias: float32 [1024], replicated
- d_w_query: float32 [1024, 1024], P(None, 'mp')
- d_w_key: float32 [1024, 1024], P(None, 'mp')
- d_w_value: float32 [1024, 1024], P(None, 'mp')
- d_w_out: float32 [1024, 1024], P('mp')
- d_c_query: float32 [1024, 1024], P(None, 'mp')
- d_c_key: float32 [768, 1024], P(None, 'mp')
- d_c_value: float32 [768, 1024], P(None, 'mp')
- d_c_out: float32 [1024, 1024], P('mp')
- d_w_up: float32 [1024, 4096], P(None, 'mp')
- d_w_down: float32 [4096, 1024], P('mp')
- rms_stats: float32 [4], replicated
The draws below stay inside these ranges and needn't reach their ends.
Inputs may be any that keep to these rules, and one draw needn't show every extreme that they name: `text_len`: mostly short; the first item of each aligned block of 8 items has 256 tokens. `frame_valid`: the first item of each aligned block of 8 items has all 512 frames valid.
All inputs are finite; a program needn't handle non-finite values.
Results may differ from the reference program's by a relative error of at most 0.023.
Values may be sent and summed in bfloat16 or wider, within the bound.
No kernel may reach another device: no remote copies, remote signals or barrier semaphores. Data moves between devices by JAX's collectives and lax.ppermute only.
A program may use at most 256 MiB of HBM per device.

```python
import jax
import jax.numpy as jnp
from jax import lax

D = 1024
H = 16
HD = 64
FF = 4096
DT = 768
FRAMES = 512
TEXT = 256
ITEMS = 32


def draw_text_len(key, part):
    first_key = jax.random.fold_in(key, 11)
    second_key = jax.random.fold_in(key, 12)
    third_key = jax.random.fold_in(key, 13)
    first_draw = jax.random.randint(first_key, (ITEMS,), 1, TEXT + 1)
    second_draw = jax.random.randint(second_key, (ITEMS,), 1, TEXT + 1)
    third_draw = jax.random.randint(third_key, (ITEMS,), 1, TEXT + 1)
    shorter = jnp.minimum(jnp.minimum(first_draw, second_draw), third_draw)
    leading = jnp.arange(ITEMS) % 8 == 0
    return jnp.where(leading, TEXT, shorter).astype(jnp.int32)


def draw_frame_valid(key, part):
    frame_key = jax.random.fold_in(key, 21)
    counts = jax.random.randint(frame_key, (ITEMS,), FRAMES // 2, FRAMES + 1)
    leading = jnp.arange(ITEMS) % 8 == 0
    return jnp.where(leading, FRAMES, counts).astype(jnp.int32)


def block_scale(key, shape, split, least, high):
    level, own = 1.0, jax.random.fold_in(key, 6)
    for position, parts in split:
        heights = jnp.exp(jax.random.uniform(jax.random.fold_in(own, position), (parts,), jnp.float32, least / len(split), high / len(split)))
        level = level * jnp.repeat(heights, shape[position] // parts).reshape([-1 if axis == position else 1 for axis in range(len(shape))])
    return level


def normal_values(own_key, shape, deviation, limit, shards=(), kind=jnp.bfloat16):
    values = jax.random.normal(own_key, shape, jnp.float32) * deviation
    if len(shards) > 0:
        values = block_scale(own_key, shape, shards, -0.22, 0.18) * values
    return jnp.clip(values, min=-limit, max=limit).astype(kind)


def setup_inputs(seed: int = 0) -> dict:
    keys = jax.random.split(jax.random.key(seed), 22)
    tokens = normal_values(keys[0], (ITEMS, FRAMES, D), 1.0, 6.0, ((0, 16),))
    text_states = normal_values(keys[1], (ITEMS, TEXT, DT), 1.0, 6.0, ((0, 16), (1, 2)))
    text_len = draw_text_len(jax.random.fold_in(keys[21], 71), 0)
    frame_valid = draw_frame_valid(jax.random.fold_in(keys[21], 71), 0)
    ln1_gain = jnp.clip(1.0 + 0.1 * jax.random.normal(keys[4], (D,), jnp.float32), 0.5, 1.5).astype(jnp.bfloat16)
    ln1_bias = normal_values(keys[5], (D,), 0.2, 1.0)
    ln2_gain = jnp.clip(1.0 + 0.1 * jax.random.normal(keys[6], (D,), jnp.float32), 0.5, 1.5).astype(jnp.bfloat16)
    ln2_bias = normal_values(keys[7], (D,), 0.2, 1.0)
    ln3_gain = jnp.clip(1.0 + 0.1 * jax.random.normal(keys[8], (D,), jnp.float32), 0.5, 1.5).astype(jnp.bfloat16)
    ln3_bias = normal_values(keys[9], (D,), 0.2, 1.0)
    w_query = normal_values(keys[10], (D, D), D ** -0.5, 0.1875, ((1, 2),))
    w_key = normal_values(keys[11], (D, D), D ** -0.5, 0.1875, ((1, 2),))
    w_value = normal_values(keys[12], (D, D), D ** -0.5, 0.1875, ((1, 2),))
    w_out = normal_values(keys[13], (D, D), (D // 16) ** -0.5, 0.75, ((0, 2),))
    c_query = normal_values(keys[14], (D, D), D ** -0.5, 0.1875, ((1, 2),))
    c_key = normal_values(keys[15], (DT, D), DT ** -0.5, 0.21875, ((1, 2),))
    c_value = normal_values(keys[16], (DT, D), DT ** -0.5, 0.21875, ((1, 2),))
    c_out = normal_values(keys[17], (D, D), (D // 8) ** -0.5, 0.5, ((0, 2),))
    w_up = normal_values(keys[18], (D, FF), D ** -0.5, 0.1875, ((1, 2),))
    w_down = normal_values(keys[19], (FF, D), FF ** -0.5, 0.09375, ((0, 2),))
    grad_out = normal_values(keys[20], (ITEMS, FRAMES, D), 1.0, 6.0, ((0, 16), (1, 2)))
    return dict(tokens=tokens, text_states=text_states, text_len=text_len, frame_valid=frame_valid, ln1_gain=ln1_gain, ln1_bias=ln1_bias, ln2_gain=ln2_gain, ln2_bias=ln2_bias, ln3_gain=ln3_gain, ln3_bias=ln3_bias, w_query=w_query, w_key=w_key, w_value=w_value, w_out=w_out, c_query=c_query, c_key=c_key, c_value=c_value, c_out=c_out, w_up=w_up, w_down=w_down, grad_out=grad_out)


@jax.custom_vjp
def low(v):
    return lax.optimization_barrier(v.astype(jnp.bfloat16)).astype(jnp.float32)

@jax.custom_vjp
def low_back(v):
    return v

def low_keep(v):
    return (low(v), None)

def low_pass(kept, grad):
    return (grad,)

def back_keep(v):
    return (v, None)

def back_low(kept, grad):
    return (low(grad),)
low.defvjp(low_keep, low_pass)
low_back.defvjp(back_keep, back_low)
norm_eps = 1e-05
score_scale = 0.125
masked_fill = -1e+30
highest_precision = lax.Precision.HIGHEST

def layer_norm(values, gain_vec, offset):
    average = lax.optimization_barrier(jnp.mean(values, -1, keepdims=True))
    centered = values - average
    variance = lax.optimization_barrier(jnp.mean(centered * centered, -1, keepdims=True))
    return centered * lax.rsqrt(variance + norm_eps) * gain_vec + offset

def matmul_rows(inputs, weight):
    return jnp.einsum('bfd,de->bfe', inputs, weight, precision=highest_precision)

def split_heads(values):
    return values.reshape(values.shape[0], values.shape[1], H, HD)

def attend(query_rows, key_rows, value_rows, allowed):
    scores = low_back(jnp.einsum('bfhd,bjhd->bhfj', query_rows, key_rows, precision=highest_precision) * score_scale)
    scores = jnp.where(allowed[:, None], scores, masked_fill)
    highest = lax.optimization_barrier(jnp.max(scores, -1, keepdims=True))
    powers = jnp.exp(scores - highest)
    attn_probs = powers / lax.optimization_barrier(jnp.sum(powers, -1, keepdims=True))
    mixture = jnp.einsum('bhfj,bjhd->bfhd', low(attn_probs), value_rows, precision=highest_precision)
    return low_back(low(mixture.reshape(mixture.shape[0], mixture.shape[1], D)))

def layer_forward(param_set, tok_in, text_in, allowed_self, allowed_cross):
    gain_one, bias_one, gain_two, bias_two, gain_three, bias_three, w_query, w_key, w_value, w_out, c_query, c_key, c_value, c_out, w_up, w_down = param_set
    normed_one = low(layer_norm(tok_in, gain_one, bias_one))
    query_rows = split_heads(low_back(low(matmul_rows(normed_one, w_query))))
    key_rows = split_heads(low_back(low(matmul_rows(normed_one, w_key))))
    value_rows = split_heads(low_back(low(matmul_rows(normed_one, w_value))))
    attn_out = low_back(matmul_rows(attend(query_rows, key_rows, value_rows, allowed_self), w_out))
    hidden_one = tok_in + attn_out
    normed_two = low(layer_norm(hidden_one, gain_two, bias_two))
    cross_query = split_heads(low_back(low(matmul_rows(normed_two, c_query))))
    cross_key = split_heads(low_back(low(matmul_rows(text_in, c_key))))
    cross_value = split_heads(low_back(low(matmul_rows(text_in, c_value))))
    cross_out = low_back(matmul_rows(attend(cross_query, cross_key, cross_value, allowed_cross), c_out))
    hidden_two = hidden_one + cross_out
    normed_three = low(layer_norm(hidden_two, gain_three, bias_three))
    activated = low(jax.nn.gelu(low_back(matmul_rows(normed_three, w_up)), approximate=False))
    ff_out = low_back(matmul_rows(activated, w_down))
    return (hidden_two + ff_out, (attn_out, cross_out, ff_out))

def reference(tokens, text_states, text_len, frame_valid, ln1_gain, ln1_bias, ln2_gain, ln2_bias, ln3_gain, ln3_bias, w_query, w_key, w_value, w_out, c_query, c_key, c_value, c_out, w_up, w_down, grad_out):
    params = tuple((weight.astype(jnp.float32) for weight in (ln1_gain, ln1_bias, ln2_gain, ln2_bias, ln3_gain, ln3_bias, w_query, w_key, w_value, w_out, c_query, c_key, c_value, c_out, w_up, w_down)))
    group_items = 8
    groups = ITEMS // group_items

    def regroup(array):
        return array.reshape((groups, group_items) + array.shape[1:])
    positions = jnp.arange(FRAMES)
    causal = positions[None, :] <= positions[:, None]
    text_positions = jnp.arange(TEXT)

    def one_group(carry, group):
        grad_sums, stat_sums = carry
        tok_group, text_group, len_group, valid_group, cot_group = group
        allowed_self = causal[None] & (positions[None, None, :] < valid_group[:, None, None])
        allowed_cross = jnp.broadcast_to(text_positions[None, None, :] < len_group[:, None, None], (group_items, FRAMES, TEXT))

        def forward(param_set, tok_in, text_in):
            return layer_forward(param_set, tok_in, text_in, allowed_self, allowed_cross)
        output, pullback, branches = jax.vjp(forward, params, tok_group.astype(jnp.float32), text_group.astype(jnp.float32), has_aux=True)
        grad_params, grad_tokens, grad_text = pullback(cot_group.astype(jnp.float32))
        row_valid = (positions[None, :] < valid_group[:, None]).astype(jnp.float32)[:, :, None]
        terms = jnp.stack([jnp.sum(row_valid * output * output)] + [jnp.sum(row_valid * branch_out * branch_out) for branch_out in branches] + [jnp.sum(row_valid) + jnp.float32(0.0)])
        new_carry = (jax.tree.map(jnp.add, grad_sums, grad_params), stat_sums + terms)
        return (new_carry, (output.astype(jnp.bfloat16), grad_tokens, grad_text))
    start = (jax.tree.map(jnp.zeros_like, params), jnp.zeros((5,), jnp.float32))
    inputs = (regroup(tokens), regroup(text_states), regroup(text_len), regroup(frame_valid), regroup(grad_out))
    (grad_params, stat_sums), (outputs, grad_tokens, grad_text) = lax.scan(one_group, start, inputs)
    rms_stats = jnp.sqrt(stat_sums[:4] / (stat_sums[4] * D))
    result = outputs.reshape(ITEMS, FRAMES, D)
    d_tokens = grad_tokens.reshape(ITEMS, FRAMES, D)
    d_text = grad_text.reshape(ITEMS, TEXT, DT)
    return (result, d_tokens, d_text) + tuple(grad_params) + (rms_stats,)
```

```python
from functools import partial

import jax
import jax.numpy as jnp
from jax import lax
from jax.sharding import PartitionSpec as P

HD = 64


norm_eps = 1e-05
score_scale = 0.125
masked_fill = -1e30


def layer_norm(values, gain_vec, offset):
    average = jnp.mean(values, -1, keepdims=True)
    centered = values - average
    variance = jnp.mean(centered * centered, -1, keepdims=True)
    return centered * lax.rsqrt(variance + norm_eps) * gain_vec + offset


def project(inputs, weight):
    return jnp.einsum("bfd,de->bfe", inputs, weight, preferred_element_type=jnp.float32)


def project_back(gradients, weight):
    return jnp.einsum("bfe,de->bfd", gradients, weight, preferred_element_type=jnp.float32)


def weight_grad(inputs, gradients):
    return jnp.einsum("bfd,bfe->de", inputs, gradients, preferred_element_type=jnp.float32)


def block_scores(query_rows, key_rows, allowed):
    scores = (
        jnp.einsum("fhd,jhd->hfj", query_rows, key_rows, preferred_element_type=jnp.float32)
        * score_scale
    )
    return jnp.where(allowed[None], scores, masked_fill)


def attend_forward(query_rows, key_rows, value_rows, allowed):
    scores = block_scores(query_rows, key_rows, allowed)
    highest = jnp.max(scores, -1, keepdims=True)
    powers = jnp.exp(scores - highest)
    row_total = jnp.sum(powers, -1, keepdims=True)
    attn_probs = powers / row_total
    mixture = jnp.einsum(
        "hfj,jhd->fhd",
        attn_probs.astype(jnp.bfloat16),
        value_rows,
        preferred_element_type=jnp.float32,
    )
    return (mixture.astype(jnp.bfloat16), highest + jnp.log(row_total), attn_probs)


def probs_again(query_rows, key_rows, allowed, log_total):
    return jnp.exp(block_scores(query_rows, key_rows, allowed) - log_total)


def attend_backward(query_rows, key_rows, value_rows, attn_probs, grad_mixture):
    grad_probs = jnp.einsum(
        "fhd,jhd->hfj", grad_mixture, value_rows, preferred_element_type=jnp.float32
    )
    grad_values = jnp.einsum(
        "hfj,fhd->jhd",
        attn_probs.astype(jnp.bfloat16),
        grad_mixture,
        preferred_element_type=jnp.float32,
    )
    inner_sum = jnp.sum(grad_probs * attn_probs, -1, keepdims=True)
    grad_scores = (attn_probs * (grad_probs - inner_sum)).astype(jnp.bfloat16)
    grad_queries = (
        jnp.einsum("hfj,jhd->fhd", grad_scores, key_rows, preferred_element_type=jnp.float32)
        * score_scale
    )
    grad_keys = (
        jnp.einsum("hfj,fhd->jhd", grad_scores, query_rows, preferred_element_type=jnp.float32)
        * score_scale
    )
    return (
        grad_queries.astype(jnp.bfloat16),
        grad_keys.astype(jnp.bfloat16),
        grad_values.astype(jnp.bfloat16),
    )


SWAP = [(0, 1), (1, 0)]


def swap_cores(values):
    return lax.ppermute(values, "mp", SWAP)


def sum_scatter(partial):
    rank = lax.axis_index("mp")
    half = partial.shape[1] // 2
    other = lax.dynamic_slice_in_dim(partial, (1 - rank) * half, half, 1)
    own = lax.dynamic_slice_in_dim(partial, rank * half, half, 1)
    received = swap_cores(other.astype(jnp.bfloat16))
    return own.astype(jnp.float32) + received.astype(jnp.float32)


def gather_halves(own):
    first = lax.axis_index("mp") == 0
    received = swap_cores(own)
    return jnp.concatenate(
        [jnp.where(first, own, received), jnp.where(first, received, own)], 1
    )


def bit_orders():
    bits = lax.axis_size("dp").bit_length() - 1
    along_x = (bits - 2) // 2
    x_bits = list(range(along_x))
    y_bits = list(range(along_x, bits - 2))
    z_bits = [bits - 2, bits - 1]
    return (x_bits + y_bits + z_bits, y_bits + x_bits + z_bits, z_bits + x_bits + y_bits)


def exchange(values, bit):
    pairs = [(d, d ^ (1 << bit)) for d in range(lax.axis_size("dp"))]
    return lax.ppermute(values, "dp", pairs)


def my_bit(bit):
    return (lax.axis_index("dp") >> bit) & 1


def sum_over_items(values, order):
    kept = values.astype(jnp.bfloat16)
    for bit in order:
        half = kept.shape[0] // 2
        side = my_bit(bit)
        send = lax.dynamic_slice_in_dim(kept, (1 - side) * half, half, 0)
        keep = lax.dynamic_slice_in_dim(kept, side * half, half, 0)
        received = exchange(send, bit)
        kept = (keep.astype(jnp.float32) + received.astype(jnp.float32)).astype(jnp.bfloat16)
    for bit in reversed(order):
        received = exchange(kept, bit)
        lower = my_bit(bit) == 0
        kept = jnp.concatenate(
            [jnp.where(lower, kept, received), jnp.where(lower, received, kept)], 0
        )
    return kept.astype(jnp.float32)


def sum_small(values):
    total = values + swap_cores(values)
    for bit in bit_orders()[0]:
        total = total + exchange(total, bit)
    return total


def fold_rows(values):
    half = values.shape[0] // 2
    return jnp.concatenate([values[:half], values[half:]], 1)


def unfold_rows(values):
    half = values.shape[1] // 2
    return jnp.concatenate([values[:, :half], values[:, half:]], 0)


def per_device(
    tokens,
    text_states,
    text_len,
    frame_valid,
    ln1_gain,
    ln1_bias,
    ln2_gain,
    ln2_bias,
    ln3_gain,
    ln3_bias,
    w_query,
    w_key,
    w_value,
    w_out,
    c_query,
    c_key,
    c_value,
    c_out,
    w_up,
    w_down,
    grad_out,
):
    items, frames, width = tokens.shape
    parts = lax.axis_size("mp")
    rank = lax.axis_index("mp")
    shard_rows = frames // parts
    text_rows = text_states.shape[1] * parts
    local_width = w_query.shape[1]
    heads_here = local_width // HD
    gain_one = ln1_gain.astype(jnp.float32)
    bias_one = ln1_bias.astype(jnp.float32)
    gain_two = ln2_gain.astype(jnp.float32)
    bias_two = ln2_bias.astype(jnp.float32)
    gain_three = ln3_gain.astype(jnp.float32)
    bias_three = ln3_bias.astype(jnp.float32)
    positions = jnp.arange(frames)
    causal = positions[None, :] <= positions[:, None]
    text_positions = jnp.arange(text_rows)

    def self_allowed(valid_count):
        return causal & (positions[None, :] < valid_count)

    def cross_allowed(length):
        return jnp.broadcast_to(text_positions[None, :] < length, (frames, text_rows))

    def self_forward(block):
        results = attend_forward(block[0], block[1], block[2], self_allowed(block[3]))
        return results[:2]

    def cross_forward(block):
        results = attend_forward(block[0], block[1], block[2], cross_allowed(block[3]))
        return results[:2]

    def self_backward(block):
        attn_probs = probs_again(block[0], block[1], self_allowed(block[3]), block[4])
        return attend_backward(block[0], block[1], block[2], attn_probs, block[5])

    def cross_backward(block):
        attn_probs = probs_again(block[0], block[1], cross_allowed(block[3]), block[4])
        return attend_backward(block[0], block[1], block[2], attn_probs, block[5])

    def to_heads(values, rows):
        return values.reshape(items, rows, heads_here, HD)

    tokens_full = tokens.astype(jnp.float32)
    normed_one = layer_norm(tokens_full, gain_one, bias_one).astype(jnp.bfloat16)
    w_joined = jnp.concatenate([w_query, w_key, w_value], 1)
    joined_rows = project(normed_one, w_joined).astype(jnp.bfloat16)
    query_self = to_heads(joined_rows[..., :local_width], frames)
    key_self = to_heads(joined_rows[..., local_width : 2 * local_width], frames)
    value_self = to_heads(joined_rows[..., 2 * local_width :], frames)
    self_saved = lax.map(self_forward, (query_self, key_self, value_self, frame_valid))
    mix_self = self_saved[0].reshape(items, frames, local_width)
    attn_out = sum_scatter(project(mix_self, w_out))
    first_row = rank * shard_rows
    own_rows = lax.dynamic_slice_in_dim(tokens_full, first_row, shard_rows, 1)
    hidden_one = own_rows + attn_out
    normed_two_own = layer_norm(hidden_one, gain_two, bias_two).astype(jnp.bfloat16)
    normed_two, text_full = gather_halves(normed_two_own), gather_halves(text_states)
    query_cross = to_heads(project(normed_two, c_query).astype(jnp.bfloat16), frames)
    c_joined = jnp.concatenate([c_key, c_value], 1)
    text_joined = project(text_full, c_joined).astype(jnp.bfloat16)
    key_cross = to_heads(text_joined[..., :local_width], text_rows)
    value_cross = to_heads(text_joined[..., local_width:], text_rows)
    cross_saved = lax.map(cross_forward, (query_cross, key_cross, value_cross, text_len))
    mix_cross = cross_saved[0].reshape(items, frames, local_width)
    cross_out = sum_scatter(project(mix_cross, c_out))
    hidden_two = hidden_one + cross_out
    normed_three = gather_halves(
        layer_norm(hidden_two, gain_three, bias_three).astype(jnp.bfloat16)
    )
    up_rows = project(normed_three, w_up)
    activated = jax.nn.gelu(up_rows, approximate=False).astype(jnp.bfloat16)
    ff_out = sum_scatter(project(activated, w_down))
    result_full = hidden_two + ff_out
    result = result_full.astype(jnp.bfloat16)
    row_valid = ((first_row + jnp.arange(shard_rows))[None, :] < frame_valid[:, None]).astype(
        jnp.float32
    )[:, :, None]

    def masked_square(values):
        return jnp.sum(row_valid * values * values)

    stat_terms = jnp.stack(
        [
            masked_square(result_full),
            masked_square(attn_out),
            masked_square(cross_out),
            masked_square(ff_out),
            jnp.sum(row_valid),
        ]
    )
    grad_ff = gather_halves(grad_out)
    grad_act = project_back(grad_ff, w_down)
    d_w_down = weight_grad(activated, grad_ff)
    gelu_pull = jax.vjp(partial(jax.nn.gelu, approximate=False), up_rows)[1]
    grad_up = gelu_pull(grad_act)[0].astype(jnp.bfloat16)
    d_w_up = weight_grad(normed_three, grad_up)
    grad_n3 = sum_scatter(project_back(grad_up, w_up))
    norm_pull = jax.vjp(layer_norm, hidden_two, gain_three, bias_three)[1]
    grad_h2_norm, d_gain_three, d_bias_three = norm_pull(grad_n3)
    grad_h2 = grad_out.astype(jnp.float32) + grad_h2_norm
    grad_cross = gather_halves(grad_h2.astype(jnp.bfloat16))
    d_c_out = weight_grad(mix_cross, grad_cross)
    grad_mix_cross = to_heads(project_back(grad_cross, c_out).astype(jnp.bfloat16), frames)
    cross_kept = cross_saved[1]
    cross_grads = lax.map(
        cross_backward, (query_cross, key_cross, value_cross, text_len, cross_kept, grad_mix_cross)
    )
    grad_q_cross = cross_grads[0].reshape(items, frames, local_width)
    grad_kv_cross = jnp.concatenate(
        [
            cross_grads[1].reshape(items, text_rows, local_width),
            cross_grads[2].reshape(items, text_rows, local_width),
        ],
        -1,
    )
    d_c_query = weight_grad(normed_two, grad_q_cross)
    d_c_joined = weight_grad(text_full, grad_kv_cross)
    grad_n2 = sum_scatter(project_back(grad_q_cross, c_query))
    d_text_part = sum_scatter(project_back(grad_kv_cross, c_joined))
    norm_pull = jax.vjp(layer_norm, hidden_one, gain_two, bias_two)[1]
    grad_h1_norm, d_gain_two, d_bias_two = norm_pull(grad_n2)
    grad_h1 = grad_h2 + grad_h1_norm
    grad_attn = gather_halves(grad_h1.astype(jnp.bfloat16))
    d_w_out = weight_grad(mix_self, grad_attn)
    grad_mix_self = to_heads(project_back(grad_attn, w_out).astype(jnp.bfloat16), frames)
    self_kept = self_saved[1]
    self_grads = lax.map(
        self_backward, (query_self, key_self, value_self, frame_valid, self_kept, grad_mix_self)
    )
    grad_joined = jnp.concatenate(
        [
            self_grads[0].reshape(items, frames, local_width),
            self_grads[1].reshape(items, frames, local_width),
            self_grads[2].reshape(items, frames, local_width),
        ],
        -1,
    )
    d_w_joined = weight_grad(normed_one, grad_joined)
    grad_n1 = sum_scatter(project_back(grad_joined, w_joined))
    norm_pull = jax.vjp(layer_norm, own_rows, gain_one, bias_one)[1]
    grad_x_norm, d_gain_one, d_bias_one = norm_pull(grad_n1)
    d_tokens = grad_h1 + grad_x_norm
    order_x, order_y, order_z = bit_orders()
    cut_down, cut_up = width * 3 // 4, w_up.shape[1] * 3 // 4
    down_sum = sum_over_items(d_w_down[:, :cut_down], order_x)
    up_sum = sum_over_items(d_w_up[:, :cut_up], order_y)
    rest_sum = sum_over_items(
        jnp.concatenate([d_w_up[:, cut_up:], fold_rows(d_w_down[:, cut_down:])], 0), order_z
    )
    rest_rows = d_w_up.shape[0]
    d_w_up_sum = jnp.concatenate([up_sum, rest_sum[:rest_rows]], 1)
    d_w_down_sum = jnp.concatenate([down_sum, unfold_rows(rest_sum[rest_rows:])], 1)
    key_value_sum = sum_over_items(d_c_joined, order_x)
    query_out_sum = sum_over_items(
        jnp.concatenate([d_c_query, jnp.concatenate([d_c_out[:, : width // 2], d_c_out[:, width // 2 :]], 0)], 1), order_y
    )
    d_c_query_sum = query_out_sum[:, :local_width]
    folded = query_out_sum[:, local_width:]
    d_c_out_sum = jnp.concatenate([folded[:local_width], folded[local_width:]], 1)
    d_w_out_sum = sum_over_items(d_w_out, order_z)
    joined_cut = d_w_joined.shape[1] // 2
    joined_sum = jnp.concatenate(
        [
            sum_over_items(d_w_joined[:, :joined_cut], order_x),
            sum_over_items(d_w_joined[:, joined_cut:], order_y),
        ],
        1,
    )
    small_rows = jnp.stack(
        [
            d_gain_one,
            d_bias_one,
            d_gain_two,
            d_bias_two,
            d_gain_three,
            d_bias_three,
            jnp.pad(stat_terms, (0, width - 5)),
            jnp.zeros((width,), jnp.float32),
        ]
    )
    small = sum_small(small_rows)
    stat_totals = small[6]
    rms_stats = jnp.sqrt(stat_totals[:4] / (stat_totals[4] * width))
    return (
        result,
        d_tokens,
        d_text_part,
        small[0],
        small[1],
        small[2],
        small[3],
        small[4],
        small[5],
        joined_sum[:, :local_width],
        joined_sum[:, local_width : 2 * local_width],
        joined_sum[:, 2 * local_width :],
        d_w_out_sum,
        d_c_query_sum,
        key_value_sum[:, :local_width],
        key_value_sum[:, local_width:],
        d_c_out_sum,
        d_w_up_sum,
        d_w_down_sum,
        rms_stats,
    )


def solution(mesh):
    return jax.shard_map(
        per_device,
        mesh=mesh,
        in_specs=(
            P("dp", None, None),
            P("dp", "mp", None),
            P("dp"),
            P("dp"),
            P(),
            P(),
            P(),
            P(),
            P(),
            P(),
            P(None, "mp"),
            P(None, "mp"),
            P(None, "mp"),
            P("mp", None),
            P(None, "mp"),
            P(None, "mp"),
            P(None, "mp"),
            P("mp", None),
            P(None, "mp"),
            P("mp", None),
            P("dp", "mp", None),
        ),
        out_specs=(
            P("dp", "mp", None),
            P("dp", "mp", None),
            P("dp", "mp", None),
            P(),
            P(),
            P(),
            P(),
            P(),
            P(),
            P(None, "mp"),
            P(None, "mp"),
            P(None, "mp"),
            P("mp", None),
            P(None, "mp"),
            P(None, "mp"),
            P(None, "mp"),
            P("mp", None),
            P(None, "mp"),
            P("mp", None),
            P(),
        ),
        check_vma=False,
    )
```

```python
import math
from collections import namedtuple

import jax
import jax.numpy as jnp
from jax import lax
from jax.experimental import pallas as pl
from jax.experimental.pallas import tpu as pltpu
from jax.sharding import PartitionSpec as P

HD = 64
PAIR = 2 * HD
norm_eps = 1e-05
score_scale = 0.125
masked_fill = -1e30
F32 = jnp.float32
BF16 = jnp.bfloat16
SLACK_BYTES = 6 * 1024 * 1024
SMEM_SPEC = pl.BlockSpec(memory_space=pltpu.SMEM)


def dot(a, b):
    return lax.dot_general(a, b, (((1,), (0,)), ((), ())), preferred_element_type=F32)


def dot_rt(a, b):
    return lax.dot_general(a, b, (((1,), (1,)), ((), ())), preferred_element_type=F32)


def dot_lt(a, b):
    return lax.dot_general(a, b, (((0,), (0,)), ((), ())), preferred_element_type=F32)


def whole(shape):
    zeros = (0,) * len(shape)
    return pl.BlockSpec(tuple(shape), lambda *_: zeros)


def shape_of(shape, kind):
    return jax.ShapeDtypeStruct(tuple(shape), kind)


def vmem_bytes(specs, arrays, scratch=()):
    total = SLACK_BYTES
    for spec, array in zip(specs, arrays):
        if spec.block_shape is not None:
            total += 2 * math.prod(spec.block_shape) * jnp.dtype(array.dtype).itemsize
    for buffer in scratch:
        total += math.prod(buffer.shape) * jnp.dtype(buffer.dtype).itemsize
    return min(total, 60 * 1024 * 1024)


def call(body, grid, in_specs, out_specs, out_shape, args, scratch=(), flops=0):
    return pl.pallas_call(
        body,
        grid=grid,
        in_specs=in_specs,
        out_specs=out_specs,
        out_shape=out_shape,
        scratch_shapes=list(scratch),
        compiler_params=pltpu.CompilerParams(
            vmem_limit_bytes=vmem_bytes(
                [*in_specs, *out_specs], [*args, *out_shape], scratch
            )
        ),
        cost_estimate=pl.CostEstimate(flops=flops, bytes_accessed=1024, transcendentals=0),
    )(*args)


def norm_parts(values):
    average = jnp.mean(values, -1, keepdims=True)
    centered = values - average
    variance = jnp.mean(centered * centered, -1, keepdims=True)
    scale = lax.rsqrt(variance + norm_eps)
    return centered * scale, scale


def layer_norm(values, gain_ref, bias_ref):
    normed, _ = norm_parts(values)
    return normed * gain_ref[...].astype(F32) + bias_ref[...].astype(F32)


ROW_BLOCK = 256


def add_row(ref, row):
    first = (pl.program_id(0) == 0) & (pl.program_id(1) == 0)

    @pl.when(first)
    def _():
        ref[...] = row

    @pl.when(jnp.logical_not(first))
    def _():
        ref[...] += row


def column_sum(values):
    return jnp.sum(values, 0, keepdims=True)


def row_mask(rank_ref, half, count):
    first_row = rank_ref[0] * half + pl.program_id(1) * ROW_BLOCK
    place = first_row + lax.broadcasted_iota(jnp.int32, (ROW_BLOCK, 1), 0)
    return (place < count).astype(F32)


def project_tokens(tokens, gain, bias, w_query, w_key, w_value):
    rows, width = tokens.shape
    local = w_query.shape[1]
    block = 256

    def body(x, g, b, wq, wk, wv, n, q, k, v):
        normed = layer_norm(x[...].astype(F32), g, b).astype(BF16)
        n[...] = normed
        q[...] = dot(normed, wq[...]).astype(BF16)
        k[...] = dot(normed, wk[...]).astype(BF16)
        v[...] = dot(normed, wv[...]).astype(BF16)

    wide = pl.BlockSpec((block, width), lambda i: (i, 0))
    slim = pl.BlockSpec((block, local), lambda i: (i, 0))
    return call(
        body,
        (rows // block,),
        [wide, whole((1, width)), whole((1, width))] + [whole(w_query.shape)] * 3,
        [wide, slim, slim, slim],
        [shape_of((rows, width), BF16)] + [shape_of((rows, local), BF16)] * 3,
        (tokens, gain, bias, w_query, w_key, w_value),
    )


def project_text(text_own, text_other, c_key, c_value):
    items, text_half, depth = text_own.shape
    local = c_key.shape[1]

    def body(own, other, wk, wv, k, v):
        for half, rows in enumerate((own, other)):
            for item in range(items):
                k[item, half] = dot(rows[item], wk[...]).astype(BF16)
                v[item, half] = dot(rows[item], wv[...]).astype(BF16)

    shape = (items, 2, text_half, local)
    return call(
        body,
        (1,),
        [whole(text_own.shape)] * 2 + [whole(c_key.shape)] * 2,
        [whole(shape)] * 2,
        [shape_of(shape, BF16)] * 2,
        (text_own, text_other, c_key, c_value),
    )


def head_mask(rows, head):
    lane = lax.broadcasted_iota(jnp.int32, (rows, PAIR), 1)
    return lane < HD if head == 0 else lane >= HD


def pick(first, second):
    return jnp.where(head_mask(first.shape[0], 0), first, second)


def only(values, head):
    return jnp.where(head_mask(values.shape[0], head), values, jnp.zeros_like(values))


def scores_t(query_pair, key_pair, head, allowed):
    scores = dot_rt(key_pair, only(query_pair, head)) * score_scale
    return jnp.where(allowed, scores, masked_fill)


def attend_pair(query_pair, key_pair, value_pair, allowed, lse_ref, lse_at):
    mixed = []
    for head in range(2):
        scores = scores_t(query_pair, key_pair, head, allowed)
        highest = jnp.max(scores, 0, keepdims=True)
        powers = jnp.exp(scores - highest)
        total = jnp.sum(powers, 0, keepdims=True)
        probs = (powers / total).astype(BF16)
        mixed.append(dot_lt(probs, value_pair))
        row, columns = lse_at(head)
        lse_ref[0, row : row + 1, columns] = highest + jnp.log(total)
    return pick(mixed[0], mixed[1]).astype(BF16)


def attend_pair_back(query_pair, key_pair, value_pair, allowed, lse_rows, grad_pair):
    grads = []
    for head in range(2):
        probs = jnp.exp(scores_t(query_pair, key_pair, head, allowed) - lse_rows[head])
        grad_probs = dot_rt(value_pair, only(grad_pair, head))
        inner = jnp.sum(grad_probs * probs, 0, keepdims=True)
        grad_scores = (probs * (grad_probs - inner)).astype(BF16)
        grads.append(
            (
                dot_lt(grad_scores, key_pair),
                dot(grad_scores, query_pair),
                dot(probs.astype(BF16), grad_pair),
            )
        )
    return [pick(one, two) for one, two in zip(grads[0], grads[1])]


def causal_mask(keys, queries, first_query, count):
    key_at = lax.broadcasted_iota(jnp.int32, (keys, queries), 0)
    query_at = first_query + lax.broadcasted_iota(jnp.int32, (keys, queries), 1)
    return (key_at <= query_at) & (key_at < count)


def text_mask(text_half, queries, rank, count):
    key_at = lax.broadcasted_iota(jnp.int32, (2 * text_half, queries), 0)
    swapped = jnp.where(key_at < text_half, key_at + text_half, key_at - text_half)
    return jnp.where(rank == 0, key_at, swapped) < count


def self_forward(rank, valid, query, key, value, w_out):
    items, frames, local = query.shape
    width = w_out.shape[1]
    half = frames // 2
    heads = local // HD

    def body(rank_ref, valid_ref, q, k, v, w, mix, lse, own, send):
        me = rank_ref[0]
        count = valid_ref[pl.program_id(0)]
        for part in range(2):
            keys = (part + 1) * half
            allowed = causal_mask(keys, half, part * half, count)
            rows = slice(part * half, (part + 1) * half)
            for pair in range(local // PAIR):
                columns = slice(pair * PAIR, (pair + 1) * PAIR)
                mix[part ^ me, 0, :, columns] = attend_pair(
                    q[0, rows, columns],
                    k[0, :keys, columns],
                    v[0, :keys, columns],
                    allowed,
                    lse,
                    lambda head: (2 * pair + head, rows),
                )
        send[0] = dot(mix[1, 0], w[...]).astype(BF16)
        own[0] = dot(mix[0, 0], w[...])

    tall = pl.BlockSpec((1, frames, local), lambda i: (i, 0, 0))
    out = pl.BlockSpec((1, half, width), lambda i: (i, 0, 0))
    return call(
        body,
        (items,),
        [SMEM_SPEC, SMEM_SPEC, tall, tall, tall, whole(w_out.shape)],
        [
            pl.BlockSpec((2, 1, half, local), lambda i: (0, i, 0, 0)),
            pl.BlockSpec((1, heads, frames), lambda i: (i, 0, 0)),
            out,
            out,
        ],
        [
            shape_of((2, items, half, local), BF16),
            shape_of((items, heads, frames), F32),
            shape_of((items, half, width), F32),
            shape_of((items, half, width), BF16),
        ],
        (rank, valid, query, key, value, w_out),
    )


def cross_forward(rank, text_len, normed_own, normed_other, c_query, key, value, c_out):
    items, half, width = normed_own.shape
    text_half = key.shape[2]
    local = c_query.shape[1]
    heads = local // HD

    def body(rank_ref, len_ref, own_n, other_n, wq, k, v, w, q, mix, lse, own, send):
        allowed = text_mask(text_half, half, rank_ref[0], len_ref[pl.program_id(0)])
        for part, normed in enumerate((own_n, other_n)):
            q[part, 0] = dot(normed[0], wq[...]).astype(BF16)
            for pair in range(local // PAIR):
                columns = slice(pair * PAIR, (pair + 1) * PAIR)
                mix[part, 0, :, columns] = attend_pair(
                    q[part, 0, :, columns],
                    k[0, :, :, columns].reshape(2 * text_half, PAIR),
                    v[0, :, :, columns].reshape(2 * text_half, PAIR),
                    allowed,
                    lse,
                    lambda head: (2 * pair + head, slice(part * half, (part + 1) * half)),
                )
        send[0] = dot(mix[1, 0], w[...]).astype(BF16)
        own[0] = dot(mix[0, 0], w[...])

    out = pl.BlockSpec((1, half, width), lambda i: (i, 0, 0))
    text = pl.BlockSpec((1, 2, text_half, local), lambda i: (i, 0, 0, 0))
    both = pl.BlockSpec((2, 1, half, local), lambda i: (0, i, 0, 0))
    return call(
        body,
        (items,),
        [SMEM_SPEC, SMEM_SPEC, out, out, whole(c_query.shape), text, text, whole(c_out.shape)],
        [both, both, pl.BlockSpec((1, heads, 2 * half), lambda i: (i, 0, 0)), out, out],
        [
            shape_of((2, items, half, local), BF16),
            shape_of((2, items, half, local), BF16),
            shape_of((items, heads, 2 * half), F32),
            shape_of((items, half, width), F32),
            shape_of((items, half, width), BF16),
        ],
        (rank, text_len, normed_own, normed_other, c_query, key, value, c_out),
    )


def residual_norm(rank, valid, base, own, received, gain, bias):
    items, half, width = own.shape

    def body(rank_ref, valid_ref, x, part, other, g, b, hidden, normed, square):
        item = pl.program_id(0)
        branch = part[0] + other[0].astype(F32)
        total = x[0].astype(F32) + branch
        hidden[0] = total
        normed[0] = layer_norm(total, g, b).astype(BF16)
        mask = row_mask(rank_ref, half, valid_ref[item])
        add_row(square, column_sum(mask * branch * branch))

    steps = half // ROW_BLOCK
    block = pl.BlockSpec((1, ROW_BLOCK, width), lambda i, r, *_: (i, r, 0))
    row = whole((1, width))
    if base.shape[1] == half:
        base_spec = block
    else:
        base_spec = pl.BlockSpec(
            (1, ROW_BLOCK, width), lambda i, r, me, _: (i, me[0] * steps + r, 0)
        )
    return pl.pallas_call(
        body,
        grid_spec=pltpu.PrefetchScalarGridSpec(
            num_scalar_prefetch=2,
            grid=(items, steps),
            in_specs=[base_spec, block, block, row, row],
            out_specs=[block, block, row],
        ),
        out_shape=[
            shape_of(own.shape, F32),
            shape_of(own.shape, BF16),
            shape_of((1, width), F32),
        ],
        compiler_params=pltpu.CompilerParams(vmem_limit_bytes=3 * SLACK_BYTES),
        cost_estimate=pl.CostEstimate(flops=0, bytes_accessed=1024, transcendentals=0),
    )(rank, valid, base, own, received, gain, bias)


def gelu_parts(values):
    normal = 0.5 * (1.0 + lax.erf(values * (0.5**0.5)))
    density = jnp.exp(-0.5 * values * values) * 0.3989422804014327
    return values * normal, normal + values * density


def feed_forward(
    block_index, orders, normed_own, normed_other, grad_own, grad_other, w_up, w_down
):
    rows, width = normed_own.shape
    units = w_up.shape[1]
    steps = units // LANES
    down_each, up_each = units // BLOCKS, width // BLOCKS
    sizes = dict(down=down_each, up=up_each * (steps - 1), rest=down_each + up_each)

    def body(me_ref, n_own, n_other, g_own, g_other, up_w, down_w, act, grad, *rest):
        me = me_ref[0]
        packets = {name: rest[2 * k : 2 * k + 2] for k, name in enumerate(sizes)}
        down_part, up_part = rest[2 * len(sizes) :]
        step = pl.program_id(0)
        down_sum, up_sum = 0.0, 0.0
        for half, (n, g) in enumerate(((n_own, g_own), (n_other, g_other))):
            value, slope = gelu_parts(dot(n[...], up_w[...]))
            act[half] = value.astype(BF16)
            grad[half] = (dot_rt(g[...], down_w[...]) * slope).astype(BF16)
            down_sum = down_sum + dot_lt(act[half], g[...])
            up_sum = up_sum + dot_lt(n[...], grad[half])
        down_part[...] = down_sum.astype(BF16)
        up_part[...] = up_sum.astype(BF16)

        def put(name, block, first, values):
            place = place_of(block ^ me, orders[name])
            keep, send = packets[name]
            where = pl.ds(first, values.shape[0])

            @pl.when(place < BLOCKS // 2)
            def _():
                keep[place, where, :] = values

            @pl.when(place >= BLOCKS // 2)
            def _():
                send[place - BLOCKS // 2, where, :] = values

        for sub in range(LANES // down_each):
            part = slice(sub * down_each, (sub + 1) * down_each)
            block = step * (LANES // down_each) + sub
            put("down", block, 0, down_part[part, :LANES])
            put("rest", block, 0, down_part[part, LANES:])

        @pl.when(step < steps - 1)
        def _():
            for block in range(BLOCKS):
                part = slice(block * up_each, (block + 1) * up_each)
                put("up", block, step * up_each, up_part[part, :])

        @pl.when(step == steps - 1)
        def _():
            for block in range(BLOCKS):
                part = slice(block * up_each, (block + 1) * up_each)
                put("rest", block, down_each, up_part[part, :])

    out = pl.BlockSpec((2, rows, LANES), lambda j: (0, 0, j))
    shapes = [(BLOCKS // 2, sizes[name], LANES) for name in sizes for _ in range(2)]
    results = call(
        body,
        (steps,),
        [SMEM_SPEC]
        + [whole(normed_own.shape)] * 4
        + [
            pl.BlockSpec((width, LANES), lambda j: (0, j)),
            pl.BlockSpec((LANES, width), lambda j: (j, 0)),
        ],
        [out, out] + [whole(shape) for shape in shapes],
        [shape_of((2, rows, units), BF16)] * 2 + [shape_of(shape, BF16) for shape in shapes],
        (block_index, normed_own, normed_other, grad_own, grad_other, w_up, w_down),
        scratch=[pltpu.VMEM((LANES, width), BF16), pltpu.VMEM((width, LANES), BF16)],
    )
    pairs = {name: results[2 + 2 * k : 4 + 2 * k] for k, name in enumerate(sizes)}
    return results[0], results[1], pairs


def project_halves(values, weight, transposed):
    _, rows, depth = values.shape
    width = weight.shape[0] if transposed else weight.shape[1]

    def body(a, w, own, send):
        multiply = dot_rt if transposed else dot
        product = multiply(a[0], w[...])

        @pl.when(pl.program_id(0) == 0)
        def _():
            send[...] = product.astype(BF16)

        @pl.when(pl.program_id(0) == 1)
        def _():
            own[...] = product

    return call(
        body,
        (2,),
        [pl.BlockSpec((1, rows, depth), lambda j: (1 - j, 0, 0)), whole(weight.shape)],
        [whole((rows, width))] * 2,
        [shape_of((rows, width), F32), shape_of((rows, width), BF16)],
        (values, weight),
    )


def finish_output(rank, valid, hidden, own, received):
    items, half, width = hidden.shape

    def body(rank_ref, valid_ref, x, part, other, out, square, branch_square):
        branch = part[0] + other[0].astype(F32)
        total = x[0] + branch
        out[0] = total.astype(BF16)
        mask = row_mask(rank_ref, half, valid_ref[pl.program_id(0)])
        add_row(square, column_sum(mask * total * total))
        add_row(branch_square, column_sum(mask * branch * branch))

    steps = half // ROW_BLOCK
    block = pl.BlockSpec((1, ROW_BLOCK, width), lambda i, r: (i, r, 0))
    return call(
        body,
        (items, steps),
        [SMEM_SPEC, SMEM_SPEC, block, block, block],
        [block, whole((1, width)), whole((1, width))],
        [shape_of(hidden.shape, BF16)] + [shape_of((1, width), F32)] * 2,
        (rank, valid, hidden, own, received),
    )


def norm_backward(rank, values, gain, own, received, grad_base, last):
    items, half, width = own.shape

    def body(rank_ref, x, g, part, other, base, *outs):
        normed, scale = norm_parts(x[0].astype(F32))
        grad = part[0] + other[0].astype(F32)
        add_row(outs[1], column_sum(grad * normed))
        add_row(outs[2], column_sum(grad))
        scaled = grad * g[...].astype(F32)
        first = jnp.mean(scaled, -1, keepdims=True)
        second = jnp.mean(scaled * normed, -1, keepdims=True)
        total = base[0].astype(F32) + scale * (scaled - first - normed * second)
        outs[0][0] = total
        if not last:
            outs[3][0] = total.astype(BF16)

    steps = half // ROW_BLOCK
    block = pl.BlockSpec((1, ROW_BLOCK, width), lambda i, r, *_: (i, r, 0))
    row = whole((1, width))
    if values.shape[1] == half:
        values_spec = block
    else:
        values_spec = pl.BlockSpec(
            (1, ROW_BLOCK, width), lambda i, r, me: (i, me[0] * steps + r, 0)
        )
    out_specs = [block, row, row]
    out_shape = [
        shape_of(own.shape, F32),
        shape_of((1, width), F32),
        shape_of((1, width), F32),
    ]
    if not last:
        out_specs.append(block)
        out_shape.append(shape_of(own.shape, BF16))
    return pl.pallas_call(
        body,
        grid_spec=pltpu.PrefetchScalarGridSpec(
            num_scalar_prefetch=1,
            grid=(items, steps),
            in_specs=[values_spec, row, block, block, block],
            out_specs=out_specs,
        ),
        out_shape=out_shape,
        compiler_params=pltpu.CompilerParams(vmem_limit_bytes=3 * SLACK_BYTES),
        cost_estimate=pl.CostEstimate(flops=0, bytes_accessed=1024, transcendentals=0),
    )(rank, values, gain, own, received, grad_base)


def cross_backward(
    rank, text_len, grad_own, grad_other, c_out, query, key, value, lse, c_query, c_key, c_value
):
    items, half, width = grad_own.shape
    text_half = key.shape[2]
    depth, local = c_key.shape
    heads = local // HD

    def body(
        rank_ref, len_ref, g_own, g_other, w, q, k, v, stats, wq, wk, wv,
        dq, dk, dv, own, send, text_own, text_send, grad_mix,
    ):
        allowed = text_mask(text_half, half, rank_ref[0], len_ref[pl.program_id(0)])
        for part, grad in enumerate((g_own, g_other)):
            grad_mix[part] = dot_rt(grad[0], w[...]).astype(BF16)
        for pair in range(local // PAIR):
            columns = slice(pair * PAIR, (pair + 1) * PAIR)
            key_sum, value_sum = 0.0, 0.0
            for part in range(2):
                rows = slice(part * half, (part + 1) * half)
                one, two, three = attend_pair_back(
                    q[part, 0, :, columns],
                    k[0, :, :, columns].reshape(2 * text_half, PAIR),
                    v[0, :, :, columns].reshape(2 * text_half, PAIR),
                    allowed,
                    [stats[0, 2 * pair + head : 2 * pair + head + 1, rows] for head in range(2)],
                    grad_mix[part, :, columns],
                )
                dq[part, 0, :, columns] = (one * score_scale).astype(BF16)
                key_sum, value_sum = key_sum + two, value_sum + three
            key_sum = (key_sum * score_scale).astype(BF16)
            value_sum = value_sum.astype(BF16)
            for part in range(2):
                rows = slice(part * text_half, (part + 1) * text_half)
                dk[0, part, :, columns] = key_sum[rows]
                dv[0, part, :, columns] = value_sum[rows]
        send[0] = dot_rt(dq[1, 0], wq[...]).astype(BF16)
        own[0] = dot_rt(dq[0, 0], wq[...])
        text_send[0] = (dot_rt(dk[0, 1], wk[...]) + dot_rt(dv[0, 1], wv[...])).astype(BF16)
        text_own[0] = dot_rt(dk[0, 0], wk[...]) + dot_rt(dv[0, 0], wv[...])

    out = pl.BlockSpec((1, half, width), lambda i: (i, 0, 0))
    text = pl.BlockSpec((1, 2, text_half, local), lambda i: (i, 0, 0, 0))
    both = pl.BlockSpec((2, 1, half, local), lambda i: (0, i, 0, 0))
    deep = pl.BlockSpec((1, text_half, depth), lambda i: (i, 0, 0))
    return call(
        body,
        (items,),
        [
            SMEM_SPEC, SMEM_SPEC, out, out, whole(c_out.shape), both, text, text,
            pl.BlockSpec((1, heads, 2 * half), lambda i: (i, 0, 0)),
            whole(c_query.shape), whole(c_key.shape), whole(c_value.shape),
        ],
        [both, text, text, out, out, deep, deep],
        [
            shape_of(query.shape, BF16),
            shape_of(key.shape, BF16),
            shape_of(key.shape, BF16),
            shape_of(grad_own.shape, F32),
            shape_of(grad_own.shape, BF16),
            shape_of((items, text_half, depth), F32),
            shape_of((items, text_half, depth), BF16),
        ],
        (
            rank, text_len, grad_own, grad_other, c_out, query, key, value, lse,
            c_query, c_key, c_value,
        ),
        scratch=[pltpu.VMEM((2, half, local), BF16)],
    )


def self_backward(
    rank, valid, grad_own, grad_other, w_out, query, key, value, lse, w_query, w_key, w_value
):
    items, half, width = grad_own.shape
    frames, local = query.shape[1:]
    heads = local // HD

    def body(
        rank_ref, valid_ref, g_own, g_other, w, q, k, v, stats, wq, wk, wv,
        dq, dk, dv, own, send, grad_mix,
    ):
        me = rank_ref[0]
        count = valid_ref[pl.program_id(0)]
        grad_mix[me] = dot_rt(g_own[0], w[...]).astype(BF16)
        grad_mix[1 - me] = dot_rt(g_other[0], w[...]).astype(BF16)
        masks = [causal_mask((part + 1) * half, half, part * half, count) for part in range(2)]
        for pair in range(local // PAIR):
            columns = slice(pair * PAIR, (pair + 1) * PAIR)
            sums = []
            for part in range(2):
                keys = (part + 1) * half
                rows = slice(part * half, keys)
                one, two, three = attend_pair_back(
                    q[0, rows, columns],
                    k[0, :keys, columns],
                    v[0, :keys, columns],
                    masks[part],
                    [stats[0, 2 * pair + head : 2 * pair + head + 1, rows] for head in range(2)],
                    grad_mix[part, :, columns],
                )
                dq[0, rows, columns] = (one * score_scale).astype(BF16)
                sums.append((two, three))
            (key_a, value_a), (key_b, value_b) = sums
            dk[0, :half, columns] = ((key_a + key_b[:half]) * score_scale).astype(BF16)
            dk[0, half:, columns] = (key_b[half:] * score_scale).astype(BF16)
            dv[0, :half, columns] = (value_a + value_b[:half]).astype(BF16)
            dv[0, half:, columns] = value_b[half:].astype(BF16)

        def back(part):
            rows = pl.ds(pl.multiple_of(part * half, half), half)
            return (
                dot_rt(dq[0, rows, :], wq[...])
                + dot_rt(dk[0, rows, :], wk[...])
                + dot_rt(dv[0, rows, :], wv[...])
            )

        send[0] = back(1 - me).astype(BF16)
        own[0] = back(me)

    out = pl.BlockSpec((1, half, width), lambda i: (i, 0, 0))
    tall = pl.BlockSpec((1, frames, local), lambda i: (i, 0, 0))
    return call(
        body,
        (items,),
        [
            SMEM_SPEC, SMEM_SPEC, out, out, whole(w_out.shape), tall, tall, tall,
            pl.BlockSpec((1, heads, frames), lambda i: (i, 0, 0)),
            whole(w_query.shape), whole(w_key.shape), whole(w_value.shape),
        ],
        [tall, tall, tall, out, out],
        [shape_of(query.shape, BF16)] * 3
        + [shape_of(grad_own.shape, F32), shape_of(grad_own.shape, BF16)],
        (
            rank, valid, grad_own, grad_other, w_out, query, key, value, lse,
            w_query, w_key, w_value,
        ),
        scratch=[pltpu.VMEM((2, half, local), BF16)],
    )


BLOCKS = 16
LEVELS = 4
LANES = 512
Piece = namedtuple("Piece", ("terms", "rows", "first", "width", "tile", "full"))


def place_of(block, order):
    place = 0
    for k, bit in enumerate(order):
        place = place + (((block >> bit) & 1) << (LEVELS - 1 - k))
    return place


def block_at(place, order):
    return sum(((place >> (LEVELS - 1 - k)) & 1) << bit for k, bit in enumerate(order))


def gradient_packet(block_index, pieces, order, operands):
    rows_each = sum(piece.rows // BLOCKS * (piece.width // LANES) for piece in pieces)
    count = len(operands)
    starts = []
    steps = 0
    for piece in pieces:
        starts.append(steps)
        steps += piece.rows // piece.tile if piece.tile < piece.rows else piece.width // LANES

    def body(*refs):
        me = refs[0][0]
        given = refs[1 : 1 + count]
        keep, send, natural = refs[1 + count :]
        step = pl.program_id(0)
        offset = 0
        for start, piece in zip(starts, pieces):
            by_rows = piece.tile < piece.rows
            number = piece.rows // piece.tile if by_rows else piece.width // LANES
            each = piece.rows // BLOCKS

            @pl.when((step >= start) & (step < start + number))
            def _(start=start, piece=piece, by_rows=by_rows, each=each, offset=offset):
                total = None
                for (left, left_at), (right, right_at) in piece.terms:
                    term = dot_lt(given[left][left_at], given[right][right_at])
                    total = term if total is None else total + term
                natural[: piece.tile, :] = total.astype(BF16)
                at = step - start
                for sub in range(piece.tile // each):
                    block = (at * (piece.tile // each) + sub if by_rows else sub) ^ me
                    place = place_of(block, order)
                    base = offset if by_rows else offset + at * each
                    rows = pl.ds(base, each)
                    values = natural[sub * each : (sub + 1) * each, :]

                    @pl.when(place < BLOCKS // 2)
                    def _():
                        keep[place, rows, :] = values

                    @pl.when(place >= BLOCKS // 2)
                    def _():
                        send[place - BLOCKS // 2, rows, :] = values

            offset += each * (piece.width // LANES)

    def spec(array, axis, start, number, block):
        if axis is None:
            return whole(array.shape)
        shape = list(array.shape)
        shape[axis] = block
        first, at = start

        def index(i):
            place = [0] * len(shape)
            place[axis] = first + jnp.clip(i - at, 0, number - 1)
            return tuple(place)

        return pl.BlockSpec(tuple(shape), index)

    half_shape = (BLOCKS // 2, rows_each, LANES)
    return call(
        body,
        (steps,),
        [SMEM_SPEC] + [spec(*operand) for operand in operands],
        [whole(half_shape)] * 2,
        [shape_of(half_shape, BF16)] * 2,
        (block_index, *(operand[0] for operand in operands)),
        scratch=[pltpu.VMEM((max(piece.tile for piece in pieces), LANES), BF16)],
    )


def open_packet(block_index, pieces, order, kept, received, before):
    steps = 4
    group = BLOCKS // steps
    previous = [x for x in before if x is not None]

    def body(*refs):
        me = refs[0][0]
        low, high = refs[1], refs[2]
        outs = refs[3 + len(previous) :]
        for step in range(group):
            place = place_of((pl.program_id(0) * group + step) ^ me, order)
            inner = place & (BLOCKS // 2 - 1)
            upper = place >= BLOCKS // 2
            offset = 0
            for out, piece in zip(outs, pieces):
                each = piece.rows // BLOCKS
                for column in range(piece.width // LANES):
                    part = slice(offset, offset + each)
                    values = jnp.where(upper, high[inner, part, :], low[inner, part, :])
                    lanes = slice(column * LANES, (column + 1) * LANES)
                    out[step * each : (step + 1) * each, lanes] = values.astype(F32)
                    offset += each

    out_specs, out_shape, aliases = [], [], {}
    for number, (piece, old) in enumerate(zip(pieces, before)):
        at = piece.first // piece.width
        out_specs.append(
            pl.BlockSpec((piece.rows // steps, piece.width), lambda i, at=at: (i, at))
        )
        out_shape.append(shape_of((piece.rows, piece.full), F32))
        if old is not None:
            aliases[3 + len(aliases)] = number
    return pl.pallas_call(
        body,
        grid=(steps,),
        in_specs=[SMEM_SPEC, whole(kept.shape), whole(kept.shape)]
        + [pl.BlockSpec(memory_space=pl.ANY)] * len(previous),
        out_specs=out_specs,
        out_shape=out_shape,
        input_output_aliases=aliases,
        compiler_params=pltpu.CompilerParams(vmem_limit_bytes=3 * SLACK_BYTES),
        cost_estimate=pl.CostEstimate(flops=0, bytes_accessed=1024, transcendentals=0),
    )(block_index, kept, received, *previous)


def main_bits():
    bits = lax.axis_size("dp").bit_length() - 1
    along_x = (bits - 2) // 2
    main = [0, along_x, bits - 2, bits - 1]
    return main, [bit for bit in range(bits) if bit not in main]


def exchange(values, bit):
    pairs = [(d, d ^ (1 << bit)) for d in range(lax.axis_size("dp"))]
    return lax.ppermute(values, "dp", pairs)


def add_rounded(one, two):
    return (one.astype(F32) + two.astype(F32)).astype(BF16)


SWAP = [(0, 1), (1, 0)]


def swap_cores(values):
    return lax.ppermute(values, "mp", SWAP)


class Program:
    def __init__(self, given):
        self.v = dict(given)
        self.token = jnp.zeros((8, 128), F32)
        self.packets = {}

    def tie(self, values):
        values, self.token = lax.optimization_barrier((values, self.token))
        return values

    def start(self, name):
        packet = self.packets[name]
        order, step = packet["order"], packet["step"]
        bit = (order + order[::-1])[step]
        if step < LEVELS:
            values = self.tie(packet["send"])
        else:
            values = packet["keep"] = self.tie(packet["keep"])
        packet["arrived"] = exchange(values, self.main[bit])

    def finish(self, name):
        packet = self.packets[name]
        step, keep = packet["step"], packet["keep"]
        arrived = self.tie(packet["arrived"])
        packet["step"] = step + 1
        if step < LEVELS - 1:
            half = keep.shape[0] // 2
            packet["send"] = add_rounded(keep[half:], arrived[half:])
            packet["keep"] = add_rounded(keep[:half], arrived[:half])
            packet["send"] = self.tie(packet["send"])
        elif step == LEVELS - 1:
            keep = add_rounded(keep, arrived)
            for bit in self.extra:
                keep = add_rounded(keep, exchange(keep, bit))
            packet["keep"] = self.tie(keep)
        elif step < 2 * LEVELS - 1:
            packet["keep"] = self.tie(jnp.concatenate([keep, arrived], 0))
        else:
            outs = open_packet(
                self.block,
                packet["pieces"],
                packet["order"],
                keep,
                arrived,
                [self.v.get(out) for out in packet["outs"]],
            )
            for out, values in zip(packet["outs"], outs):
                self.v[out] = values
            self.v[packet["outs"][0]] = self.tie(outs[0])

    def packet(self, name, outs, pieces, operands):
        order = ORDERS[name]
        operands = [
            x if isinstance(x, tuple) else (x, None, None, None, None) for x in operands
        ]
        operands[0] = (self.tie(operands[0][0]), *operands[0][1:])
        self.add(name, gradient_packet(self.block, pieces, order, operands), pieces, outs)

    def add(self, name, halves_of, pieces, outs):
        keep, send = halves_of
        self.packets[name] = dict(
            order=ORDERS[name], step=0, keep=keep, send=self.tie(send), pieces=pieces, outs=outs
        )


def stage_text(p):
    v = p.v
    v["k_cross"], v["v_cross"] = project_text(
        v["text_own"], v["text_other"], v["c_key"], v["c_value"]
    )


def stage_tokens(p):
    v = p.v
    items, frames, width = v["tokens"].shape
    normed, *heads = project_tokens(
        v["tokens"].reshape(items * frames, width),
        v["gain_one"],
        v["bias_one"],
        v["w_query"],
        v["w_key"],
        v["w_value"],
    )
    v["normed_one"] = normed
    v["q_self"], v["k_self"], v["v_self"] = [x.reshape(items, frames, -1) for x in heads]


def stage_self(p):
    v = p.v
    v["mix_self"], v["lse_self"], v["attn_own"], send = self_forward(
        p.rank, v["frame_valid"], v["q_self"], v["k_self"], v["v_self"], v["w_out"]
    )
    v["attn_other"] = swap_cores(send)


def stage_norm_two(p):
    v = p.v
    v["hidden_one"], v["n2_own"], v["square_attn"] = residual_norm(
        p.rank, v["frame_valid"], v["tokens"], v["attn_own"], v["attn_other"],
        v["gain_two"], v["bias_two"],
    )
    v["n2_other"] = swap_cores(v["n2_own"])


def stage_cross(p):
    v = p.v
    v["q_cross"], v["mix_cross"], v["lse_cross"], v["cross_own"], send = cross_forward(
        p.rank, v["text_len"], v["n2_own"], v["n2_other"], v["c_query"],
        v["k_cross"], v["v_cross"], v["c_out"],
    )
    v["cross_other"] = swap_cores(send)


def stage_norm_three(p):
    v = p.v
    v["hidden_two"], v["n3_own"], v["square_cross"] = residual_norm(
        p.rank, v["frame_valid"], v["hidden_one"], v["cross_own"], v["cross_other"],
        v["gain_three"], v["bias_three"],
    )
    v["n3_other"] = swap_cores(v["n3_own"])


def flat(values):
    return values.reshape(-1, values.shape[-1])


def stage_units(p):
    v = p.v
    units, width = v["w_down"].shape
    v["activated"], v["grad_up"], pairs = feed_forward(
        p.block, ORDERS, flat(v["n3_own"]), flat(v["n3_other"]), flat(v["grad_own"]),
        flat(v["grad_other"]), v["w_up"], v["w_down"],
    )
    down = [Piece(None, units, at, LANES, None, width) for at in (0, LANES)]
    up = [
        Piece(None, width, 0, units - LANES, None, units),
        Piece(None, width, units - LANES, LANES, None, units),
    ]
    p.add("down", pairs["down"], down[:1], ["d_w_down"])
    p.add("up", pairs["up"], up[:1], ["d_w_up"])
    p.add("rest", pairs["rest"], [down[1], up[1]], ["d_w_down", "d_w_up"])


HALF_TERMS = [((0, (0,)), (1, ())), ((0, (1,)), (2, ()))]


def stage_back_units(p):
    v = p.v
    own, send = project_halves(v["grad_up"], v["w_up"], True)
    shape = v["hidden_two"].shape
    v["gn3_own"], v["gn3_other"] = own.reshape(shape), swap_cores(send).reshape(shape)


def stage_back_three(p):
    v = p.v
    v["g_h2"], v["d_gain_three"], v["d_bias_three"], v["g_cross_own"] = norm_backward(
        p.rank, v["hidden_two"], v["gain_three"], v["gn3_own"], v["gn3_other"],
        v["grad_own"], False,
    )
    v["g_cross_other"] = swap_cores(v["g_cross_own"])


def stage_out(p):
    v = p.v
    own, send = project_halves(v["activated"], v["w_down"], False)
    shape = v["hidden_two"].shape
    v["ff_own"], v["ff_other"] = own.reshape(shape), swap_cores(send).reshape(shape)


def stage_result(p):
    v = p.v
    v["out"], v["square_out"], v["square_ff"] = finish_output(
        p.rank, v["frame_valid"], v["hidden_two"], v["ff_own"], v["ff_other"]
    )


def stage_back_cross(p):
    v = p.v
    (
        v["dq_cross"], v["dk_cross"], v["dv_cross"], v["gn2_own"], send,
        v["text_grad_own"], text_send,
    ) = cross_backward(
        p.rank, v["text_len"], v["g_cross_own"], v["g_cross_other"], v["c_out"],
        v["q_cross"], v["k_cross"], v["v_cross"], v["lse_cross"],
        v["c_query"], v["c_key"], v["c_value"],
    )
    v["gn2_other"] = swap_cores(send)
    v["text_grad_other"] = swap_cores(text_send)


def halves(values):
    return values.reshape(2, -1, values.shape[-1])


def stage_cross_packet(p):
    v = p.v
    items, _, _, local = v["dk_cross"].shape
    depth = v["c_key"].shape[0]
    width = v["c_query"].shape[0]
    query_terms = [((1, ()), (0, (0,))), ((2, ()), (0, (1,)))]

    def text_terms(place):
        return [
            ((3 + half, (item,)), (place, (item, half))) for item in range(items) for half in (0, 1)
        ]

    p.packet(
        "cross", ["d_c_query", "d_c_key", "d_c_value"],
        [
            Piece(query_terms, width, 0, local, width, local),
            Piece(text_terms(5), depth, 0, local, depth, local),
            Piece(text_terms(6), depth, 0, local, depth, local),
        ],
        [
            halves(v["dq_cross"]), flat(v["n2_own"]), flat(v["n2_other"]),
            v["text_own"], v["text_other"], v["dk_cross"], v["dv_cross"],
        ],
    )


def stage_back_two(p):
    v = p.v
    v["g_h1"], v["d_gain_two"], v["d_bias_two"], v["g_attn_own"] = norm_backward(
        p.rank, v["hidden_one"], v["gain_two"], v["gn2_own"], v["gn2_other"], v["g_h2"], False
    )
    v["g_attn_other"] = swap_cores(v["g_attn_own"])


def stage_back_self(p):
    v = p.v
    v["dq_self"], v["dk_self"], v["dv_self"], v["gn1_own"], send = self_backward(
        p.rank, v["frame_valid"], v["g_attn_own"], v["g_attn_other"], v["w_out"],
        v["q_self"], v["k_self"], v["v_self"], v["lse_self"],
        v["w_query"], v["w_key"], v["w_value"],
    )
    v["gn1_other"] = swap_cores(send)


def stage_proj_packet(p):
    v = p.v
    local, width = v["w_out"].shape
    terms = [((3, (0,)), (4, ())), ((3, (1,)), (5, ()))]
    steps = width // LANES

    def streamed(name, first):
        return (flat(v[name]), 1, (0, first), steps, LANES)

    p.packet(
        "proj", ["d_c_out", "d_w_out"],
        [
            Piece(HALF_TERMS, local, 0, width, local, width),
            Piece(terms, local, 0, width, local, width),
        ],
        [
            halves(v["mix_cross"]), streamed("g_cross_own", 0), streamed("g_cross_other", 0),
            halves(v["mix_self"]), streamed("g_attn_own", steps),
            streamed("g_attn_other", steps),
        ],
    )


def self_packet(p, name, grad, out):
    v = p.v
    width, local = v["w_query"].shape
    piece = Piece([((0, ()), (1, ()))], width, 0, local, width, local)
    p.packet(name, [out], [piece], [v["normed_one"], flat(v[grad])])


def stage_query_packet(p):
    self_packet(p, "query", "dq_self", "d_w_query")


def stage_key_packet(p):
    self_packet(p, "key", "dk_self", "d_w_key")


def stage_value_packet(p):
    self_packet(p, "value", "dv_self", "d_w_value")


def stage_back_one(p):
    v = p.v
    v["d_tokens"], v["d_gain_one"], v["d_bias_one"] = norm_backward(
        p.rank, v["tokens"], v["gain_one"], v["gn1_own"], v["gn1_other"], v["g_h1"], True
    )


def stage_text_grad(p):
    v = p.v
    v["d_text"] = v["text_grad_own"] + v["text_grad_other"].astype(F32)


SMALL = (
    "d_gain_one", "d_bias_one", "d_gain_two", "d_bias_two", "d_gain_three", "d_bias_three",
    "square_out", "square_attn", "square_cross", "square_ff",
)


def stage_small(p):
    v = p.v
    half = v["hidden_one"].shape[1]
    width = v["hidden_one"].shape[2]
    own = jnp.clip(v["frame_valid"] - p.rank * half, 0, half).sum().astype(F32)
    rows = [v[name] for name in SMALL] + [jnp.full((1, width), own / width, F32)]
    rows.append(jnp.zeros((16 - len(rows), width), F32))
    total = p.tie(jnp.concatenate(rows, 0))
    v["small"] = total
    v["small_other"] = swap_cores(total)
    p.hops = list(range(lax.axis_size("dp").bit_length() - 1))


def stage_hop(p):
    v = p.v
    total = v["small"] = p.tie(v["small"] + v["small_other"])
    if p.hops:
        v["small_other"] = exchange(total, p.hops.pop(0))


def stage_rms(p):
    v = p.v
    while p.hops:
        stage_hop(p)
    total = v["small"] + v["small_other"]
    width = total.shape[1]
    v["small"] = total[:6]
    sums = jnp.sum(total[6:11], -1)
    v["rms"] = jnp.sqrt(sums[:4] / (sums[4] * width))


def stage_end(p):
    p.v["rms"] = p.v["rms"] + p.token[0, :4] * 0.0


ORDERS = {
    "down": [2, 0, 1, 3],
    "up": [0, 1, 2, 3],
    "rest": [1, 0, 2, 3],
    "cross": [2, 1, 0, 3],
    "proj": [1, 0, 3, 2],
    "query": [0, 1, 2, 3],
    "key": [1, 0, 3, 2],
    "value": [0, 1, 2, 3],
}

CHAIN = dict(
    text=("text_own", "k_cross"), tokens=("tokens", "q_self"), self=("q_self", "attn_own"),
    norm_two=("attn_own", "n2_own"), cross=("n2_own", "cross_own"),
    norm_three=("cross_own", "n3_own"), units=("n3_own", "grad_up"),
    back_units=("grad_up", "gn3_own"), back_three=("gn3_own", "g_cross_own"),
    out=("activated", "ff_own"), result=("ff_own", "out"), back_cross=("g_cross_own", "gn2_own"),
    back_two=("gn2_own", "g_attn_own"), back_self=("g_attn_own", "gn1_own"),
    back_one=("gn1_own", "d_tokens"), text_grad=("text_grad_own", "d_text"),
)

STAGES = dict(
    text=stage_text, tokens=stage_tokens, self=stage_self, norm_two=stage_norm_two,
    cross=stage_cross, norm_three=stage_norm_three, units=stage_units,
    back_units=stage_back_units, back_three=stage_back_three, out=stage_out,
    result=stage_result, back_cross=stage_back_cross, cross_packet=stage_cross_packet, proj_packet=stage_proj_packet,
    query_packet=stage_query_packet, key_packet=stage_key_packet,
    value_packet=stage_value_packet,
    back_two=stage_back_two, back_self=stage_back_self,
    back_one=stage_back_one, text_grad=stage_text_grad,
    small=stage_small, hop=stage_hop, rms=stage_rms, end=stage_end,
)

PLAN = [
    ("do", "tokens"), ("do", "self"), ("do", "text"), ("do", "norm_two"), ("do", "cross"),
    ("do", "norm_three"), ("do", "units"), ("send", "rest"), ("send", "up"), ("send", "down"),
    ("do", "back_units"), ("do", "back_three"), ("do", "back_cross"), ("take", "down"),
    ("take", "rest"), ("take", "up"), ("do", "cross_packet"), ("do", "back_two"),
    ("send", "rest"), ("send", "up"), ("send", "cross"), ("send", "down"), ("do", "back_self"),
    ("take", "rest"), ("take", "up"), ("take", "down"), ("take", "cross"), ("do", "proj_packet"),
    ("do", "query_packet"), ("do", "key_packet"), ("do", "value_packet"), ("send", "rest"),
    ("send", "up"), ("send", "proj"), ("send", "cross"), ("send", "key"), ("send", "query"),
    ("send", "value"), ("send", "down"), ("take", "rest"), ("send", "rest"), ("do", "out"),
    ("do", "back_one"), ("take", "up"), ("send", "up"), ("take", "query"), ("take", "rest"),
    ("send", "rest"), ("take", "proj"), ("send", "proj"), ("send", "query"), ("take", "value"),
    ("take", "up"), ("send", "up"), ("do", "result"), ("take", "cross"), ("send", "cross"),
    ("send", "value"), ("take", "rest"), ("send", "rest"), ("take", "proj"), ("send", "proj"),
    ("take", "up"), ("send", "up"), ("take", "key"), ("send", "key"), ("take", "cross"),
    ("send", "cross"), ("take", "down"), ("take", "rest"), ("send", "rest"), ("send", "down"),
    ("take", "query"), ("take", "proj"), ("send", "proj"), ("take", "key"), ("take", "up"),
    ("send", "up"), ("send", "key"), ("take", "value"), ("take", "cross"), ("send", "cross"),
    ("take", "down"), ("send", "query"), ("take", "proj"), ("send", "proj"), ("take", "rest"),
    ("send", "rest"), ("take", "key"), ("send", "key"), ("take", "query"), ("send", "value"),
    ("take", "cross"), ("send", "cross"), ("send", "query"), ("take", "proj"), ("send", "proj"),
    ("take", "up"), ("send", "up"), ("take", "key"), ("send", "key"), ("take", "value"),
    ("send", "value"), ("take", "query"), ("send", "query"), ("take", "cross"),
    ("send", "cross"), ("take", "key"), ("send", "key"), ("take", "proj"), ("send", "proj"),
    ("send", "down"), ("take", "value"), ("send", "value"), ("take", "query"), ("send", "query"),
    ("take", "key"), ("send", "key"), ("take", "rest"), ("take", "down"), ("send", "down"),
    ("take", "value"), ("send", "value"), ("take", "query"), ("send", "query"),
    ("take", "cross"), ("send", "cross"), ("take", "up"), ("take", "value"), ("send", "value"),
    ("take", "down"), ("send", "down"), ("take", "proj"), ("send", "proj"), ("take", "query"),
    ("send", "query"), ("take", "key"), ("send", "key"), ("take", "value"), ("send", "value"),
    ("do", "text_grad"), ("take", "down"), ("send", "down"), ("do", "small"), ("do", "hop"),
    ("take", "cross"), ("do", "hop"), ("take", "query"), ("take", "proj"), ("do", "hop"),
    ("do", "hop"), ("do", "rms"), ("take", "value"), ("take", "key"), ("take", "down"),
    ("do", "end"),
]

NAMES = (
    "tokens", "text_own", "text_len", "frame_valid", "gain_one", "bias_one", "gain_two",
    "bias_two", "gain_three", "bias_three", "w_query", "w_key", "w_value", "w_out", "c_query",
    "c_key", "c_value", "c_out", "w_up", "w_down", "grad_own",
)


def per_device(*args):
    given = dict(zip(NAMES, args))
    for name in NAMES[4:10]:
        given[name] = given[name].reshape(1, -1)
    p = Program(given)
    p.rank = lax.axis_index("mp").astype(jnp.int32).reshape(1)
    p.main, p.extra = main_bits()
    place = lax.axis_index("dp")
    p.block = sum(((place >> bit) & 1) << k for k, bit in enumerate(p.main))
    p.block = p.block.astype(jnp.int32).reshape(1)
    v = p.v
    v["text_other"] = swap_cores(v["text_own"])
    v["grad_other"] = swap_cores(v["grad_own"])
    for kind, name in PLAN:
        if kind == "do":
            before, after = CHAIN.get(name, (None, None))
            if before:
                v[before] = p.tie(v[before])
            STAGES[name](p)
            if after:
                v[after] = p.tie(v[after])
        elif kind == "send":
            p.start(name)
        else:
            p.finish(name)
    return (
        v["out"],
        v["d_tokens"],
        v["d_text"],
        *(v["small"][n] for n in range(6)),
        *(v["d_" + name] for name in NAMES[10:20]),
        v["rms"],
    )


def solution(mesh):
    split = P("dp", "mp", None)
    columns, rows = P(None, "mp"), P("mp", None)
    weights = (columns,) * 3 + (rows,) + (columns,) * 3 + (rows, columns, rows)
    return jax.shard_map(
        per_device,
        mesh=mesh,
        in_specs=(P("dp", None, None), split, P("dp"), P("dp"))
        + (P(),) * 6
        + weights
        + (split,),
        out_specs=(split,) * 3 + (P(),) * 6 + weights + (P(),),
        check_vma=False,
    )
```

```python
import math
from types import SimpleNamespace

import jax
import jax.numpy as jnp
from jax import lax
from jax.experimental import pallas as pl
from jax.experimental.pallas import tpu as pltpu
from jax.sharding import PartitionSpec as P

HD = 64
PAIR = 2 * HD
norm_eps = 1e-05
score_scale = 0.125
masked_fill = -1e30
F32 = jnp.float32
BF16 = jnp.bfloat16
SLACK_BYTES = 6 * 1024 * 1024
SMEM_SPEC = pl.BlockSpec(memory_space=pltpu.SMEM)


def dot(a, b):
    return lax.dot_general(a, b, (((1,), (0,)), ((), ())), preferred_element_type=F32)


def dot_rt(a, b):
    return lax.dot_general(a, b, (((1,), (1,)), ((), ())), preferred_element_type=F32)


def dot_lt(a, b):
    return lax.dot_general(a, b, (((0,), (0,)), ((), ())), preferred_element_type=F32)


def whole(shape):
    zeros = (0,) * len(shape)
    return pl.BlockSpec(tuple(shape), lambda *_: zeros)


def shape_of(shape, kind):
    return jax.ShapeDtypeStruct(tuple(shape), kind)


def vmem_bytes(specs, arrays, scratch=()):
    total = SLACK_BYTES
    for spec, array in zip(specs, arrays):
        if spec.block_shape is not None:
            total += 2 * math.prod(spec.block_shape) * jnp.dtype(array.dtype).itemsize
    for buffer in scratch:
        total += math.prod(buffer.shape) * jnp.dtype(buffer.dtype).itemsize
    return min(total, 60 * 1024 * 1024)


def call(body, grid, in_specs, out_specs, out_shape, args, scratch=(), flops=0):
    return pl.pallas_call(
        body,
        grid=grid,
        in_specs=in_specs,
        out_specs=out_specs,
        out_shape=out_shape,
        scratch_shapes=list(scratch),
        compiler_params=pltpu.CompilerParams(
            vmem_limit_bytes=vmem_bytes(
                [*in_specs, *out_specs], [*args, *out_shape], scratch
            )
        ),
        cost_estimate=pl.CostEstimate(flops=flops, bytes_accessed=1024, transcendentals=0),
    )(*args)


def norm_parts(values):
    average = jnp.mean(values, -1, keepdims=True)
    centered = values - average
    variance = jnp.mean(centered * centered, -1, keepdims=True)
    scale = lax.rsqrt(variance + norm_eps)
    return centered * scale, scale


def layer_norm(values, gain_ref, bias_ref):
    normed, _ = norm_parts(values)
    return normed * gain_ref[...].astype(F32) + bias_ref[...].astype(F32)


ROW_BLOCK = 256


def add_row(ref, row):
    first = (pl.program_id(0) == 0) & (pl.program_id(1) == 0)

    @pl.when(first)
    def _():
        ref[...] = row

    @pl.when(jnp.logical_not(first))
    def _():
        ref[...] += row


def column_sum(values):
    return jnp.sum(values, 0, keepdims=True)


def row_mask(rank_ref, half, count):
    first_row = rank_ref[0] * half + pl.program_id(1) * ROW_BLOCK
    place = first_row + lax.broadcasted_iota(jnp.int32, (ROW_BLOCK, 1), 0)
    return (place < count).astype(F32)


def project_tokens(tokens, gain, bias, w_query, w_key, w_value):
    rows, width = tokens.shape
    local = w_query.shape[1]
    block = 256

    def body(x, g, b, wq, wk, wv, n, q, k, v):
        normed = layer_norm(x[...].astype(F32), g, b).astype(BF16)
        n[...] = normed
        q[...] = dot(normed, wq[...]).astype(BF16)
        k[...] = dot(normed, wk[...]).astype(BF16)
        v[...] = dot(normed, wv[...]).astype(BF16)

    wide = pl.BlockSpec((block, width), lambda i: (i, 0))
    slim = pl.BlockSpec((block, local), lambda i: (i, 0))
    return call(
        body,
        (rows // block,),
        [wide, whole((1, width)), whole((1, width))] + [whole(w_query.shape)] * 3,
        [wide, slim, slim, slim],
        [shape_of((rows, width), BF16)] + [shape_of((rows, local), BF16)] * 3,
        (tokens, gain, bias, w_query, w_key, w_value),
    )


def project_text(text_own, text_other, c_key, c_value):
    items, text_half, depth = text_own.shape
    local = c_key.shape[1]

    def body(own, other, wk, wv, k, v):
        for half, rows in enumerate((own, other)):
            for item in range(items):
                k[item, half] = dot(rows[item], wk[...]).astype(BF16)
                v[item, half] = dot(rows[item], wv[...]).astype(BF16)

    shape = (items, 2, text_half, local)
    return call(
        body,
        (1,),
        [whole(text_own.shape)] * 2 + [whole(c_key.shape)] * 2,
        [whole(shape)] * 2,
        [shape_of(shape, BF16)] * 2,
        (text_own, text_other, c_key, c_value),
    )


def head_mask(rows, head):
    lane = lax.broadcasted_iota(jnp.int32, (rows, PAIR), 1)
    return lane < HD if head == 0 else lane >= HD


def pick(first, second):
    return jnp.where(head_mask(first.shape[0], 0), first, second)


def only(values, head):
    return jnp.where(head_mask(values.shape[0], head), values, jnp.zeros_like(values))


def scores_t(query_pair, key_pair, head, allowed):
    scores = dot_rt(key_pair, only(query_pair, head)) * score_scale
    return jnp.where(allowed, scores, masked_fill)


def attend_pair(query_pair, key_pair, value_pair, allowed, lse_ref, lse_at):
    mixed = []
    for head in range(2):
        scores = scores_t(query_pair, key_pair, head, allowed)
        highest = jnp.max(scores, 0, keepdims=True)
        powers = jnp.exp(scores - highest)
        total = jnp.sum(powers, 0, keepdims=True)
        probs = (powers / total).astype(BF16)
        mixed.append(dot_lt(probs, value_pair))
        row, columns = lse_at(head)
        lse_ref[0, row : row + 1, columns] = highest + jnp.log(total)
    return pick(mixed[0], mixed[1]).astype(BF16)


def attend_pair_back(query_pair, key_pair, value_pair, allowed, lse_rows, grad_pair):
    grads = []
    for head in range(2):
        probs = jnp.exp(scores_t(query_pair, key_pair, head, allowed) - lse_rows[head])
        grad_probs = dot_rt(value_pair, only(grad_pair, head))
        inner = jnp.sum(grad_probs * probs, 0, keepdims=True)
        grad_scores = (probs * (grad_probs - inner)).astype(BF16)
        grads.append(
            (
                dot_lt(grad_scores, key_pair),
                dot(grad_scores, query_pair),
                dot(probs.astype(BF16), grad_pair),
            )
        )
    return [pick(one, two) for one, two in zip(grads[0], grads[1])]


def causal_mask(keys, queries, first_query, count):
    key_at = lax.broadcasted_iota(jnp.int32, (keys, queries), 0)
    query_at = first_query + lax.broadcasted_iota(jnp.int32, (keys, queries), 1)
    return (key_at <= query_at) & (key_at < count)


def text_mask(text_half, queries, rank, count):
    key_at = lax.broadcasted_iota(jnp.int32, (2 * text_half, queries), 0)
    swapped = jnp.where(key_at < text_half, key_at + text_half, key_at - text_half)
    return jnp.where(rank == 0, key_at, swapped) < count


def self_forward(rank, valid, query, key, value, w_out):
    items, frames, local = query.shape
    width = w_out.shape[1]
    half = frames // 2
    heads = local // HD

    def body(rank_ref, valid_ref, q, k, v, w, mix, lse, own, send):
        me = rank_ref[0]
        count = valid_ref[pl.program_id(0)]
        for part in range(2):
            keys = (part + 1) * half
            allowed = causal_mask(keys, half, part * half, count)
            rows = slice(part * half, (part + 1) * half)
            for pair in range(local // PAIR):
                columns = slice(pair * PAIR, (pair + 1) * PAIR)
                mix[part ^ me, 0, :, columns] = attend_pair(
                    q[0, rows, columns],
                    k[0, :keys, columns],
                    v[0, :keys, columns],
                    allowed,
                    lse,
                    lambda head: (2 * pair + head, rows),
                )
        send[0] = dot(mix[1, 0], w[...]).astype(BF16)
        own[0] = dot(mix[0, 0], w[...])

    tall = pl.BlockSpec((1, frames, local), lambda i: (i, 0, 0))
    out = pl.BlockSpec((1, half, width), lambda i: (i, 0, 0))
    return call(
        body,
        (items,),
        [SMEM_SPEC, SMEM_SPEC, tall, tall, tall, whole(w_out.shape)],
        [
            pl.BlockSpec((2, 1, half, local), lambda i: (0, i, 0, 0)),
            pl.BlockSpec((1, heads, frames), lambda i: (i, 0, 0)),
            out,
            out,
        ],
        [
            shape_of((2, items, half, local), BF16),
            shape_of((items, heads, frames), F32),
            shape_of((items, half, width), F32),
            shape_of((items, half, width), BF16),
        ],
        (rank, valid, query, key, value, w_out),
    )


def cross_forward(rank, text_len, normed_own, normed_other, c_query, key, value, c_out):
    items, half, width = normed_own.shape
    text_half = key.shape[2]
    local = c_query.shape[1]
    heads = local // HD

    def body(rank_ref, len_ref, own_n, other_n, wq, k, v, w, q, mix, lse, own, send):
        allowed = text_mask(text_half, half, rank_ref[0], len_ref[pl.program_id(0)])
        for part, normed in enumerate((own_n, other_n)):
            q[part, 0] = dot(normed[0], wq[...]).astype(BF16)
            for pair in range(local // PAIR):
                columns = slice(pair * PAIR, (pair + 1) * PAIR)
                mix[part, 0, :, columns] = attend_pair(
                    q[part, 0, :, columns],
                    k[0, :, :, columns].reshape(2 * text_half, PAIR),
                    v[0, :, :, columns].reshape(2 * text_half, PAIR),
                    allowed,
                    lse,
                    lambda head: (2 * pair + head, slice(part * half, (part + 1) * half)),
                )
        send[0] = dot(mix[1, 0], w[...]).astype(BF16)
        own[0] = dot(mix[0, 0], w[...])

    out = pl.BlockSpec((1, half, width), lambda i: (i, 0, 0))
    text = pl.BlockSpec((1, 2, text_half, local), lambda i: (i, 0, 0, 0))
    both = pl.BlockSpec((2, 1, half, local), lambda i: (0, i, 0, 0))
    return call(
        body,
        (items,),
        [SMEM_SPEC, SMEM_SPEC, out, out, whole(c_query.shape), text, text, whole(c_out.shape)],
        [both, both, pl.BlockSpec((1, heads, 2 * half), lambda i: (i, 0, 0)), out, out],
        [
            shape_of((2, items, half, local), BF16),
            shape_of((2, items, half, local), BF16),
            shape_of((items, heads, 2 * half), F32),
            shape_of((items, half, width), F32),
            shape_of((items, half, width), BF16),
        ],
        (rank, text_len, normed_own, normed_other, c_query, key, value, c_out),
    )


def residual_norm(rank, valid, base, own, received, gain, bias):
    items, half, width = own.shape

    def body(rank_ref, valid_ref, x, part, other, g, b, hidden, normed, square):
        item = pl.program_id(0)
        branch = part[0] + other[0].astype(F32)
        total = x[0].astype(F32) + branch
        hidden[0] = total
        normed[0] = layer_norm(total, g, b).astype(BF16)
        mask = row_mask(rank_ref, half, valid_ref[item])
        add_row(square, column_sum(mask * branch * branch))

    steps = half // ROW_BLOCK
    block = pl.BlockSpec((1, ROW_BLOCK, width), lambda i, r, *_: (i, r, 0))
    row = whole((1, width))
    if base.shape[1] == half:
        base_spec = block
    else:
        base_spec = pl.BlockSpec(
            (1, ROW_BLOCK, width), lambda i, r, me, _: (i, me[0] * steps + r, 0)
        )
    return pl.pallas_call(
        body,
        grid_spec=pltpu.PrefetchScalarGridSpec(
            num_scalar_prefetch=2,
            grid=(items, steps),
            in_specs=[base_spec, block, block, row, row],
            out_specs=[block, block, row],
        ),
        out_shape=[
            shape_of(own.shape, F32),
            shape_of(own.shape, BF16),
            shape_of((1, width), F32),
        ],
        compiler_params=pltpu.CompilerParams(vmem_limit_bytes=3 * SLACK_BYTES),
        cost_estimate=pl.CostEstimate(flops=0, bytes_accessed=1024, transcendentals=0),
    )(rank, valid, base, own, received, gain, bias)


def gelu_parts(values):
    normal = 0.5 * (1.0 + lax.erf(values * (0.5**0.5)))
    density = jnp.exp(-0.5 * values * values) * 0.3989422804014327
    return values * normal, normal + values * density


def feed_forward(
    block_index, orders, normed_own, normed_other, grad_own, grad_other, w_up, w_down
):
    rows, width = normed_own.shape
    units = w_up.shape[1]
    steps = units // LANES
    down_each, up_each = units // BLOCKS, width // BLOCKS
    sizes = {DOWN: down_each, UP: up_each * (steps - 1), REST: down_each + up_each}

    def body(me_ref, n_own, n_other, g_own, g_other, up_w, down_w, act, grad, *rest):
        me = me_ref[0]
        packets = {name: rest[2 * k : 2 * k + 2] for k, name in enumerate(sizes)}
        down_part, up_part = rest[2 * len(sizes) :]
        step = pl.program_id(0)
        down_sum, up_sum = 0.0, 0.0
        for half, (n, g) in enumerate(((n_own, g_own), (n_other, g_other))):
            value, slope = gelu_parts(dot(n[...], up_w[...]))
            act[half] = value.astype(BF16)
            grad[half] = (dot_rt(g[...], down_w[...]) * slope).astype(BF16)
            down_sum = down_sum + dot_lt(act[half], g[...])
            up_sum = up_sum + dot_lt(n[...], grad[half])
        down_part[...] = down_sum.astype(BF16)
        up_part[...] = up_sum.astype(BF16)

        def put(name, block, first, values):
            place = place_of(block ^ me, orders[name])
            keep, send = packets[name]
            where = pl.ds(first, values.shape[0])

            @pl.when(place < BLOCKS // 2)
            def _():
                keep[place, where, :] = values

            @pl.when(place >= BLOCKS // 2)
            def _():
                send[place - BLOCKS // 2, where, :] = values

        for sub in range(LANES // down_each):
            part = slice(sub * down_each, (sub + 1) * down_each)
            block = step * (LANES // down_each) + sub
            put(DOWN, block, 0, down_part[part, :LANES])
            put(REST, block, 0, down_part[part, LANES:])

        @pl.when(step < steps - 1)
        def _():
            for block in range(BLOCKS):
                part = slice(block * up_each, (block + 1) * up_each)
                put(UP, block, step * up_each, up_part[part, :])

        @pl.when(step == steps - 1)
        def _():
            for block in range(BLOCKS):
                part = slice(block * up_each, (block + 1) * up_each)
                put(REST, block, down_each, up_part[part, :])

    out = pl.BlockSpec((2, rows, LANES), lambda j: (0, 0, j))
    shapes = [(BLOCKS // 2, sizes[name], LANES) for name in sizes for _ in range(2)]
    results = call(
        body,
        (steps,),
        [SMEM_SPEC]
        + [whole(normed_own.shape)] * 4
        + [
            pl.BlockSpec((width, LANES), lambda j: (0, j)),
            pl.BlockSpec((LANES, width), lambda j: (j, 0)),
        ],
        [out, out] + [whole(shape) for shape in shapes],
        [shape_of((2, rows, units), BF16)] * 2 + [shape_of(shape, BF16) for shape in shapes],
        (block_index, normed_own, normed_other, grad_own, grad_other, w_up, w_down),
        scratch=[pltpu.VMEM((LANES, width), BF16), pltpu.VMEM((width, LANES), BF16)],
    )
    pairs = {name: results[2 + 2 * k : 4 + 2 * k] for k, name in enumerate(sizes)}
    return results[0], results[1], pairs


def project_halves(values, weight, transposed):
    _, rows, depth = values.shape
    width = weight.shape[0] if transposed else weight.shape[1]

    def body(a, w, own, send):
        multiply = dot_rt if transposed else dot
        product = multiply(a[0], w[...])

        @pl.when(pl.program_id(0) == 0)
        def _():
            send[...] = product.astype(BF16)

        @pl.when(pl.program_id(0) == 1)
        def _():
            own[...] = product

    return call(
        body,
        (2,),
        [pl.BlockSpec((1, rows, depth), lambda j: (1 - j, 0, 0)), whole(weight.shape)],
        [whole((rows, width))] * 2,
        [shape_of((rows, width), F32), shape_of((rows, width), BF16)],
        (values, weight),
    )


def finish_output(rank, valid, hidden, own, received):
    items, half, width = hidden.shape

    def body(rank_ref, valid_ref, x, part, other, out, square, branch_square):
        branch = part[0] + other[0].astype(F32)
        total = x[0] + branch
        out[0] = total.astype(BF16)
        mask = row_mask(rank_ref, half, valid_ref[pl.program_id(0)])
        add_row(square, column_sum(mask * total * total))
        add_row(branch_square, column_sum(mask * branch * branch))

    steps = half // ROW_BLOCK
    block = pl.BlockSpec((1, ROW_BLOCK, width), lambda i, r: (i, r, 0))
    return call(
        body,
        (items, steps),
        [SMEM_SPEC, SMEM_SPEC, block, block, block],
        [block, whole((1, width)), whole((1, width))],
        [shape_of(hidden.shape, BF16)] + [shape_of((1, width), F32)] * 2,
        (rank, valid, hidden, own, received),
    )


def norm_backward(rank, values, gain, own, received, grad_base, last):
    items, half, width = own.shape

    def body(rank_ref, x, g, part, other, base, *outs):
        normed, scale = norm_parts(x[0].astype(F32))
        grad = part[0] + other[0].astype(F32)
        add_row(outs[1], column_sum(grad * normed))
        add_row(outs[2], column_sum(grad))
        scaled = grad * g[...].astype(F32)
        first = jnp.mean(scaled, -1, keepdims=True)
        second = jnp.mean(scaled * normed, -1, keepdims=True)
        total = base[0].astype(F32) + scale * (scaled - first - normed * second)
        outs[0][0] = total
        if not last:
            outs[3][0] = total.astype(BF16)

    steps = half // ROW_BLOCK
    block = pl.BlockSpec((1, ROW_BLOCK, width), lambda i, r, *_: (i, r, 0))
    row = whole((1, width))
    if values.shape[1] == half:
        values_spec = block
    else:
        values_spec = pl.BlockSpec(
            (1, ROW_BLOCK, width), lambda i, r, me: (i, me[0] * steps + r, 0)
        )
    out_specs = [block, row, row]
    out_shape = [
        shape_of(own.shape, F32),
        shape_of((1, width), F32),
        shape_of((1, width), F32),
    ]
    if not last:
        out_specs.append(block)
        out_shape.append(shape_of(own.shape, BF16))
    return pl.pallas_call(
        body,
        grid_spec=pltpu.PrefetchScalarGridSpec(
            num_scalar_prefetch=1,
            grid=(items, steps),
            in_specs=[values_spec, row, block, block, block],
            out_specs=out_specs,
        ),
        out_shape=out_shape,
        compiler_params=pltpu.CompilerParams(vmem_limit_bytes=3 * SLACK_BYTES),
        cost_estimate=pl.CostEstimate(flops=0, bytes_accessed=1024, transcendentals=0),
    )(rank, values, gain, own, received, grad_base)


def cross_backward(
    rank, text_len, grad_own, grad_other, c_out, query, key, value, lse, c_query, c_key, c_value
):
    items, half, width = grad_own.shape
    text_half = key.shape[2]
    depth, local = c_key.shape
    heads = local // HD

    def body(
        rank_ref, len_ref, g_own, g_other, w, q, k, v, stats, wq, wk, wv,
        dq, dk, dv, own, send, text_own, text_send, grad_mix,
    ):
        allowed = text_mask(text_half, half, rank_ref[0], len_ref[pl.program_id(0)])
        for part, grad in enumerate((g_own, g_other)):
            grad_mix[part] = dot_rt(grad[0], w[...]).astype(BF16)
        for pair in range(local // PAIR):
            columns = slice(pair * PAIR, (pair + 1) * PAIR)
            key_sum, value_sum = 0.0, 0.0
            for part in range(2):
                rows = slice(part * half, (part + 1) * half)
                one, two, three = attend_pair_back(
                    q[part, 0, :, columns],
                    k[0, :, :, columns].reshape(2 * text_half, PAIR),
                    v[0, :, :, columns].reshape(2 * text_half, PAIR),
                    allowed,
                    [stats[0, 2 * pair + head : 2 * pair + head + 1, rows] for head in range(2)],
                    grad_mix[part, :, columns],
                )
                dq[part, 0, :, columns] = (one * score_scale).astype(BF16)
                key_sum, value_sum = key_sum + two, value_sum + three
            key_sum = (key_sum * score_scale).astype(BF16)
            value_sum = value_sum.astype(BF16)
            for part in range(2):
                rows = slice(part * text_half, (part + 1) * text_half)
                dk[0, part, :, columns] = key_sum[rows]
                dv[0, part, :, columns] = value_sum[rows]
        send[0] = dot_rt(dq[1, 0], wq[...]).astype(BF16)
        own[0] = dot_rt(dq[0, 0], wq[...])
        text_send[0] = (dot_rt(dk[0, 1], wk[...]) + dot_rt(dv[0, 1], wv[...])).astype(BF16)
        text_own[0] = dot_rt(dk[0, 0], wk[...]) + dot_rt(dv[0, 0], wv[...])

    out = pl.BlockSpec((1, half, width), lambda i: (i, 0, 0))
    text = pl.BlockSpec((1, 2, text_half, local), lambda i: (i, 0, 0, 0))
    both = pl.BlockSpec((2, 1, half, local), lambda i: (0, i, 0, 0))
    deep = pl.BlockSpec((1, text_half, depth), lambda i: (i, 0, 0))
    return call(
        body,
        (items,),
        [
            SMEM_SPEC, SMEM_SPEC, out, out, whole(c_out.shape), both, text, text,
            pl.BlockSpec((1, heads, 2 * half), lambda i: (i, 0, 0)),
            whole(c_query.shape), whole(c_key.shape), whole(c_value.shape),
        ],
        [both, text, text, out, out, deep, deep],
        [
            shape_of(query.shape, BF16),
            shape_of(key.shape, BF16),
            shape_of(key.shape, BF16),
            shape_of(grad_own.shape, F32),
            shape_of(grad_own.shape, BF16),
            shape_of((items, text_half, depth), F32),
            shape_of((items, text_half, depth), BF16),
        ],
        (
            rank, text_len, grad_own, grad_other, c_out, query, key, value, lse,
            c_query, c_key, c_value,
        ),
        scratch=[pltpu.VMEM((2, half, local), BF16)],
    )


def self_backward(
    rank, valid, grad_own, grad_other, w_out, query, key, value, lse, w_query, w_key, w_value
):
    items, half, width = grad_own.shape
    frames, local = query.shape[1:]
    heads = local // HD

    def body(
        rank_ref, valid_ref, g_own, g_other, w, q, k, v, stats, wq, wk, wv,
        dq, dk, dv, own, send, grad_mix,
    ):
        me = rank_ref[0]
        count = valid_ref[pl.program_id(0)]
        grad_mix[me] = dot_rt(g_own[0], w[...]).astype(BF16)
        grad_mix[1 - me] = dot_rt(g_other[0], w[...]).astype(BF16)
        masks = [causal_mask((part + 1) * half, half, part * half, count) for part in range(2)]
        for pair in range(local // PAIR):
            columns = slice(pair * PAIR, (pair + 1) * PAIR)
            sums = []
            for part in range(2):
                keys = (part + 1) * half
                rows = slice(part * half, keys)
                one, two, three = attend_pair_back(
                    q[0, rows, columns],
                    k[0, :keys, columns],
                    v[0, :keys, columns],
                    masks[part],
                    [stats[0, 2 * pair + head : 2 * pair + head + 1, rows] for head in range(2)],
                    grad_mix[part, :, columns],
                )
                dq[0, rows, columns] = (one * score_scale).astype(BF16)
                sums.append((two, three))
            (key_a, value_a), (key_b, value_b) = sums
            dk[0, :half, columns] = ((key_a + key_b[:half]) * score_scale).astype(BF16)
            dk[0, half:, columns] = (key_b[half:] * score_scale).astype(BF16)
            dv[0, :half, columns] = (value_a + value_b[:half]).astype(BF16)
            dv[0, half:, columns] = value_b[half:].astype(BF16)

        def back(part):
            rows = pl.ds(pl.multiple_of(part * half, half), half)
            return (
                dot_rt(dq[0, rows, :], wq[...])
                + dot_rt(dk[0, rows, :], wk[...])
                + dot_rt(dv[0, rows, :], wv[...])
            )

        send[0] = back(1 - me).astype(BF16)
        own[0] = back(me)

    out = pl.BlockSpec((1, half, width), lambda i: (i, 0, 0))
    tall = pl.BlockSpec((1, frames, local), lambda i: (i, 0, 0))
    return call(
        body,
        (items,),
        [
            SMEM_SPEC, SMEM_SPEC, out, out, whole(w_out.shape), tall, tall, tall,
            pl.BlockSpec((1, heads, frames), lambda i: (i, 0, 0)),
            whole(w_query.shape), whole(w_key.shape), whole(w_value.shape),
        ],
        [tall, tall, tall, out, out],
        [shape_of(query.shape, BF16)] * 3
        + [shape_of(grad_own.shape, F32), shape_of(grad_own.shape, BF16)],
        (
            rank, valid, grad_own, grad_other, w_out, query, key, value, lse,
            w_query, w_key, w_value,
        ),
        scratch=[pltpu.VMEM((2, half, local), BF16)],
    )


DOWN, UP, REST, CROSS, PROJ, QUERY, KEY, VALUE = range(8)
(
    D_W_QUERY,
    D_W_KEY,
    D_W_VALUE,
    D_W_OUT,
    D_C_QUERY,
    D_C_KEY,
    D_C_VALUE,
    D_C_OUT,
    D_W_UP,
    D_W_DOWN,
) = range(10)
BLOCKS = 16
LEVELS = 4
LANES = 512


class Piece:
    def __init__(self, terms, rows, first, width, tile, full):
        self.terms, self.rows, self.first = terms, rows, first
        self.width, self.tile, self.full = width, tile, full


def place_of(block, order):
    place = 0
    for k, bit in enumerate(order):
        place = place + (((block >> bit) & 1) << (LEVELS - 1 - k))
    return place


def block_at(place, order):
    return sum(((place >> (LEVELS - 1 - k)) & 1) << bit for k, bit in enumerate(order))


def gradient_packet(block_index, pieces, order, operands):
    rows_each = sum(piece.rows // BLOCKS * (piece.width // LANES) for piece in pieces)
    count = len(operands)
    starts = []
    steps = 0
    for piece in pieces:
        starts.append(steps)
        steps += piece.rows // piece.tile if piece.tile < piece.rows else piece.width // LANES

    def body(*refs):
        me = refs[0][0]
        given = refs[1 : 1 + count]
        keep, send, natural = refs[1 + count :]
        step = pl.program_id(0)
        offset = 0
        for start, piece in zip(starts, pieces):
            by_rows = piece.tile < piece.rows
            number = piece.rows // piece.tile if by_rows else piece.width // LANES
            each = piece.rows // BLOCKS

            @pl.when((step >= start) & (step < start + number))
            def _(start=start, piece=piece, by_rows=by_rows, each=each, offset=offset):
                total = None
                for (left, left_at), (right, right_at) in piece.terms:
                    term = dot_lt(given[left][left_at], given[right][right_at])
                    total = term if total is None else total + term
                natural[: piece.tile, :] = total.astype(BF16)
                at = step - start
                for sub in range(piece.tile // each):
                    block = (at * (piece.tile // each) + sub if by_rows else sub) ^ me
                    place = place_of(block, order)
                    base = offset if by_rows else offset + at * each
                    rows = pl.ds(base, each)
                    values = natural[sub * each : (sub + 1) * each, :]

                    @pl.when(place < BLOCKS // 2)
                    def _():
                        keep[place, rows, :] = values

                    @pl.when(place >= BLOCKS // 2)
                    def _():
                        send[place - BLOCKS // 2, rows, :] = values

            offset += each * (piece.width // LANES)

    def spec(array, axis, start, number, block):
        if axis is None:
            return whole(array.shape)
        shape = list(array.shape)
        shape[axis] = block
        first, at = start

        def index(i):
            place = [0] * len(shape)
            place[axis] = first + jnp.clip(i - at, 0, number - 1)
            return tuple(place)

        return pl.BlockSpec(tuple(shape), index)

    half_shape = (BLOCKS // 2, rows_each, LANES)
    return call(
        body,
        (steps,),
        [SMEM_SPEC] + [spec(*operand) for operand in operands],
        [whole(half_shape)] * 2,
        [shape_of(half_shape, BF16)] * 2,
        (block_index, *(operand[0] for operand in operands)),
        scratch=[pltpu.VMEM((max(piece.tile for piece in pieces), LANES), BF16)],
    )


def open_packet(block_index, pieces, order, kept, received, before):
    steps = 4
    group = BLOCKS // steps
    previous = [x for x in before if x is not None]

    def body(*refs):
        me = refs[0][0]
        low, high = refs[1], refs[2]
        outs = refs[3 + len(previous) :]
        for step in range(group):
            place = place_of((pl.program_id(0) * group + step) ^ me, order)
            inner = place & (BLOCKS // 2 - 1)
            upper = place >= BLOCKS // 2
            offset = 0
            for out, piece in zip(outs, pieces):
                each = piece.rows // BLOCKS
                for column in range(piece.width // LANES):
                    part = slice(offset, offset + each)
                    values = jnp.where(upper, high[inner, part, :], low[inner, part, :])
                    lanes = slice(column * LANES, (column + 1) * LANES)
                    out[step * each : (step + 1) * each, lanes] = values.astype(F32)
                    offset += each

    out_specs, out_shape, aliases = [], [], {}
    for number, (piece, old) in enumerate(zip(pieces, before)):
        at = piece.first // piece.width
        out_specs.append(
            pl.BlockSpec((piece.rows // steps, piece.width), lambda i, at=at: (i, at))
        )
        out_shape.append(shape_of((piece.rows, piece.full), F32))
        if old is not None:
            aliases[3 + len(aliases)] = number
    return pl.pallas_call(
        body,
        grid=(steps,),
        in_specs=[SMEM_SPEC, whole(kept.shape), whole(kept.shape)]
        + [pl.BlockSpec(memory_space=pl.ANY)] * len(previous),
        out_specs=out_specs,
        out_shape=out_shape,
        input_output_aliases=aliases,
        compiler_params=pltpu.CompilerParams(vmem_limit_bytes=3 * SLACK_BYTES),
        cost_estimate=pl.CostEstimate(flops=0, bytes_accessed=1024, transcendentals=0),
    )(block_index, kept, received, *previous)


def main_bits():
    bits = lax.axis_size("dp").bit_length() - 1
    along_x = (bits - 2) // 2
    main = [0, along_x, bits - 2, bits - 1]
    return main, [bit for bit in range(bits) if bit not in main]


def exchange(values, bit):
    pairs = [(d, d ^ (1 << bit)) for d in range(lax.axis_size("dp"))]
    return lax.ppermute(values, "dp", pairs)


def add_rounded(one, two):
    return (one.astype(F32) + two.astype(F32)).astype(BF16)


SWAP = [(0, 1), (1, 0)]


def swap_cores(values):
    return lax.ppermute(values, "mp", SWAP)


class Program:
    def __init__(self, given):
        self.v = given
        self.out = {}
        self.token = jnp.zeros((8, 128), F32)
        self.packets = {}

    def tie(self, values):
        values, self.token = lax.optimization_barrier((values, self.token))
        return values

    def start(self, name):
        packet = self.packets[name]
        order, step = packet.order, packet.step
        bit = (order + order[::-1])[step]
        if step < LEVELS:
            values = self.tie(packet.send)
        else:
            values = packet.keep = self.tie(packet.keep)
        packet.arrived = exchange(values, self.main[bit])

    def finish(self, name):
        packet = self.packets[name]
        step, keep = packet.step, packet.keep
        arrived = self.tie(packet.arrived)
        packet.arrived = None
        packet.step = step + 1
        if step < LEVELS - 1:
            half = keep.shape[0] // 2
            packet.send = add_rounded(keep[half:], arrived[half:])
            packet.keep = add_rounded(keep[:half], arrived[:half])
            packet.send = self.tie(packet.send)
        elif step == LEVELS - 1:
            keep = add_rounded(keep, arrived)
            for bit in self.extra:
                keep = add_rounded(keep, exchange(keep, bit))
            packet.keep = self.tie(keep)
        elif step < 2 * LEVELS - 1:
            packet.keep = self.tie(jnp.concatenate([keep, arrived], 0))
        else:
            outs = open_packet(
                self.block,
                packet.pieces,
                packet.order,
                keep,
                arrived,
                [self.out.get(out) for out in packet.outs],
            )
            for out, values in zip(packet.outs, outs):
                self.out[out] = values
            self.out[packet.outs[0]] = self.tie(outs[0])

    def packet(self, name, outs, pieces, operands):
        order = ORDERS[name]
        operands = [
            x if isinstance(x, tuple) else (x, None, None, None, None) for x in operands
        ]
        operands[0] = (self.tie(operands[0][0]), *operands[0][1:])
        self.add(name, gradient_packet(self.block, pieces, order, operands), pieces, outs)

    def add(self, name, halves_of, pieces, outs):
        keep, send = halves_of
        self.packets[name] = SimpleNamespace(
            order=ORDERS[name], step=0, keep=keep, send=self.tie(send), pieces=pieces,
            outs=outs, arrived=None,
        )


def stage_text(p):
    v = p.v
    v.text_own = p.tie(v.text_own)
    v.k_cross, v.v_cross = project_text(
        v.text_own, v.text_other, v.c_key, v.c_value
    )
    v.k_cross = p.tie(v.k_cross)


def stage_tokens(p):
    v = p.v
    v.tokens = p.tie(v.tokens)
    items, frames, width = v.tokens.shape
    normed, *heads = project_tokens(
        v.tokens.reshape(items * frames, width),
        v.gain_one,
        v.bias_one,
        v.w_query,
        v.w_key,
        v.w_value,
    )
    v.normed_one = normed
    v.q_self, v.k_self, v.v_self = [x.reshape(items, frames, -1) for x in heads]
    v.q_self = p.tie(v.q_self)


def stage_self(p):
    v = p.v
    v.q_self = p.tie(v.q_self)
    v.mix_self, v.lse_self, v.attn_own, send = self_forward(
        p.rank, v.frame_valid, v.q_self, v.k_self, v.v_self, v.w_out
    )
    v.attn_other = swap_cores(send)
    v.attn_own = p.tie(v.attn_own)


def stage_norm_two(p):
    v = p.v
    v.attn_own = p.tie(v.attn_own)
    v.hidden_one, v.n2_own, v.square_attn = residual_norm(
        p.rank, v.frame_valid, v.tokens, v.attn_own, v.attn_other,
        v.gain_two, v.bias_two,
    )
    v.n2_other = swap_cores(v.n2_own)
    v.n2_own = p.tie(v.n2_own)


def stage_cross(p):
    v = p.v
    v.n2_own = p.tie(v.n2_own)
    v.q_cross, v.mix_cross, v.lse_cross, v.cross_own, send = cross_forward(
        p.rank, v.text_len, v.n2_own, v.n2_other, v.c_query,
        v.k_cross, v.v_cross, v.c_out,
    )
    v.cross_other = swap_cores(send)
    v.cross_own = p.tie(v.cross_own)


def stage_norm_three(p):
    v = p.v
    v.cross_own = p.tie(v.cross_own)
    v.hidden_two, v.n3_own, v.square_cross = residual_norm(
        p.rank, v.frame_valid, v.hidden_one, v.cross_own, v.cross_other,
        v.gain_three, v.bias_three,
    )
    v.n3_other = swap_cores(v.n3_own)
    v.n3_own = p.tie(v.n3_own)


def flat(values):
    return values.reshape(-1, values.shape[-1])


def stage_units(p):
    v = p.v
    v.n3_own = p.tie(v.n3_own)
    units, width = v.w_down.shape
    v.activated, v.grad_up, pairs = feed_forward(
        p.block, ORDERS, flat(v.n3_own), flat(v.n3_other), flat(v.grad_own),
        flat(v.grad_other), v.w_up, v.w_down,
    )
    down = [Piece(None, units, at, LANES, None, width) for at in (0, LANES)]
    up = [
        Piece(None, width, 0, units - LANES, None, units),
        Piece(None, width, units - LANES, LANES, None, units),
    ]
    p.add(DOWN, pairs[DOWN], down[:1], [D_W_DOWN])
    p.add(UP, pairs[UP], up[:1], [D_W_UP])
    p.add(REST, pairs[REST], [down[1], up[1]], [D_W_DOWN, D_W_UP])
    v.grad_up = p.tie(v.grad_up)


HALF_TERMS = [((0, (0,)), (1, ())), ((0, (1,)), (2, ()))]


def stage_back_units(p):
    v = p.v
    v.grad_up = p.tie(v.grad_up)
    own, send = project_halves(v.grad_up, v.w_up, True)
    shape = v.hidden_two.shape
    v.gn3_own, v.gn3_other = own.reshape(shape), swap_cores(send).reshape(shape)
    v.gn3_own = p.tie(v.gn3_own)


def stage_back_three(p):
    v = p.v
    v.gn3_own = p.tie(v.gn3_own)
    v.g_h2, v.d_gain_three, v.d_bias_three, v.g_cross_own = norm_backward(
        p.rank, v.hidden_two, v.gain_three, v.gn3_own, v.gn3_other,
        v.grad_own, False,
    )
    v.g_cross_other = swap_cores(v.g_cross_own)
    v.g_cross_own = p.tie(v.g_cross_own)


def stage_out(p):
    v = p.v
    v.activated = p.tie(v.activated)
    own, send = project_halves(v.activated, v.w_down, False)
    shape = v.hidden_two.shape
    v.ff_own, v.ff_other = own.reshape(shape), swap_cores(send).reshape(shape)
    v.ff_own = p.tie(v.ff_own)


def stage_result(p):
    v = p.v
    v.ff_own = p.tie(v.ff_own)
    v.out, v.square_out, v.square_ff = finish_output(
        p.rank, v.frame_valid, v.hidden_two, v.ff_own, v.ff_other
    )
    v.out = p.tie(v.out)


def stage_back_cross(p):
    v = p.v
    v.g_cross_own = p.tie(v.g_cross_own)
    (
        v.dq_cross, v.dk_cross, v.dv_cross, v.gn2_own, send,
        v.text_grad_own, text_send,
    ) = cross_backward(
        p.rank, v.text_len, v.g_cross_own, v.g_cross_other, v.c_out,
        v.q_cross, v.k_cross, v.v_cross, v.lse_cross,
        v.c_query, v.c_key, v.c_value,
    )
    v.gn2_other = swap_cores(send)
    v.text_grad_other = swap_cores(text_send)
    v.gn2_own = p.tie(v.gn2_own)


def halves(values):
    return values.reshape(2, -1, values.shape[-1])


def stage_cross_packet(p):
    v = p.v
    items, _, _, local = v.dk_cross.shape
    depth = v.c_key.shape[0]
    width = v.c_query.shape[0]
    query_terms = [((1, ()), (0, (0,))), ((2, ()), (0, (1,)))]

    def text_terms(place):
        return [
            ((3 + half, (item,)), (place, (item, half))) for item in range(items) for half in (0, 1)
        ]

    p.packet(
        CROSS, [D_C_QUERY, D_C_KEY, D_C_VALUE],
        [
            Piece(query_terms, width, 0, local, width, local),
            Piece(text_terms(5), depth, 0, local, depth, local),
            Piece(text_terms(6), depth, 0, local, depth, local),
        ],
        [
            halves(v.dq_cross), flat(v.n2_own), flat(v.n2_other),
            v.text_own, v.text_other, v.dk_cross, v.dv_cross,
        ],
    )


def stage_back_two(p):
    v = p.v
    v.gn2_own = p.tie(v.gn2_own)
    v.g_h1, v.d_gain_two, v.d_bias_two, v.g_attn_own = norm_backward(
        p.rank, v.hidden_one, v.gain_two, v.gn2_own, v.gn2_other, v.g_h2, False
    )
    v.g_attn_other = swap_cores(v.g_attn_own)
    v.g_attn_own = p.tie(v.g_attn_own)


def stage_back_self(p):
    v = p.v
    v.g_attn_own = p.tie(v.g_attn_own)
    v.dq_self, v.dk_self, v.dv_self, v.gn1_own, send = self_backward(
        p.rank, v.frame_valid, v.g_attn_own, v.g_attn_other, v.w_out,
        v.q_self, v.k_self, v.v_self, v.lse_self,
        v.w_query, v.w_key, v.w_value,
    )
    v.gn1_other = swap_cores(send)
    v.gn1_own = p.tie(v.gn1_own)


def stage_proj_packet(p):
    v = p.v
    local, width = v.w_out.shape
    terms = [((3, (0,)), (4, ())), ((3, (1,)), (5, ()))]
    steps = width // LANES

    def streamed(name, first):
        return (flat(name), 1, (0, first), steps, LANES)

    p.packet(
        PROJ, [D_C_OUT, D_W_OUT],
        [
            Piece(HALF_TERMS, local, 0, width, local, width),
            Piece(terms, local, 0, width, local, width),
        ],
        [
            halves(v.mix_cross), streamed(v.g_cross_own, 0), streamed(v.g_cross_other, 0),
            halves(v.mix_self), streamed(v.g_attn_own, steps),
            streamed(v.g_attn_other, steps),
        ],
    )


def self_packet(p, name, grad, out):
    v = p.v
    width, local = v.w_query.shape
    piece = Piece([((0, ()), (1, ()))], width, 0, local, width, local)
    p.packet(name, [out], [piece], [v.normed_one, flat(grad)])


def stage_query_packet(p):
    self_packet(p, QUERY, p.v.dq_self, D_W_QUERY)


def stage_key_packet(p):
    self_packet(p, KEY, p.v.dk_self, D_W_KEY)


def stage_value_packet(p):
    self_packet(p, VALUE, p.v.dv_self, D_W_VALUE)


def stage_back_one(p):
    v = p.v
    v.gn1_own = p.tie(v.gn1_own)
    v.d_tokens, v.d_gain_one, v.d_bias_one = norm_backward(
        p.rank, v.tokens, v.gain_one, v.gn1_own, v.gn1_other, v.g_h1, True
    )
    v.d_tokens = p.tie(v.d_tokens)


def stage_text_grad(p):
    v = p.v
    v.text_grad_own = p.tie(v.text_grad_own)
    v.d_text = v.text_grad_own + v.text_grad_other.astype(F32)
    v.d_text = p.tie(v.d_text)


def stage_small(p):
    v = p.v
    half = v.hidden_one.shape[1]
    width = v.hidden_one.shape[2]
    own = jnp.clip(v.frame_valid - p.rank * half, 0, half).sum().astype(F32)
    rows = [
        v.d_gain_one, v.d_bias_one, v.d_gain_two, v.d_bias_two,
        v.d_gain_three, v.d_bias_three, v.square_out, v.square_attn,
        v.square_cross, v.square_ff, jnp.full((1, width), own / width, F32),
    ]
    rows.append(jnp.zeros((16 - len(rows), width), F32))
    total = p.tie(jnp.concatenate(rows, 0))
    v.small = total
    v.small_other = swap_cores(total)
    p.hops = list(range(lax.axis_size("dp").bit_length() - 1))


def stage_hop(p):
    v = p.v
    total = v.small = p.tie(v.small + v.small_other)
    if p.hops:
        v.small_other = exchange(total, p.hops.pop(0))


def stage_rms(p):
    v = p.v
    while p.hops:
        stage_hop(p)
    total = v.small + v.small_other
    width = total.shape[1]
    v.small = total[:6]
    sums = jnp.sum(total[6:11], -1)
    v.rms = jnp.sqrt(sums[:4] / (sums[4] * width))


def stage_end(p):
    p.v.rms = p.v.rms + p.token[0, :4] * 0.0


ORDERS = {
    DOWN: [2, 0, 1, 3],
    UP: [0, 1, 2, 3],
    REST: [1, 0, 2, 3],
    CROSS: [2, 1, 0, 3],
    PROJ: [1, 0, 3, 2],
    QUERY: [0, 1, 2, 3],
    KEY: [1, 0, 3, 2],
    VALUE: [0, 1, 2, 3],
}


PLAN = [
    stage_tokens, stage_self, stage_text, stage_norm_two, stage_cross, stage_norm_three,
    stage_units, REST, UP, DOWN, stage_back_units, stage_back_three, stage_back_cross, DOWN,
    REST, UP, stage_cross_packet, stage_back_two, REST, UP, CROSS, DOWN, stage_back_self, REST,
    UP, DOWN, CROSS, stage_proj_packet, stage_query_packet, stage_key_packet, stage_value_packet,
    REST, UP, PROJ, CROSS, KEY, QUERY, VALUE, DOWN, REST, REST, stage_out, stage_back_one, UP,
    UP, QUERY, REST, REST, PROJ, PROJ, QUERY, VALUE, UP, UP, stage_result, CROSS, CROSS, VALUE,
    REST, REST, PROJ, PROJ, UP, UP, KEY, KEY, CROSS, CROSS, DOWN, REST, REST, DOWN, QUERY, PROJ,
    PROJ, KEY, UP, UP, KEY, VALUE, CROSS, CROSS, DOWN, QUERY, PROJ, PROJ, REST, REST, KEY, KEY,
    QUERY, VALUE, CROSS, CROSS, QUERY, PROJ, PROJ, UP, UP, KEY, KEY, VALUE, VALUE, QUERY, QUERY,
    CROSS, CROSS, KEY, KEY, PROJ, PROJ, DOWN, VALUE, VALUE, QUERY, QUERY, KEY, KEY, REST, DOWN,
    DOWN, VALUE, VALUE, QUERY, QUERY, CROSS, CROSS, UP, VALUE, VALUE, DOWN, DOWN, PROJ, PROJ,
    QUERY, QUERY, KEY, KEY, VALUE, VALUE, stage_text_grad, DOWN, DOWN, stage_small, stage_hop,
    CROSS, stage_hop, QUERY, PROJ, stage_hop, stage_hop, stage_rms, VALUE, KEY, DOWN, stage_end,
]

def per_device(
    tokens,
    text_own,
    text_len,
    frame_valid,
    gain_one,
    bias_one,
    gain_two,
    bias_two,
    gain_three,
    bias_three,
    w_query,
    w_key,
    w_value,
    w_out,
    c_query,
    c_key,
    c_value,
    c_out,
    w_up,
    w_down,
    grad_own,
):
    v = SimpleNamespace()
    v.tokens = tokens
    v.text_own = text_own
    v.text_len = text_len
    v.frame_valid = frame_valid
    v.gain_one = gain_one.reshape(1, -1)
    v.bias_one = bias_one.reshape(1, -1)
    v.gain_two = gain_two.reshape(1, -1)
    v.bias_two = bias_two.reshape(1, -1)
    v.gain_three = gain_three.reshape(1, -1)
    v.bias_three = bias_three.reshape(1, -1)
    v.w_query = w_query
    v.w_key = w_key
    v.w_value = w_value
    v.w_out = w_out
    v.c_query = c_query
    v.c_key = c_key
    v.c_value = c_value
    v.c_out = c_out
    v.w_up = w_up
    v.w_down = w_down
    v.grad_own = grad_own
    p = Program(v)
    p.rank = lax.axis_index("mp").astype(jnp.int32).reshape(1)
    p.main, p.extra = main_bits()
    place = lax.axis_index("dp")
    p.block = sum(((place >> bit) & 1) << k for k, bit in enumerate(p.main))
    p.block = p.block.astype(jnp.int32).reshape(1)
    v.text_other = swap_cores(v.text_own)
    v.grad_other = swap_cores(v.grad_own)
    for action in PLAN:
        if callable(action):
            action(p)
        elif p.packets[action].arrived is None:
            p.start(action)
        else:
            p.finish(action)
    return (
        v.out,
        v.d_tokens,
        v.d_text,
        *(v.small[n] for n in range(6)),
        *(p.out[name] for name in range(10)),
        v.rms,
    )


def solution(mesh):
    split = P("dp", "mp", None)
    columns, rows = P(None, "mp"), P("mp", None)
    weights = (columns,) * 3 + (rows,) + (columns,) * 3 + (rows, columns, rows)
    return jax.shard_map(
        per_device,
        mesh=mesh,
        in_specs=(P("dp", None, None), split, P("dp"), P("dp"))
        + (P(),) * 6
        + weights
        + (split,),
        out_specs=(split,) * 3 + (P(),) * 6 + weights + (P(),),
        check_vma=False,
    )
```

```python
import math
from types import SimpleNamespace

import jax
import jax.numpy as jnp
from jax import lax
from jax.experimental import pallas as pl
from jax.experimental.pallas import tpu as pltpu
from jax.sharding import PartitionSpec as P

HD = 64
PAIR = 2 * HD
norm_eps = 1e-05
score_scale = 0.125
masked_fill = -1e30
F32 = jnp.float32
BF16 = jnp.bfloat16
SLACK_BYTES = 6 * 1024 * 1024
SMEM_SPEC = pl.BlockSpec(memory_space=pltpu.SMEM)


def dot(a, b):
    return lax.dot_general(a, b, (((1,), (0,)), ((), ())), preferred_element_type=F32)


def dot_rt(a, b):
    return lax.dot_general(a, b, (((1,), (1,)), ((), ())), preferred_element_type=F32)


def dot_lt(a, b):
    return lax.dot_general(a, b, (((0,), (0,)), ((), ())), preferred_element_type=F32)


def whole(shape):
    zeros = (0,) * len(shape)
    return pl.BlockSpec(tuple(shape), lambda *_: zeros)


def shape_of(shape, kind):
    return jax.ShapeDtypeStruct(tuple(shape), kind)


def vmem_bytes(specs, arrays, scratch=()):
    total = SLACK_BYTES
    for spec, array in zip(specs, arrays):
        if spec.block_shape is not None:
            total += 2 * math.prod(spec.block_shape) * jnp.dtype(array.dtype).itemsize
    for buffer in scratch:
        total += math.prod(buffer.shape) * jnp.dtype(buffer.dtype).itemsize
    return min(total, 60 * 1024 * 1024)


def call(body, grid, in_specs, out_specs, out_shape, args, scratch=(), flops=0):
    return pl.pallas_call(
        body,
        grid=grid,
        in_specs=in_specs,
        out_specs=out_specs,
        out_shape=out_shape,
        scratch_shapes=list(scratch),
        compiler_params=pltpu.CompilerParams(
            vmem_limit_bytes=vmem_bytes(
                [*in_specs, *out_specs], [*args, *out_shape], scratch
            )
        ),
        cost_estimate=pl.CostEstimate(flops=flops, bytes_accessed=1024, transcendentals=0),
    )(*args)


def norm_parts(values):
    average = jnp.mean(values, -1, keepdims=True)
    centered = values - average
    variance = jnp.mean(centered * centered, -1, keepdims=True)
    scale = lax.rsqrt(variance + norm_eps)
    return centered * scale, scale


def layer_norm(values, gain_ref, bias_ref):
    normed, _ = norm_parts(values)
    return normed * gain_ref[...].astype(F32) + bias_ref[...].astype(F32)


ROW_BLOCK = 256


def add_row(ref, row):
    first = (pl.program_id(0) == 0) & (pl.program_id(1) == 0)

    @pl.when(first)
    def _():
        ref[...] = row

    @pl.when(jnp.logical_not(first))
    def _():
        ref[...] += row


def column_sum(values):
    return jnp.sum(values, 0, keepdims=True)


def row_mask(rank_ref, half, count):
    first_row = rank_ref[0] * half + pl.program_id(1) * ROW_BLOCK
    place = first_row + lax.broadcasted_iota(jnp.int32, (ROW_BLOCK, 1), 0)
    return (place < count).astype(F32)


def project_tokens(tokens, gain, bias, w_query, w_key, w_value):
    rows, width = tokens.shape
    local = w_query.shape[1]
    block = 256

    def body(x, g, b, wq, wk, wv, n, q, k, v):
        normed = layer_norm(x[...].astype(F32), g, b).astype(BF16)
        n[...] = normed
        q[...] = dot(normed, wq[...]).astype(BF16)
        k[...] = dot(normed, wk[...]).astype(BF16)
        v[...] = dot(normed, wv[...]).astype(BF16)

    wide = pl.BlockSpec((block, width), lambda i: (i, 0))
    slim = pl.BlockSpec((block, local), lambda i: (i, 0))
    return call(
        body,
        (rows // block,),
        [wide, whole((1, width)), whole((1, width))] + [whole(w_query.shape)] * 3,
        [wide, slim, slim, slim],
        [shape_of((rows, width), BF16)] + [shape_of((rows, local), BF16)] * 3,
        (tokens, gain, bias, w_query, w_key, w_value),
    )


def project_text(text_own, text_other, c_key, c_value):
    items, text_half, depth = text_own.shape
    local = c_key.shape[1]

    def body(own, other, wk, wv, k, v):
        for half, rows in enumerate((own, other)):
            for item in range(items):
                k[item, half] = dot(rows[item], wk[...]).astype(BF16)
                v[item, half] = dot(rows[item], wv[...]).astype(BF16)

    shape = (items, 2, text_half, local)
    return call(
        body,
        (1,),
        [whole(text_own.shape)] * 2 + [whole(c_key.shape)] * 2,
        [whole(shape)] * 2,
        [shape_of(shape, BF16)] * 2,
        (text_own, text_other, c_key, c_value),
    )


def head_mask(rows, head):
    lane = lax.broadcasted_iota(jnp.int32, (rows, PAIR), 1)
    return lane < HD if head == 0 else lane >= HD


def pick(first, second):
    return jnp.where(head_mask(first.shape[0], 0), first, second)


def only(values, head):
    return jnp.where(head_mask(values.shape[0], head), values, jnp.zeros_like(values))


def scores_t(query_pair, key_pair, head, allowed):
    scores = dot_rt(key_pair, only(query_pair, head)) * score_scale
    return jnp.where(allowed, scores, masked_fill)


def attend_pair(query_pair, key_pair, value_pair, allowed, lse_ref, lse_at):
    mixed = []
    for head in range(2):
        scores = scores_t(query_pair, key_pair, head, allowed)
        highest = jnp.max(scores, 0, keepdims=True)
        powers = jnp.exp(scores - highest)
        total = jnp.sum(powers, 0, keepdims=True)
        probs = (powers / total).astype(BF16)
        mixed.append(dot_lt(probs, value_pair))
        row, columns = lse_at(head)
        lse_ref[0, row : row + 1, columns] = highest + jnp.log(total)
    return pick(mixed[0], mixed[1]).astype(BF16)


def attend_pair_back(query_pair, key_pair, value_pair, allowed, lse_rows, grad_pair):
    grads = []
    for head in range(2):
        probs = jnp.exp(scores_t(query_pair, key_pair, head, allowed) - lse_rows[head])
        grad_probs = dot_rt(value_pair, only(grad_pair, head))
        inner = jnp.sum(grad_probs * probs, 0, keepdims=True)
        grad_scores = (probs * (grad_probs - inner)).astype(BF16)
        grads.append(
            (
                dot_lt(grad_scores, key_pair),
                dot(grad_scores, query_pair),
                dot(probs.astype(BF16), grad_pair),
            )
        )
    return [pick(one, two) for one, two in zip(grads[0], grads[1])]


def causal_mask(keys, queries, first_query, count):
    key_at = lax.broadcasted_iota(jnp.int32, (keys, queries), 0)
    query_at = first_query + lax.broadcasted_iota(jnp.int32, (keys, queries), 1)
    return (key_at <= query_at) & (key_at < count)


def text_mask(text_half, queries, rank, count):
    key_at = lax.broadcasted_iota(jnp.int32, (2 * text_half, queries), 0)
    swapped = jnp.where(key_at < text_half, key_at + text_half, key_at - text_half)
    return jnp.where(rank == 0, key_at, swapped) < count


def self_forward(rank, valid, query, key, value, w_out):
    items, frames, local = query.shape
    width = w_out.shape[1]
    half = frames // 2
    heads = local // HD

    def body(rank_ref, valid_ref, q, k, v, w, mix, lse, own, send):
        me = rank_ref[0]
        count = valid_ref[pl.program_id(0)]
        for part in range(2):
            keys = (part + 1) * half
            allowed = causal_mask(keys, half, part * half, count)
            rows = slice(part * half, (part + 1) * half)
            for pair in range(local // PAIR):
                columns = slice(pair * PAIR, (pair + 1) * PAIR)
                mix[part ^ me, 0, :, columns] = attend_pair(
                    q[0, rows, columns],
                    k[0, :keys, columns],
                    v[0, :keys, columns],
                    allowed,
                    lse,
                    lambda head: (2 * pair + head, rows),
                )
        send[0] = dot(mix[1, 0], w[...]).astype(BF16)
        own[0] = dot(mix[0, 0], w[...])

    tall = pl.BlockSpec((1, frames, local), lambda i: (i, 0, 0))
    out = pl.BlockSpec((1, half, width), lambda i: (i, 0, 0))
    return call(
        body,
        (items,),
        [SMEM_SPEC, SMEM_SPEC, tall, tall, tall, whole(w_out.shape)],
        [
            pl.BlockSpec((2, 1, half, local), lambda i: (0, i, 0, 0)),
            pl.BlockSpec((1, heads, frames), lambda i: (i, 0, 0)),
            out,
            out,
        ],
        [
            shape_of((2, items, half, local), BF16),
            shape_of((items, heads, frames), F32),
            shape_of((items, half, width), F32),
            shape_of((items, half, width), BF16),
        ],
        (rank, valid, query, key, value, w_out),
    )


def cross_forward(rank, text_len, normed_own, normed_other, c_query, key, value, c_out):
    items, half, width = normed_own.shape
    text_half = key.shape[2]
    local = c_query.shape[1]
    heads = local // HD

    def body(rank_ref, len_ref, own_n, other_n, wq, k, v, w, q, mix, lse, own, send):
        allowed = text_mask(text_half, half, rank_ref[0], len_ref[pl.program_id(0)])
        for part, normed in enumerate((own_n, other_n)):
            q[part, 0] = dot(normed[0], wq[...]).astype(BF16)
            for pair in range(local // PAIR):
                columns = slice(pair * PAIR, (pair + 1) * PAIR)
                mix[part, 0, :, columns] = attend_pair(
                    q[part, 0, :, columns],
                    k[0, :, :, columns].reshape(2 * text_half, PAIR),
                    v[0, :, :, columns].reshape(2 * text_half, PAIR),
                    allowed,
                    lse,
                    lambda head: (2 * pair + head, slice(part * half, (part + 1) * half)),
                )
        send[0] = dot(mix[1, 0], w[...]).astype(BF16)
        own[0] = dot(mix[0, 0], w[...])

    out = pl.BlockSpec((1, half, width), lambda i: (i, 0, 0))
    text = pl.BlockSpec((1, 2, text_half, local), lambda i: (i, 0, 0, 0))
    both = pl.BlockSpec((2, 1, half, local), lambda i: (0, i, 0, 0))
    return call(
        body,
        (items,),
        [SMEM_SPEC, SMEM_SPEC, out, out, whole(c_query.shape), text, text, whole(c_out.shape)],
        [both, both, pl.BlockSpec((1, heads, 2 * half), lambda i: (i, 0, 0)), out, out],
        [
            shape_of((2, items, half, local), BF16),
            shape_of((2, items, half, local), BF16),
            shape_of((items, heads, 2 * half), F32),
            shape_of((items, half, width), F32),
            shape_of((items, half, width), BF16),
        ],
        (rank, text_len, normed_own, normed_other, c_query, key, value, c_out),
    )


def residual_norm(rank, valid, base, own, received, gain, bias):
    items, half, width = own.shape

    def body(rank_ref, valid_ref, x, part, other, g, b, hidden, normed, square):
        item = pl.program_id(0)
        branch = part[0] + other[0].astype(F32)
        total = x[0].astype(F32) + branch
        hidden[0] = total
        normed[0] = layer_norm(total, g, b).astype(BF16)
        mask = row_mask(rank_ref, half, valid_ref[item])
        add_row(square, column_sum(mask * branch * branch))

    steps = half // ROW_BLOCK
    block = pl.BlockSpec((1, ROW_BLOCK, width), lambda i, r, *_: (i, r, 0))
    row = whole((1, width))
    if base.shape[1] == half:
        base_spec = block
    else:
        base_spec = pl.BlockSpec(
            (1, ROW_BLOCK, width), lambda i, r, me, _: (i, me[0] * steps + r, 0)
        )
    return pl.pallas_call(
        body,
        grid_spec=pltpu.PrefetchScalarGridSpec(
            num_scalar_prefetch=2,
            grid=(items, steps),
            in_specs=[base_spec, block, block, row, row],
            out_specs=[block, block, row],
        ),
        out_shape=[
            shape_of(own.shape, F32),
            shape_of(own.shape, BF16),
            shape_of((1, width), F32),
        ],
        compiler_params=pltpu.CompilerParams(vmem_limit_bytes=3 * SLACK_BYTES),
        cost_estimate=pl.CostEstimate(flops=0, bytes_accessed=1024, transcendentals=0),
    )(rank, valid, base, own, received, gain, bias)


def gelu_parts(values):
    normal = 0.5 * (1.0 + lax.erf(values * (0.5**0.5)))
    density = jnp.exp(-0.5 * values * values) * 0.3989422804014327
    return values * normal, normal + values * density


def feed_forward(
    block_index, orders, normed_own, normed_other, grad_own, grad_other, w_up, w_down
):
    rows, width = normed_own.shape
    units = w_up.shape[1]
    steps = units // LANES
    down_each, up_each = units // BLOCKS, width // BLOCKS
    sizes = {DOWN: down_each, UP: up_each * (steps - 1), REST: down_each + up_each}

    def body(me_ref, n_own, n_other, g_own, g_other, up_w, down_w, act, grad, *rest):
        me = me_ref[0]
        packets = {name: rest[2 * k : 2 * k + 2] for k, name in enumerate(sizes)}
        down_part, up_part = rest[2 * len(sizes) :]
        step = pl.program_id(0)
        down_sum, up_sum = 0.0, 0.0
        for half, (n, g) in enumerate(((n_own, g_own), (n_other, g_other))):
            value, slope = gelu_parts(dot(n[...], up_w[...]))
            act[half] = value.astype(BF16)
            grad[half] = (dot_rt(g[...], down_w[...]) * slope).astype(BF16)
            down_sum = down_sum + dot_lt(act[half], g[...])
            up_sum = up_sum + dot_lt(n[...], grad[half])
        down_part[...] = down_sum.astype(BF16)
        up_part[...] = up_sum.astype(BF16)

        def put(name, block, first, values):
            place = place_of(block ^ me, orders[name])
            keep, send = packets[name]
            where = pl.ds(first, values.shape[0])

            @pl.when(place < BLOCKS // 2)
            def _():
                keep[place, where, :] = values

            @pl.when(place >= BLOCKS // 2)
            def _():
                send[place - BLOCKS // 2, where, :] = values

        for sub in range(LANES // down_each):
            part = slice(sub * down_each, (sub + 1) * down_each)
            block = step * (LANES // down_each) + sub
            put(DOWN, block, 0, down_part[part, :LANES])
            put(REST, block, 0, down_part[part, LANES:])

        @pl.when(step < steps - 1)
        def _():
            for block in range(BLOCKS):
                part = slice(block * up_each, (block + 1) * up_each)
                put(UP, block, step * up_each, up_part[part, :])

        @pl.when(step == steps - 1)
        def _():
            for block in range(BLOCKS):
                part = slice(block * up_each, (block + 1) * up_each)
                put(REST, block, down_each, up_part[part, :])

    out = pl.BlockSpec((2, rows, LANES), lambda j: (0, 0, j))
    shapes = [(BLOCKS // 2, sizes[name], LANES) for name in sizes for _ in range(2)]
    results = call(
        body,
        (steps,),
        [SMEM_SPEC]
        + [whole(normed_own.shape)] * 4
        + [
            pl.BlockSpec((width, LANES), lambda j: (0, j)),
            pl.BlockSpec((LANES, width), lambda j: (j, 0)),
        ],
        [out, out] + [whole(shape) for shape in shapes],
        [shape_of((2, rows, units), BF16)] * 2 + [shape_of(shape, BF16) for shape in shapes],
        (block_index, normed_own, normed_other, grad_own, grad_other, w_up, w_down),
        scratch=[pltpu.VMEM((LANES, width), BF16), pltpu.VMEM((width, LANES), BF16)],
    )
    pairs = {name: results[2 + 2 * k : 4 + 2 * k] for k, name in enumerate(sizes)}
    return results[0], results[1], pairs


def project_halves(values, weight, transposed):
    _, rows, depth = values.shape
    width = weight.shape[0] if transposed else weight.shape[1]

    def body(a, w, own, send):
        multiply = dot_rt if transposed else dot
        product = multiply(a[0], w[...])

        @pl.when(pl.program_id(0) == 0)
        def _():
            send[...] = product.astype(BF16)

        @pl.when(pl.program_id(0) == 1)
        def _():
            own[...] = product

    return call(
        body,
        (2,),
        [pl.BlockSpec((1, rows, depth), lambda j: (1 - j, 0, 0)), whole(weight.shape)],
        [whole((rows, width))] * 2,
        [shape_of((rows, width), F32), shape_of((rows, width), BF16)],
        (values, weight),
    )


def finish_output(rank, valid, hidden, own, received):
    items, half, width = hidden.shape

    def body(rank_ref, valid_ref, x, part, other, out, square, branch_square):
        branch = part[0] + other[0].astype(F32)
        total = x[0] + branch
        out[0] = total.astype(BF16)
        mask = row_mask(rank_ref, half, valid_ref[pl.program_id(0)])
        add_row(square, column_sum(mask * total * total))
        add_row(branch_square, column_sum(mask * branch * branch))

    steps = half // ROW_BLOCK
    block = pl.BlockSpec((1, ROW_BLOCK, width), lambda i, r: (i, r, 0))
    return call(
        body,
        (items, steps),
        [SMEM_SPEC, SMEM_SPEC, block, block, block],
        [block, whole((1, width)), whole((1, width))],
        [shape_of(hidden.shape, BF16)] + [shape_of((1, width), F32)] * 2,
        (rank, valid, hidden, own, received),
    )


def norm_backward(rank, values, gain, own, received, grad_base, last):
    items, half, width = own.shape

    def body(rank_ref, x, g, part, other, base, *outs):
        normed, scale = norm_parts(x[0].astype(F32))
        grad = part[0] + other[0].astype(F32)
        add_row(outs[1], column_sum(grad * normed))
        add_row(outs[2], column_sum(grad))
        scaled = grad * g[...].astype(F32)
        first = jnp.mean(scaled, -1, keepdims=True)
        second = jnp.mean(scaled * normed, -1, keepdims=True)
        total = base[0].astype(F32) + scale * (scaled - first - normed * second)
        outs[0][0] = total
        if not last:
            outs[3][0] = total.astype(BF16)

    steps = half // ROW_BLOCK
    block = pl.BlockSpec((1, ROW_BLOCK, width), lambda i, r, *_: (i, r, 0))
    row = whole((1, width))
    if values.shape[1] == half:
        values_spec = block
    else:
        values_spec = pl.BlockSpec(
            (1, ROW_BLOCK, width), lambda i, r, me: (i, me[0] * steps + r, 0)
        )
    out_specs = [block, row, row]
    out_shape = [
        shape_of(own.shape, F32),
        shape_of((1, width), F32),
        shape_of((1, width), F32),
    ]
    if not last:
        out_specs.append(block)
        out_shape.append(shape_of(own.shape, BF16))
    return pl.pallas_call(
        body,
        grid_spec=pltpu.PrefetchScalarGridSpec(
            num_scalar_prefetch=1,
            grid=(items, steps),
            in_specs=[values_spec, row, block, block, block],
            out_specs=out_specs,
        ),
        out_shape=out_shape,
        compiler_params=pltpu.CompilerParams(vmem_limit_bytes=3 * SLACK_BYTES),
        cost_estimate=pl.CostEstimate(flops=0, bytes_accessed=1024, transcendentals=0),
    )(rank, values, gain, own, received, grad_base)


def cross_backward(
    rank, text_len, grad_own, grad_other, c_out, query, key, value, lse, c_query, c_key, c_value
):
    items, half, width = grad_own.shape
    text_half = key.shape[2]
    depth, local = c_key.shape
    heads = local // HD

    def body(
        rank_ref, len_ref, g_own, g_other, w, q, k, v, stats, wq, wk, wv,
        dq, dk, dv, own, send, text_own, text_send, grad_mix,
    ):
        allowed = text_mask(text_half, half, rank_ref[0], len_ref[pl.program_id(0)])
        for part, grad in enumerate((g_own, g_other)):
            grad_mix[part] = dot_rt(grad[0], w[...]).astype(BF16)
        for pair in range(local // PAIR):
            columns = slice(pair * PAIR, (pair + 1) * PAIR)
            key_sum, value_sum = 0.0, 0.0
            for part in range(2):
                rows = slice(part * half, (part + 1) * half)
                one, two, three = attend_pair_back(
                    q[part, 0, :, columns],
                    k[0, :, :, columns].reshape(2 * text_half, PAIR),
                    v[0, :, :, columns].reshape(2 * text_half, PAIR),
                    allowed,
                    [stats[0, 2 * pair + head : 2 * pair + head + 1, rows] for head in range(2)],
                    grad_mix[part, :, columns],
                )
                dq[part, 0, :, columns] = (one * score_scale).astype(BF16)
                key_sum, value_sum = key_sum + two, value_sum + three
            key_sum = (key_sum * score_scale).astype(BF16)
            value_sum = value_sum.astype(BF16)
            for part in range(2):
                rows = slice(part * text_half, (part + 1) * text_half)
                dk[0, part, :, columns] = key_sum[rows]
                dv[0, part, :, columns] = value_sum[rows]
        send[0] = dot_rt(dq[1, 0], wq[...]).astype(BF16)
        own[0] = dot_rt(dq[0, 0], wq[...])
        text_send[0] = (dot_rt(dk[0, 1], wk[...]) + dot_rt(dv[0, 1], wv[...])).astype(BF16)
        text_own[0] = dot_rt(dk[0, 0], wk[...]) + dot_rt(dv[0, 0], wv[...])

    out = pl.BlockSpec((1, half, width), lambda i: (i, 0, 0))
    text = pl.BlockSpec((1, 2, text_half, local), lambda i: (i, 0, 0, 0))
    both = pl.BlockSpec((2, 1, half, local), lambda i: (0, i, 0, 0))
    deep = pl.BlockSpec((1, text_half, depth), lambda i: (i, 0, 0))
    return call(
        body,
        (items,),
        [
            SMEM_SPEC, SMEM_SPEC, out, out, whole(c_out.shape), both, text, text,
            pl.BlockSpec((1, heads, 2 * half), lambda i: (i, 0, 0)),
            whole(c_query.shape), whole(c_key.shape), whole(c_value.shape),
        ],
        [both, text, text, out, out, deep, deep],
        [
            shape_of(query.shape, BF16),
            shape_of(key.shape, BF16),
            shape_of(key.shape, BF16),
            shape_of(grad_own.shape, F32),
            shape_of(grad_own.shape, BF16),
            shape_of((items, text_half, depth), F32),
            shape_of((items, text_half, depth), BF16),
        ],
        (
            rank, text_len, grad_own, grad_other, c_out, query, key, value, lse,
            c_query, c_key, c_value,
        ),
        scratch=[pltpu.VMEM((2, half, local), BF16)],
    )


def self_backward(
    rank, valid, grad_own, grad_other, w_out, query, key, value, lse, w_query, w_key, w_value
):
    items, half, width = grad_own.shape
    frames, local = query.shape[1:]
    heads = local // HD

    def body(
        rank_ref, valid_ref, g_own, g_other, w, q, k, v, stats, wq, wk, wv,
        dq, dk, dv, own, send, grad_mix,
    ):
        me = rank_ref[0]
        count = valid_ref[pl.program_id(0)]
        grad_mix[me] = dot_rt(g_own[0], w[...]).astype(BF16)
        grad_mix[1 - me] = dot_rt(g_other[0], w[...]).astype(BF16)
        masks = [causal_mask((part + 1) * half, half, part * half, count) for part in range(2)]
        for pair in range(local // PAIR):
            columns = slice(pair * PAIR, (pair + 1) * PAIR)
            sums = []
            for part in range(2):
                keys = (part + 1) * half
                rows = slice(part * half, keys)
                one, two, three = attend_pair_back(
                    q[0, rows, columns],
                    k[0, :keys, columns],
                    v[0, :keys, columns],
                    masks[part],
                    [stats[0, 2 * pair + head : 2 * pair + head + 1, rows] for head in range(2)],
                    grad_mix[part, :, columns],
                )
                dq[0, rows, columns] = (one * score_scale).astype(BF16)
                sums.append((two, three))
            (key_a, value_a), (key_b, value_b) = sums
            dk[0, :half, columns] = ((key_a + key_b[:half]) * score_scale).astype(BF16)
            dk[0, half:, columns] = (key_b[half:] * score_scale).astype(BF16)
            dv[0, :half, columns] = (value_a + value_b[:half]).astype(BF16)
            dv[0, half:, columns] = value_b[half:].astype(BF16)

        def back(part):
            rows = pl.ds(pl.multiple_of(part * half, half), half)
            return (
                dot_rt(dq[0, rows, :], wq[...])
                + dot_rt(dk[0, rows, :], wk[...])
                + dot_rt(dv[0, rows, :], wv[...])
            )

        send[0] = back(1 - me).astype(BF16)
        own[0] = back(me)

    out = pl.BlockSpec((1, half, width), lambda i: (i, 0, 0))
    tall = pl.BlockSpec((1, frames, local), lambda i: (i, 0, 0))
    return call(
        body,
        (items,),
        [
            SMEM_SPEC, SMEM_SPEC, out, out, whole(w_out.shape), tall, tall, tall,
            pl.BlockSpec((1, heads, frames), lambda i: (i, 0, 0)),
            whole(w_query.shape), whole(w_key.shape), whole(w_value.shape),
        ],
        [tall, tall, tall, out, out],
        [shape_of(query.shape, BF16)] * 3
        + [shape_of(grad_own.shape, F32), shape_of(grad_own.shape, BF16)],
        (
            rank, valid, grad_own, grad_other, w_out, query, key, value, lse,
            w_query, w_key, w_value,
        ),
        scratch=[pltpu.VMEM((2, half, local), BF16)],
    )


DOWN, UP, REST, CROSS, PROJ, QUERY, KEY, VALUE = range(8)
(
    D_W_QUERY,
    D_W_KEY,
    D_W_VALUE,
    D_W_OUT,
    D_C_QUERY,
    D_C_KEY,
    D_C_VALUE,
    D_C_OUT,
    D_W_UP,
    D_W_DOWN,
) = range(10)
BLOCKS = 16
LEVELS = 4
LANES = 512


class Piece:
    def __init__(self, terms, rows, first, width, tile, full):
        self.terms, self.rows, self.first = terms, rows, first
        self.width, self.tile, self.full = width, tile, full


def place_of(block, order):
    place = 0
    for k, bit in enumerate(order):
        place = place + (((block >> bit) & 1) << (LEVELS - 1 - k))
    return place


def block_at(place, order):
    return sum(((place >> (LEVELS - 1 - k)) & 1) << bit for k, bit in enumerate(order))


def gradient_packet(block_index, pieces, order, operands):
    rows_each = sum(piece.rows // BLOCKS * (piece.width // LANES) for piece in pieces)
    count = len(operands)
    starts = []
    steps = 0
    for piece in pieces:
        starts.append(steps)
        steps += piece.rows // piece.tile if piece.tile < piece.rows else piece.width // LANES

    def body(*refs):
        me = refs[0][0]
        given = refs[1 : 1 + count]
        keep, send, natural = refs[1 + count :]
        step = pl.program_id(0)
        offset = 0
        for start, piece in zip(starts, pieces):
            by_rows = piece.tile < piece.rows
            number = piece.rows // piece.tile if by_rows else piece.width // LANES
            each = piece.rows // BLOCKS

            @pl.when((step >= start) & (step < start + number))
            def _(start=start, piece=piece, by_rows=by_rows, each=each, offset=offset):
                total = None
                for (left, left_at), (right, right_at) in piece.terms:
                    term = dot_lt(given[left][left_at], given[right][right_at])
                    total = term if total is None else total + term
                natural[: piece.tile, :] = total.astype(BF16)
                at = step - start
                for sub in range(piece.tile // each):
                    block = (at * (piece.tile // each) + sub if by_rows else sub) ^ me
                    place = place_of(block, order)
                    base = offset if by_rows else offset + at * each
                    rows = pl.ds(base, each)
                    values = natural[sub * each : (sub + 1) * each, :]

                    @pl.when(place < BLOCKS // 2)
                    def _():
                        keep[place, rows, :] = values

                    @pl.when(place >= BLOCKS // 2)
                    def _():
                        send[place - BLOCKS // 2, rows, :] = values

            offset += each * (piece.width // LANES)

    def spec(array, axis, start, number, block):
        if axis is None:
            return whole(array.shape)
        shape = list(array.shape)
        shape[axis] = block
        first, at = start

        def index(i):
            place = [0] * len(shape)
            place[axis] = first + jnp.clip(i - at, 0, number - 1)
            return tuple(place)

        return pl.BlockSpec(tuple(shape), index)

    half_shape = (BLOCKS // 2, rows_each, LANES)
    return call(
        body,
        (steps,),
        [SMEM_SPEC] + [spec(*operand) for operand in operands],
        [whole(half_shape)] * 2,
        [shape_of(half_shape, BF16)] * 2,
        (block_index, *(operand[0] for operand in operands)),
        scratch=[pltpu.VMEM((max(piece.tile for piece in pieces), LANES), BF16)],
    )


def open_packet(block_index, pieces, order, kept, received, before):
    steps = 4
    group = BLOCKS // steps
    previous = [x for x in before if x is not None]

    def body(*refs):
        me = refs[0][0]
        low, high = refs[1], refs[2]
        outs = refs[3 + len(previous) :]
        for step in range(group):
            place = place_of((pl.program_id(0) * group + step) ^ me, order)
            inner = place & (BLOCKS // 2 - 1)
            upper = place >= BLOCKS // 2
            offset = 0
            for out, piece in zip(outs, pieces):
                each = piece.rows // BLOCKS
                for column in range(piece.width // LANES):
                    part = slice(offset, offset + each)
                    values = jnp.where(upper, high[inner, part, :], low[inner, part, :])
                    lanes = slice(column * LANES, (column + 1) * LANES)
                    out[step * each : (step + 1) * each, lanes] = values.astype(F32)
                    offset += each

    out_specs, out_shape, aliases = [], [], {}
    for number, (piece, old) in enumerate(zip(pieces, before)):
        at = piece.first // piece.width
        out_specs.append(
            pl.BlockSpec((piece.rows // steps, piece.width), lambda i, at=at: (i, at))
        )
        out_shape.append(shape_of((piece.rows, piece.full), F32))
        if old is not None:
            aliases[3 + len(aliases)] = number
    return pl.pallas_call(
        body,
        grid=(steps,),
        in_specs=[SMEM_SPEC, whole(kept.shape), whole(kept.shape)]
        + [pl.BlockSpec(memory_space=pl.ANY)] * len(previous),
        out_specs=out_specs,
        out_shape=out_shape,
        input_output_aliases=aliases,
        compiler_params=pltpu.CompilerParams(vmem_limit_bytes=3 * SLACK_BYTES),
        cost_estimate=pl.CostEstimate(flops=0, bytes_accessed=1024, transcendentals=0),
    )(block_index, kept, received, *previous)


def main_bits():
    bits = lax.axis_size("dp").bit_length() - 1
    along_x = (bits - 2) // 2
    main = [0, along_x, bits - 2, bits - 1]
    return main, [bit for bit in range(bits) if bit not in main]


def exchange(values, bit):
    pairs = [(d, d ^ (1 << bit)) for d in range(lax.axis_size("dp"))]
    return lax.ppermute(values, "dp", pairs)


def add_rounded(one, two):
    return (one.astype(F32) + two.astype(F32)).astype(BF16)


SWAP = [(0, 1), (1, 0)]


def swap_cores(values):
    return lax.ppermute(values, "mp", SWAP)


class Program:
    def __init__(self, given):
        self.v = given
        self.out = {}
        self.token = jnp.zeros((8, 128), F32)
        self.packets = {}

    def tie(self, values):
        values, self.token = lax.optimization_barrier((values, self.token))
        return values

    def start(self, name):
        packet = self.packets[name]
        order, step = packet.order, packet.step
        bit = (order + order[::-1])[step]
        if step < LEVELS:
            values = self.tie(packet.send)
        else:
            values = packet.keep = self.tie(packet.keep)
        packet.arrived = exchange(values, self.main[bit])

    def finish(self, name):
        packet = self.packets[name]
        step, keep = packet.step, packet.keep
        arrived = self.tie(packet.arrived)
        packet.arrived = None
        packet.step = step + 1
        if step < LEVELS - 1:
            half = keep.shape[0] // 2
            packet.send = add_rounded(keep[half:], arrived[half:])
            packet.keep = add_rounded(keep[:half], arrived[:half])
            packet.send = self.tie(packet.send)
        elif step == LEVELS - 1:
            keep = add_rounded(keep, arrived)
            for bit in self.extra:
                keep = add_rounded(keep, exchange(keep, bit))
            packet.keep = self.tie(keep)
        elif step < 2 * LEVELS - 1:
            packet.keep = self.tie(jnp.concatenate([keep, arrived], 0))
        else:
            outs = open_packet(
                self.block,
                packet.pieces,
                packet.order,
                keep,
                arrived,
                [self.out.get(out) for out in packet.outs],
            )
            for out, values in zip(packet.outs, outs):
                self.out[out] = values
            self.out[packet.outs[0]] = self.tie(outs[0])

    def packet(self, name, outs, pieces, operands):
        order = ORDERS[name]
        operands = [
            x if isinstance(x, tuple) else (x, None, None, None, None) for x in operands
        ]
        operands[0] = (self.tie(operands[0][0]), *operands[0][1:])
        self.add(name, gradient_packet(self.block, pieces, order, operands), pieces, outs)

    def add(self, name, halves_of, pieces, outs):
        keep, send = halves_of
        self.packets[name] = SimpleNamespace(
            order=ORDERS[name], step=0, keep=keep, send=self.tie(send), pieces=pieces,
            outs=outs, arrived=None,
        )


def stage_text(p):
    v = p.v
    v.text_own = p.tie(v.text_own)
    v.k_cross, v.v_cross = project_text(
        v.text_own, v.text_other, v.c_key, v.c_value
    )
    v.k_cross = p.tie(v.k_cross)


def stage_tokens(p):
    v = p.v
    v.tokens = p.tie(v.tokens)
    items, frames, width = v.tokens.shape
    normed, *heads = project_tokens(
        v.tokens.reshape(items * frames, width),
        v.gain_one,
        v.bias_one,
        v.w_query,
        v.w_key,
        v.w_value,
    )
    v.normed_one = normed
    v.q_self, v.k_self, v.v_self = [x.reshape(items, frames, -1) for x in heads]
    v.q_self = p.tie(v.q_self)


def stage_self(p):
    v = p.v
    v.q_self = p.tie(v.q_self)
    v.mix_self, v.lse_self, v.attn_own, send = self_forward(
        p.rank, v.frame_valid, v.q_self, v.k_self, v.v_self, v.w_out
    )
    v.attn_other = swap_cores(send)
    v.attn_own = p.tie(v.attn_own)


def stage_norm_two(p):
    v = p.v
    v.attn_own = p.tie(v.attn_own)
    v.hidden_one, v.n2_own, v.square_attn = residual_norm(
        p.rank, v.frame_valid, v.tokens, v.attn_own, v.attn_other,
        v.gain_two, v.bias_two,
    )
    v.n2_other = swap_cores(v.n2_own)
    v.n2_own = p.tie(v.n2_own)


def stage_cross(p):
    v = p.v
    v.n2_own = p.tie(v.n2_own)
    v.q_cross, v.mix_cross, v.lse_cross, v.cross_own, send = cross_forward(
        p.rank, v.text_len, v.n2_own, v.n2_other, v.c_query,
        v.k_cross, v.v_cross, v.c_out,
    )
    v.cross_other = swap_cores(send)
    v.cross_own = p.tie(v.cross_own)


def stage_norm_three(p):
    v = p.v
    v.cross_own = p.tie(v.cross_own)
    v.hidden_two, v.n3_own, v.square_cross = residual_norm(
        p.rank, v.frame_valid, v.hidden_one, v.cross_own, v.cross_other,
        v.gain_three, v.bias_three,
    )
    v.n3_other = swap_cores(v.n3_own)
    v.n3_own = p.tie(v.n3_own)


def flat(values):
    return values.reshape(-1, values.shape[-1])


def stage_units(p):
    v = p.v
    v.n3_own = p.tie(v.n3_own)
    units, width = v.w_down.shape
    v.activated, v.grad_up, pairs = feed_forward(
        p.block, ORDERS, flat(v.n3_own), flat(v.n3_other), flat(v.grad_own),
        flat(v.grad_other), v.w_up, v.w_down,
    )
    down = [Piece(None, units, at, LANES, None, width) for at in (0, LANES)]
    up = [
        Piece(None, width, 0, units - LANES, None, units),
        Piece(None, width, units - LANES, LANES, None, units),
    ]
    p.add(DOWN, pairs[DOWN], down[:1], [D_W_DOWN])
    p.add(UP, pairs[UP], up[:1], [D_W_UP])
    p.add(REST, pairs[REST], [down[1], up[1]], [D_W_DOWN, D_W_UP])
    v.grad_up = p.tie(v.grad_up)


HALF_TERMS = [((0, (0,)), (1, ())), ((0, (1,)), (2, ()))]


def stage_back_units(p):
    v = p.v
    v.grad_up = p.tie(v.grad_up)
    own, send = project_halves(v.grad_up, v.w_up, True)
    shape = v.hidden_two.shape
    v.gn3_own, v.gn3_other = own.reshape(shape), swap_cores(send).reshape(shape)
    v.gn3_own = p.tie(v.gn3_own)


def stage_back_three(p):
    v = p.v
    v.gn3_own = p.tie(v.gn3_own)
    v.g_h2, v.d_gain_three, v.d_bias_three, v.g_cross_own = norm_backward(
        p.rank, v.hidden_two, v.gain_three, v.gn3_own, v.gn3_other,
        v.grad_own, False,
    )
    v.g_cross_other = swap_cores(v.g_cross_own)
    v.g_cross_own = p.tie(v.g_cross_own)


def stage_out(p):
    v = p.v
    v.activated = p.tie(v.activated)
    own, send = project_halves(v.activated, v.w_down, False)
    shape = v.hidden_two.shape
    v.ff_own, v.ff_other = own.reshape(shape), swap_cores(send).reshape(shape)
    v.ff_own = p.tie(v.ff_own)


def stage_result(p):
    v = p.v
    v.ff_own = p.tie(v.ff_own)
    v.out, v.square_out, v.square_ff = finish_output(
        p.rank, v.frame_valid, v.hidden_two, v.ff_own, v.ff_other
    )
    v.out = p.tie(v.out)


def stage_back_cross(p):
    v = p.v
    v.g_cross_own = p.tie(v.g_cross_own)
    (
        v.dq_cross, v.dk_cross, v.dv_cross, v.gn2_own, send,
        v.text_grad_own, text_send,
    ) = cross_backward(
        p.rank, v.text_len, v.g_cross_own, v.g_cross_other, v.c_out,
        v.q_cross, v.k_cross, v.v_cross, v.lse_cross,
        v.c_query, v.c_key, v.c_value,
    )
    v.gn2_other = swap_cores(send)
    v.text_grad_other = swap_cores(text_send)
    v.gn2_own = p.tie(v.gn2_own)


def halves(values):
    return values.reshape(2, -1, values.shape[-1])


def stage_cross_packet(p):
    v = p.v
    items, _, _, local = v.dk_cross.shape
    depth = v.c_key.shape[0]
    width = v.c_query.shape[0]
    query_terms = [((1, ()), (0, (0,))), ((2, ()), (0, (1,)))]

    def text_terms(place):
        return [
            ((3 + half, (item,)), (place, (item, half))) for item in range(items) for half in (0, 1)
        ]

    p.packet(
        CROSS, [D_C_QUERY, D_C_KEY, D_C_VALUE],
        [
            Piece(query_terms, width, 0, local, width, local),
            Piece(text_terms(5), depth, 0, local, depth, local),
            Piece(text_terms(6), depth, 0, local, depth, local),
        ],
        [
            halves(v.dq_cross), flat(v.n2_own), flat(v.n2_other),
            v.text_own, v.text_other, v.dk_cross, v.dv_cross,
        ],
    )


def stage_back_two(p):
    v = p.v
    v.gn2_own = p.tie(v.gn2_own)
    v.g_h1, v.d_gain_two, v.d_bias_two, v.g_attn_own = norm_backward(
        p.rank, v.hidden_one, v.gain_two, v.gn2_own, v.gn2_other, v.g_h2, False
    )
    v.g_attn_other = swap_cores(v.g_attn_own)
    v.g_attn_own = p.tie(v.g_attn_own)


def stage_back_self(p):
    v = p.v
    v.g_attn_own = p.tie(v.g_attn_own)
    v.dq_self, v.dk_self, v.dv_self, v.gn1_own, send = self_backward(
        p.rank, v.frame_valid, v.g_attn_own, v.g_attn_other, v.w_out,
        v.q_self, v.k_self, v.v_self, v.lse_self,
        v.w_query, v.w_key, v.w_value,
    )
    v.gn1_other = swap_cores(send)
    v.gn1_own = p.tie(v.gn1_own)


def stage_proj_packet(p):
    v = p.v
    local, width = v.w_out.shape
    terms = [((3, (0,)), (4, ())), ((3, (1,)), (5, ()))]
    steps = width // LANES

    def streamed(name, first):
        return (flat(name), 1, (0, first), steps, LANES)

    p.packet(
        PROJ, [D_C_OUT, D_W_OUT],
        [
            Piece(HALF_TERMS, local, 0, width, local, width),
            Piece(terms, local, 0, width, local, width),
        ],
        [
            halves(v.mix_cross), streamed(v.g_cross_own, 0), streamed(v.g_cross_other, 0),
            halves(v.mix_self), streamed(v.g_attn_own, steps),
            streamed(v.g_attn_other, steps),
        ],
    )


def self_packet(p, name, grad, out):
    v = p.v
    width, local = v.w_query.shape
    piece = Piece([((0, ()), (1, ()))], width, 0, local, width, local)
    p.packet(name, [out], [piece], [v.normed_one, flat(grad)])


def stage_query_packet(p):
    self_packet(p, QUERY, p.v.dq_self, D_W_QUERY)


def stage_key_packet(p):
    self_packet(p, KEY, p.v.dk_self, D_W_KEY)


def stage_value_packet(p):
    self_packet(p, VALUE, p.v.dv_self, D_W_VALUE)


def stage_back_one(p):
    v = p.v
    v.gn1_own = p.tie(v.gn1_own)
    v.d_tokens, v.d_gain_one, v.d_bias_one = norm_backward(
        p.rank, v.tokens, v.gain_one, v.gn1_own, v.gn1_other, v.g_h1, True
    )
    v.d_tokens = p.tie(v.d_tokens)


def stage_text_grad(p):
    v = p.v
    v.text_grad_own = p.tie(v.text_grad_own)
    v.d_text = v.text_grad_own + v.text_grad_other.astype(F32)
    v.d_text = p.tie(v.d_text)


def stage_small(p):
    v = p.v
    half = v.hidden_one.shape[1]
    width = v.hidden_one.shape[2]
    own = jnp.clip(v.frame_valid - p.rank * half, 0, half).sum().astype(F32)
    rows = [
        v.d_gain_one, v.d_bias_one, v.d_gain_two, v.d_bias_two,
        v.d_gain_three, v.d_bias_three, v.square_out, v.square_attn,
        v.square_cross, v.square_ff, jnp.full((1, width), own / width, F32),
    ]
    rows.append(jnp.zeros((16 - len(rows), width), F32))
    total = p.tie(jnp.concatenate(rows, 0))
    v.small = total
    v.small_other = swap_cores(total)
    p.hops = list(range(lax.axis_size("dp").bit_length() - 1))


def stage_hop(p):
    v = p.v
    total = v.small = p.tie(v.small + v.small_other)
    if p.hops:
        v.small_other = exchange(total, p.hops.pop(0))


def stage_rms(p):
    v = p.v
    while p.hops:
        stage_hop(p)
    total = v.small + v.small_other
    width = total.shape[1]
    v.small = total[:6]
    sums = jnp.sum(total[6:11], -1)
    v.rms = jnp.sqrt(sums[:4] / (sums[4] * width))


def stage_end(p):
    p.v.rms = p.v.rms + p.token[0, :4] * 0.0


ORDERS = {
    DOWN: [2, 0, 1, 3],
    UP: [0, 1, 2, 3],
    REST: [1, 0, 2, 3],
    CROSS: [2, 1, 0, 3],
    PROJ: [1, 0, 3, 2],
    QUERY: [0, 1, 2, 3],
    KEY: [1, 0, 3, 2],
    VALUE: [0, 1, 2, 3],
}


PLAN = [
    stage_tokens, stage_self, stage_text, stage_norm_two, stage_cross, stage_norm_three,
    stage_units, REST, UP, DOWN, stage_back_units, stage_back_three, stage_back_cross, REST, UP,
    stage_cross_packet, DOWN, stage_back_two, REST, UP, CROSS, DOWN, stage_back_self, REST, UP,
    DOWN, stage_proj_packet, stage_key_packet, stage_value_packet, REST, CROSS, UP, PROJ,
    stage_query_packet, CROSS, KEY, QUERY, VALUE, DOWN, REST, REST, stage_back_one, UP,
    stage_out, UP, QUERY, REST, REST, PROJ, PROJ, QUERY, VALUE, UP, UP, stage_result, CROSS,
    CROSS, REST, VALUE, REST, PROJ, PROJ, UP, KEY, KEY, UP, CROSS, CROSS, DOWN, REST, REST,
    QUERY, DOWN, PROJ, PROJ, KEY, UP, UP, KEY, VALUE, CROSS, REST, CROSS, DOWN, QUERY, PROJ,
    PROJ, REST, KEY, KEY, QUERY, VALUE, CROSS, CROSS, QUERY, PROJ, PROJ, UP, UP, KEY, KEY, VALUE,
    VALUE, QUERY, QUERY, CROSS, CROSS, KEY, KEY, QUERY, PROJ, PROJ, DOWN, VALUE, VALUE, QUERY,
    KEY, KEY, REST, DOWN, DOWN, VALUE, VALUE, QUERY, QUERY, CROSS, CROSS, UP, VALUE, VALUE, DOWN,
    DOWN, PROJ, PROJ, QUERY, QUERY, KEY, KEY, VALUE, stage_text_grad, DOWN, DOWN, stage_small,
    VALUE, stage_hop, CROSS, stage_hop, QUERY, stage_hop, stage_hop, VALUE, DOWN, PROJ, KEY,
    stage_rms, stage_end,
]

def per_device(
    tokens,
    text_own,
    text_len,
    frame_valid,
    gain_one,
    bias_one,
    gain_two,
    bias_two,
    gain_three,
    bias_three,
    w_query,
    w_key,
    w_value,
    w_out,
    c_query,
    c_key,
    c_value,
    c_out,
    w_up,
    w_down,
    grad_own,
):
    v = SimpleNamespace()
    v.tokens = tokens
    v.text_own = text_own
    v.text_len = text_len
    v.frame_valid = frame_valid
    v.gain_one = gain_one.reshape(1, -1)
    v.bias_one = bias_one.reshape(1, -1)
    v.gain_two = gain_two.reshape(1, -1)
    v.bias_two = bias_two.reshape(1, -1)
    v.gain_three = gain_three.reshape(1, -1)
    v.bias_three = bias_three.reshape(1, -1)
    v.w_query = w_query
    v.w_key = w_key
    v.w_value = w_value
    v.w_out = w_out
    v.c_query = c_query
    v.c_key = c_key
    v.c_value = c_value
    v.c_out = c_out
    v.w_up = w_up
    v.w_down = w_down
    v.grad_own = grad_own
    p = Program(v)
    p.rank = lax.axis_index("mp").astype(jnp.int32).reshape(1)
    p.main, p.extra = main_bits()
    place = lax.axis_index("dp")
    p.block = sum(((place >> bit) & 1) << k for k, bit in enumerate(p.main))
    p.block = p.block.astype(jnp.int32).reshape(1)
    v.text_other = swap_cores(v.text_own)
    v.grad_other = swap_cores(v.grad_own)
    for action in PLAN:
        if callable(action):
            action(p)
        elif p.packets[action].arrived is None:
            p.start(action)
        else:
            p.finish(action)
    return (
        v.out,
        v.d_tokens,
        v.d_text,
        *(v.small[n] for n in range(6)),
        *(p.out[name] for name in range(10)),
        v.rms,
    )


def solution(mesh):
    split = P("dp", "mp", None)
    columns, rows = P(None, "mp"), P("mp", None)
    weights = (columns,) * 3 + (rows,) + (columns,) * 3 + (rows, columns, rows)
    return jax.shard_map(
        per_device,
        mesh=mesh,
        in_specs=(P("dp", None, None), split, P("dp"), P("dp"))
        + (P(),) * 6
        + weights
        + (split,),
        out_specs=(split,) * 3 + (P(),) * 6 + weights + (P(),),
        check_vma=False,
    )
```

```python
import math
from types import SimpleNamespace

import jax
import jax.numpy as jnp
from jax import lax
from jax.experimental import pallas as pl
from jax.experimental.pallas import tpu as pltpu
from jax.sharding import PartitionSpec as P

HD = 64
PAIR = 2 * HD
norm_eps = 1e-05
score_scale = 0.125
masked_fill = -1e30
F32 = jnp.float32
BF16 = jnp.bfloat16
SLACK_BYTES = 6 * 1024 * 1024
SMEM_SPEC = pl.BlockSpec(memory_space=pltpu.SMEM)


def dot(a, b):
    return lax.dot_general(a, b, (((1,), (0,)), ((), ())), preferred_element_type=F32)


def dot_rt(a, b):
    return lax.dot_general(a, b, (((1,), (1,)), ((), ())), preferred_element_type=F32)


def dot_lt(a, b):
    return lax.dot_general(a, b, (((0,), (0,)), ((), ())), preferred_element_type=F32)


def whole(shape):
    zeros = (0,) * len(shape)
    return pl.BlockSpec(tuple(shape), lambda *_: zeros)


def shape_of(shape, kind):
    return jax.ShapeDtypeStruct(tuple(shape), kind)


def vmem_bytes(specs, arrays, scratch=()):
    total = SLACK_BYTES
    for spec, array in zip(specs, arrays):
        if spec.block_shape is not None:
            total += 2 * math.prod(spec.block_shape) * jnp.dtype(array.dtype).itemsize
    for buffer in scratch:
        total += math.prod(buffer.shape) * jnp.dtype(buffer.dtype).itemsize
    return min(total, 60 * 1024 * 1024)


def call(body, grid, in_specs, out_specs, out_shape, args, scratch=(), flops=0):
    return pl.pallas_call(
        body,
        grid=grid,
        in_specs=in_specs,
        out_specs=out_specs,
        out_shape=out_shape,
        scratch_shapes=list(scratch),
        compiler_params=pltpu.CompilerParams(
            vmem_limit_bytes=vmem_bytes(
                [*in_specs, *out_specs], [*args, *out_shape], scratch
            )
        ),
        cost_estimate=pl.CostEstimate(flops=flops, bytes_accessed=1024, transcendentals=0),
    )(*args)


def norm_parts(values):
    average = jnp.mean(values, -1, keepdims=True)
    centered = values - average
    variance = jnp.mean(centered * centered, -1, keepdims=True)
    scale = lax.rsqrt(variance + norm_eps)
    return centered * scale, scale


def layer_norm(values, gain_ref, bias_ref):
    normed, _ = norm_parts(values)
    return normed * gain_ref[...].astype(F32) + bias_ref[...].astype(F32)


ROW_BLOCK = 256


def add_row(ref, row):
    first = (pl.program_id(0) == 0) & (pl.program_id(1) == 0)

    @pl.when(first)
    def _():
        ref[...] = row

    @pl.when(jnp.logical_not(first))
    def _():
        ref[...] += row


def column_sum(values):
    return jnp.sum(values, 0, keepdims=True)


def row_mask(rank_ref, half, count):
    first_row = rank_ref[0] * half + pl.program_id(1) * ROW_BLOCK
    place = first_row + lax.broadcasted_iota(jnp.int32, (ROW_BLOCK, 1), 0)
    return (place < count).astype(F32)


def project_tokens(tokens, gain, bias, w_query, w_key, w_value):
    rows, width = tokens.shape
    local = w_query.shape[1]
    block = 256

    def body(x, g, b, wq, wk, wv, n, q, k, v):
        normed = layer_norm(x[...].astype(F32), g, b).astype(BF16)
        n[...] = normed
        q[...] = dot(normed, wq[...]).astype(BF16)
        k[...] = dot(normed, wk[...]).astype(BF16)
        v[...] = dot(normed, wv[...]).astype(BF16)

    wide = pl.BlockSpec((block, width), lambda i: (i, 0))
    slim = pl.BlockSpec((block, local), lambda i: (i, 0))
    return call(
        body,
        (rows // block,),
        [wide, whole((1, width)), whole((1, width))] + [whole(w_query.shape)] * 3,
        [wide, slim, slim, slim],
        [shape_of((rows, width), BF16)] + [shape_of((rows, local), BF16)] * 3,
        (tokens, gain, bias, w_query, w_key, w_value),
    )


def project_text(text_own, text_other, c_key, c_value):
    items, text_half, depth = text_own.shape
    local = c_key.shape[1]

    def body(own, other, wk, wv, k, v):
        for half, rows in enumerate((own, other)):
            for item in range(items):
                k[item, half] = dot(rows[item], wk[...]).astype(BF16)
                v[item, half] = dot(rows[item], wv[...]).astype(BF16)

    shape = (items, 2, text_half, local)
    return call(
        body,
        (1,),
        [whole(text_own.shape)] * 2 + [whole(c_key.shape)] * 2,
        [whole(shape)] * 2,
        [shape_of(shape, BF16)] * 2,
        (text_own, text_other, c_key, c_value),
    )


def head_mask(rows, head):
    lane = lax.broadcasted_iota(jnp.int32, (rows, PAIR), 1)
    return lane < HD if head == 0 else lane >= HD


def pick(first, second):
    return jnp.where(head_mask(first.shape[0], 0), first, second)


def only(values, head):
    return jnp.where(head_mask(values.shape[0], head), values, jnp.zeros_like(values))


def scores_t(query_pair, key_pair, head, allowed):
    scores = dot_rt(key_pair, only(query_pair, head)) * score_scale
    return jnp.where(allowed, scores, masked_fill)


def attend_pair(query_pair, key_pair, value_pair, allowed, lse_ref, lse_at):
    mixed = []
    for head in range(2):
        scores = scores_t(query_pair, key_pair, head, allowed)
        highest = jnp.max(scores, 0, keepdims=True)
        powers = jnp.exp(scores - highest)
        total = jnp.sum(powers, 0, keepdims=True)
        probs = (powers / total).astype(BF16)
        mixed.append(dot_lt(probs, value_pair))
        row, columns = lse_at(head)
        lse_ref[0, row : row + 1, columns] = highest + jnp.log(total)
    return pick(mixed[0], mixed[1]).astype(BF16)


def attend_pair_back(query_pair, key_pair, value_pair, allowed, lse_rows, grad_pair):
    grads = []
    for head in range(2):
        probs = jnp.exp(scores_t(query_pair, key_pair, head, allowed) - lse_rows[head])
        grad_probs = dot_rt(value_pair, only(grad_pair, head))
        inner = jnp.sum(grad_probs * probs, 0, keepdims=True)
        grad_scores = (probs * (grad_probs - inner)).astype(BF16)
        grads.append(
            (
                dot_lt(grad_scores, key_pair),
                dot(grad_scores, query_pair),
                dot(probs.astype(BF16), grad_pair),
            )
        )
    return [pick(one, two) for one, two in zip(grads[0], grads[1])]


def causal_mask(keys, queries, first_query, count):
    key_at = lax.broadcasted_iota(jnp.int32, (keys, queries), 0)
    query_at = first_query + lax.broadcasted_iota(jnp.int32, (keys, queries), 1)
    return (key_at <= query_at) & (key_at < count)


def text_mask(text_half, queries, rank, count):
    key_at = lax.broadcasted_iota(jnp.int32, (2 * text_half, queries), 0)
    swapped = jnp.where(key_at < text_half, key_at + text_half, key_at - text_half)
    return jnp.where(rank == 0, key_at, swapped) < count


def self_forward(rank, valid, query, key, value, w_out):
    items, frames, local = query.shape
    width = w_out.shape[1]
    half = frames // 2
    heads = local // HD

    def body(rank_ref, valid_ref, q, k, v, w, mix, lse, own, send):
        me = rank_ref[0]
        count = valid_ref[pl.program_id(0)]
        for part in range(2):
            keys = (part + 1) * half
            allowed = causal_mask(keys, half, part * half, count)
            rows = slice(part * half, (part + 1) * half)
            for pair in range(local // PAIR):
                columns = slice(pair * PAIR, (pair + 1) * PAIR)
                mix[part ^ me, 0, :, columns] = attend_pair(
                    q[0, rows, columns],
                    k[0, :keys, columns],
                    v[0, :keys, columns],
                    allowed,
                    lse,
                    lambda head: (2 * pair + head, rows),
                )
        send[0] = dot(mix[1, 0], w[...]).astype(BF16)
        own[0] = dot(mix[0, 0], w[...])

    tall = pl.BlockSpec((1, frames, local), lambda i: (i, 0, 0))
    out = pl.BlockSpec((1, half, width), lambda i: (i, 0, 0))
    return call(
        body,
        (items,),
        [SMEM_SPEC, SMEM_SPEC, tall, tall, tall, whole(w_out.shape)],
        [
            pl.BlockSpec((2, 1, half, local), lambda i: (0, i, 0, 0)),
            pl.BlockSpec((1, heads, frames), lambda i: (i, 0, 0)),
            out,
            out,
        ],
        [
            shape_of((2, items, half, local), BF16),
            shape_of((items, heads, frames), F32),
            shape_of((items, half, width), F32),
            shape_of((items, half, width), BF16),
        ],
        (rank, valid, query, key, value, w_out),
    )


def cross_forward(rank, text_len, normed_own, normed_other, c_query, key, value, c_out):
    items, half, width = normed_own.shape
    text_half = key.shape[2]
    local = c_query.shape[1]
    heads = local // HD

    def body(rank_ref, len_ref, own_n, other_n, wq, k, v, w, q, mix, lse, own, send):
        allowed = text_mask(text_half, half, rank_ref[0], len_ref[pl.program_id(0)])
        for part, normed in enumerate((own_n, other_n)):
            q[part, 0] = dot(normed[0], wq[...]).astype(BF16)
            for pair in range(local // PAIR):
                columns = slice(pair * PAIR, (pair + 1) * PAIR)
                mix[part, 0, :, columns] = attend_pair(
                    q[part, 0, :, columns],
                    k[0, :, :, columns].reshape(2 * text_half, PAIR),
                    v[0, :, :, columns].reshape(2 * text_half, PAIR),
                    allowed,
                    lse,
                    lambda head: (2 * pair + head, slice(part * half, (part + 1) * half)),
                )
        send[0] = dot(mix[1, 0], w[...]).astype(BF16)
        own[0] = dot(mix[0, 0], w[...])

    out = pl.BlockSpec((1, half, width), lambda i: (i, 0, 0))
    text = pl.BlockSpec((1, 2, text_half, local), lambda i: (i, 0, 0, 0))
    both = pl.BlockSpec((2, 1, half, local), lambda i: (0, i, 0, 0))
    return call(
        body,
        (items,),
        [SMEM_SPEC, SMEM_SPEC, out, out, whole(c_query.shape), text, text, whole(c_out.shape)],
        [both, both, pl.BlockSpec((1, heads, 2 * half), lambda i: (i, 0, 0)), out, out],
        [
            shape_of((2, items, half, local), BF16),
            shape_of((2, items, half, local), BF16),
            shape_of((items, heads, 2 * half), F32),
            shape_of((items, half, width), F32),
            shape_of((items, half, width), BF16),
        ],
        (rank, text_len, normed_own, normed_other, c_query, key, value, c_out),
    )


def residual_norm(rank, valid, base, own, received, gain, bias):
    items, half, width = own.shape

    def body(rank_ref, valid_ref, x, part, other, g, b, hidden, normed, square):
        item = pl.program_id(0)
        branch = part[0] + other[0].astype(F32)
        total = x[0].astype(F32) + branch
        hidden[0] = total
        normed[0] = layer_norm(total, g, b).astype(BF16)
        mask = row_mask(rank_ref, half, valid_ref[item])
        add_row(square, column_sum(mask * branch * branch))

    steps = half // ROW_BLOCK
    block = pl.BlockSpec((1, ROW_BLOCK, width), lambda i, r, *_: (i, r, 0))
    row = whole((1, width))
    if base.shape[1] == half:
        base_spec = block
    else:
        base_spec = pl.BlockSpec(
            (1, ROW_BLOCK, width), lambda i, r, me, _: (i, me[0] * steps + r, 0)
        )
    return pl.pallas_call(
        body,
        grid_spec=pltpu.PrefetchScalarGridSpec(
            num_scalar_prefetch=2,
            grid=(items, steps),
            in_specs=[base_spec, block, block, row, row],
            out_specs=[block, block, row],
        ),
        out_shape=[
            shape_of(own.shape, F32),
            shape_of(own.shape, BF16),
            shape_of((1, width), F32),
        ],
        compiler_params=pltpu.CompilerParams(vmem_limit_bytes=3 * SLACK_BYTES),
        cost_estimate=pl.CostEstimate(flops=0, bytes_accessed=1024, transcendentals=0),
    )(rank, valid, base, own, received, gain, bias)


def gelu_parts(values):
    normal = 0.5 * (1.0 + lax.erf(values * (0.5**0.5)))
    density = jnp.exp(-0.5 * values * values) * 0.3989422804014327
    return values * normal, normal + values * density


def feed_forward(
    block_index, orders, normed_own, normed_other, grad_own, grad_other, w_up, w_down
):
    rows, width = normed_own.shape
    units = w_up.shape[1]
    steps = units // LANES
    down_each, up_each = units // BLOCKS, width // BLOCKS
    sizes = {DOWN: down_each, UP: up_each * (steps - 1), REST: down_each + up_each}

    def body(me_ref, n_own, n_other, g_own, g_other, up_w, down_w, act, grad, *rest):
        me = me_ref[0]
        packets = {name: rest[2 * k : 2 * k + 2] for k, name in enumerate(sizes)}
        down_part, up_part = rest[2 * len(sizes) :]
        step = pl.program_id(0)
        down_sum, up_sum = 0.0, 0.0
        for half, (n, g) in enumerate(((n_own, g_own), (n_other, g_other))):
            value, slope = gelu_parts(dot(n[...], up_w[...]))
            act[half] = value.astype(BF16)
            grad[half] = (dot_rt(g[...], down_w[...]) * slope).astype(BF16)
            down_sum = down_sum + dot_lt(act[half], g[...])
            up_sum = up_sum + dot_lt(n[...], grad[half])
        down_part[...] = down_sum.astype(BF16)
        up_part[...] = up_sum.astype(BF16)

        def put(name, block, first, values):
            place = place_of(block ^ me, orders[name])
            keep, send = packets[name]
            where = pl.ds(first, values.shape[0])

            @pl.when(place < BLOCKS // 2)
            def _():
                keep[place, where, :] = values

            @pl.when(place >= BLOCKS // 2)
            def _():
                send[place - BLOCKS // 2, where, :] = values

        for sub in range(LANES // down_each):
            part = slice(sub * down_each, (sub + 1) * down_each)
            block = step * (LANES // down_each) + sub
            put(DOWN, block, 0, down_part[part, :LANES])
            put(REST, block, 0, down_part[part, LANES:])

        @pl.when(step < steps - 1)
        def _():
            for block in range(BLOCKS):
                part = slice(block * up_each, (block + 1) * up_each)
                put(UP, block, step * up_each, up_part[part, :])

        @pl.when(step == steps - 1)
        def _():
            for block in range(BLOCKS):
                part = slice(block * up_each, (block + 1) * up_each)
                put(REST, block, down_each, up_part[part, :])

    out = pl.BlockSpec((2, rows, LANES), lambda j: (0, 0, j))
    shapes = [(BLOCKS // 2, sizes[name], LANES) for name in sizes for _ in range(2)]
    results = call(
        body,
        (steps,),
        [SMEM_SPEC]
        + [whole(normed_own.shape)] * 4
        + [
            pl.BlockSpec((width, LANES), lambda j: (0, j)),
            pl.BlockSpec((LANES, width), lambda j: (j, 0)),
        ],
        [out, out] + [whole(shape) for shape in shapes],
        [shape_of((2, rows, units), BF16)] * 2 + [shape_of(shape, BF16) for shape in shapes],
        (block_index, normed_own, normed_other, grad_own, grad_other, w_up, w_down),
        scratch=[pltpu.VMEM((LANES, width), BF16), pltpu.VMEM((width, LANES), BF16)],
    )
    pairs = {name: results[2 + 2 * k : 4 + 2 * k] for k, name in enumerate(sizes)}
    return results[0], results[1], pairs


def project_halves(values, weight, transposed):
    _, rows, depth = values.shape
    width = weight.shape[0] if transposed else weight.shape[1]

    def body(a, w, own, send):
        multiply = dot_rt if transposed else dot
        product = multiply(a[0], w[...])

        @pl.when(pl.program_id(0) == 0)
        def _():
            send[...] = product.astype(BF16)

        @pl.when(pl.program_id(0) == 1)
        def _():
            own[...] = product

    return call(
        body,
        (2,),
        [pl.BlockSpec((1, rows, depth), lambda j: (1 - j, 0, 0)), whole(weight.shape)],
        [whole((rows, width))] * 2,
        [shape_of((rows, width), F32), shape_of((rows, width), BF16)],
        (values, weight),
    )


def finish_output(rank, valid, hidden, own, received):
    items, half, width = hidden.shape

    def body(rank_ref, valid_ref, x, part, other, out, square, branch_square):
        branch = part[0] + other[0].astype(F32)
        total = x[0] + branch
        out[0] = total.astype(BF16)
        mask = row_mask(rank_ref, half, valid_ref[pl.program_id(0)])
        add_row(square, column_sum(mask * total * total))
        add_row(branch_square, column_sum(mask * branch * branch))

    steps = half // ROW_BLOCK
    block = pl.BlockSpec((1, ROW_BLOCK, width), lambda i, r: (i, r, 0))
    return call(
        body,
        (items, steps),
        [SMEM_SPEC, SMEM_SPEC, block, block, block],
        [block, whole((1, width)), whole((1, width))],
        [shape_of(hidden.shape, BF16)] + [shape_of((1, width), F32)] * 2,
        (rank, valid, hidden, own, received),
    )


def norm_backward(rank, values, gain, own, received, grad_base, last):
    items, half, width = own.shape

    def body(rank_ref, x, g, part, other, base, *outs):
        normed, scale = norm_parts(x[0].astype(F32))
        grad = part[0] + other[0].astype(F32)
        add_row(outs[1], column_sum(grad * normed))
        add_row(outs[2], column_sum(grad))
        scaled = grad * g[...].astype(F32)
        first = jnp.mean(scaled, -1, keepdims=True)
        second = jnp.mean(scaled * normed, -1, keepdims=True)
        total = base[0].astype(F32) + scale * (scaled - first - normed * second)
        outs[0][0] = total
        if not last:
            outs[3][0] = total.astype(BF16)

    steps = half // ROW_BLOCK
    block = pl.BlockSpec((1, ROW_BLOCK, width), lambda i, r, *_: (i, r, 0))
    row = whole((1, width))
    if values.shape[1] == half:
        values_spec = block
    else:
        values_spec = pl.BlockSpec(
            (1, ROW_BLOCK, width), lambda i, r, me: (i, me[0] * steps + r, 0)
        )
    out_specs = [block, row, row]
    out_shape = [
        shape_of(own.shape, F32),
        shape_of((1, width), F32),
        shape_of((1, width), F32),
    ]
    if not last:
        out_specs.append(block)
        out_shape.append(shape_of(own.shape, BF16))
    return pl.pallas_call(
        body,
        grid_spec=pltpu.PrefetchScalarGridSpec(
            num_scalar_prefetch=1,
            grid=(items, steps),
            in_specs=[values_spec, row, block, block, block],
            out_specs=out_specs,
        ),
        out_shape=out_shape,
        compiler_params=pltpu.CompilerParams(vmem_limit_bytes=3 * SLACK_BYTES),
        cost_estimate=pl.CostEstimate(flops=0, bytes_accessed=1024, transcendentals=0),
    )(rank, values, gain, own, received, grad_base)


def cross_backward(
    rank, text_len, grad_own, grad_other, c_out, query, key, value, lse, c_query, c_key, c_value
):
    items, half, width = grad_own.shape
    text_half = key.shape[2]
    depth, local = c_key.shape
    heads = local // HD

    def body(
        rank_ref, len_ref, g_own, g_other, w, q, k, v, stats, wq, wk, wv,
        dq, dk, dv, own, send, text_own, text_send, grad_mix,
    ):
        allowed = text_mask(text_half, half, rank_ref[0], len_ref[pl.program_id(0)])
        for part, grad in enumerate((g_own, g_other)):
            grad_mix[part] = dot_rt(grad[0], w[...]).astype(BF16)
        for pair in range(local // PAIR):
            columns = slice(pair * PAIR, (pair + 1) * PAIR)
            key_sum, value_sum = 0.0, 0.0
            for part in range(2):
                rows = slice(part * half, (part + 1) * half)
                one, two, three = attend_pair_back(
                    q[part, 0, :, columns],
                    k[0, :, :, columns].reshape(2 * text_half, PAIR),
                    v[0, :, :, columns].reshape(2 * text_half, PAIR),
                    allowed,
                    [stats[0, 2 * pair + head : 2 * pair + head + 1, rows] for head in range(2)],
                    grad_mix[part, :, columns],
                )
                dq[part, 0, :, columns] = (one * score_scale).astype(BF16)
                key_sum, value_sum = key_sum + two, value_sum + three
            key_sum = (key_sum * score_scale).astype(BF16)
            value_sum = value_sum.astype(BF16)
            for part in range(2):
                rows = slice(part * text_half, (part + 1) * text_half)
                dk[0, part, :, columns] = key_sum[rows]
                dv[0, part, :, columns] = value_sum[rows]
        send[0] = dot_rt(dq[1, 0], wq[...]).astype(BF16)
        own[0] = dot_rt(dq[0, 0], wq[...])
        text_send[0] = (dot_rt(dk[0, 1], wk[...]) + dot_rt(dv[0, 1], wv[...])).astype(BF16)
        text_own[0] = dot_rt(dk[0, 0], wk[...]) + dot_rt(dv[0, 0], wv[...])

    out = pl.BlockSpec((1, half, width), lambda i: (i, 0, 0))
    text = pl.BlockSpec((1, 2, text_half, local), lambda i: (i, 0, 0, 0))
    both = pl.BlockSpec((2, 1, half, local), lambda i: (0, i, 0, 0))
    deep = pl.BlockSpec((1, text_half, depth), lambda i: (i, 0, 0))
    return call(
        body,
        (items,),
        [
            SMEM_SPEC, SMEM_SPEC, out, out, whole(c_out.shape), both, text, text,
            pl.BlockSpec((1, heads, 2 * half), lambda i: (i, 0, 0)),
            whole(c_query.shape), whole(c_key.shape), whole(c_value.shape),
        ],
        [both, text, text, out, out, deep, deep],
        [
            shape_of(query.shape, BF16),
            shape_of(key.shape, BF16),
            shape_of(key.shape, BF16),
            shape_of(grad_own.shape, F32),
            shape_of(grad_own.shape, BF16),
            shape_of((items, text_half, depth), F32),
            shape_of((items, text_half, depth), BF16),
        ],
        (
            rank, text_len, grad_own, grad_other, c_out, query, key, value, lse,
            c_query, c_key, c_value,
        ),
        scratch=[pltpu.VMEM((2, half, local), BF16)],
    )


def self_backward(
    rank, valid, grad_own, grad_other, w_out, query, key, value, lse, w_query, w_key, w_value
):
    items, half, width = grad_own.shape
    frames, local = query.shape[1:]
    heads = local // HD

    def body(
        rank_ref, valid_ref, g_own, g_other, w, q, k, v, stats, wq, wk, wv,
        dq, dk, dv, own, send, grad_mix,
    ):
        me = rank_ref[0]
        count = valid_ref[pl.program_id(0)]
        grad_mix[me] = dot_rt(g_own[0], w[...]).astype(BF16)
        grad_mix[1 - me] = dot_rt(g_other[0], w[...]).astype(BF16)
        masks = [causal_mask((part + 1) * half, half, part * half, count) for part in range(2)]
        for pair in range(local // PAIR):
            columns = slice(pair * PAIR, (pair + 1) * PAIR)
            sums = []
            for part in range(2):
                keys = (part + 1) * half
                rows = slice(part * half, keys)
                one, two, three = attend_pair_back(
                    q[0, rows, columns],
                    k[0, :keys, columns],
                    v[0, :keys, columns],
                    masks[part],
                    [stats[0, 2 * pair + head : 2 * pair + head + 1, rows] for head in range(2)],
                    grad_mix[part, :, columns],
                )
                dq[0, rows, columns] = (one * score_scale).astype(BF16)
                sums.append((two, three))
            (key_a, value_a), (key_b, value_b) = sums
            dk[0, :half, columns] = ((key_a + key_b[:half]) * score_scale).astype(BF16)
            dk[0, half:, columns] = (key_b[half:] * score_scale).astype(BF16)
            dv[0, :half, columns] = (value_a + value_b[:half]).astype(BF16)
            dv[0, half:, columns] = value_b[half:].astype(BF16)

        def back(part):
            rows = pl.ds(pl.multiple_of(part * half, half), half)
            return (
                dot_rt(dq[0, rows, :], wq[...])
                + dot_rt(dk[0, rows, :], wk[...])
                + dot_rt(dv[0, rows, :], wv[...])
            )

        send[0] = back(1 - me).astype(BF16)
        own[0] = back(me)

    out = pl.BlockSpec((1, half, width), lambda i: (i, 0, 0))
    tall = pl.BlockSpec((1, frames, local), lambda i: (i, 0, 0))
    return call(
        body,
        (items,),
        [
            SMEM_SPEC, SMEM_SPEC, out, out, whole(w_out.shape), tall, tall, tall,
            pl.BlockSpec((1, heads, frames), lambda i: (i, 0, 0)),
            whole(w_query.shape), whole(w_key.shape), whole(w_value.shape),
        ],
        [tall, tall, tall, out, out],
        [shape_of(query.shape, BF16)] * 3
        + [shape_of(grad_own.shape, F32), shape_of(grad_own.shape, BF16)],
        (
            rank, valid, grad_own, grad_other, w_out, query, key, value, lse,
            w_query, w_key, w_value,
        ),
        scratch=[pltpu.VMEM((2, half, local), BF16)],
    )


DOWN, UP, REST, CROSS, PROJ, QUERY, KEY, VALUE = range(8)
(
    D_W_QUERY,
    D_W_KEY,
    D_W_VALUE,
    D_W_OUT,
    D_C_QUERY,
    D_C_KEY,
    D_C_VALUE,
    D_C_OUT,
    D_W_UP,
    D_W_DOWN,
) = range(10)
BLOCKS = 16
LEVELS = 4
LANES = 512


class Piece:
    def __init__(self, terms, rows, first, width, tile, full):
        self.terms, self.rows, self.first = terms, rows, first
        self.width, self.tile, self.full = width, tile, full


def place_of(block, order):
    place = 0
    for k, bit in enumerate(order):
        place = place + (((block >> bit) & 1) << (LEVELS - 1 - k))
    return place


def block_at(place, order):
    return sum(((place >> (LEVELS - 1 - k)) & 1) << bit for k, bit in enumerate(order))


def gradient_packet(block_index, pieces, order, operands):
    rows_each = sum(piece.rows // BLOCKS * (piece.width // LANES) for piece in pieces)
    count = len(operands)
    starts = []
    steps = 0
    for piece in pieces:
        starts.append(steps)
        steps += piece.rows // piece.tile if piece.tile < piece.rows else piece.width // LANES

    def body(*refs):
        me = refs[0][0]
        given = refs[1 : 1 + count]
        keep, send, natural = refs[1 + count :]
        step = pl.program_id(0)
        offset = 0
        for start, piece in zip(starts, pieces):
            by_rows = piece.tile < piece.rows
            number = piece.rows // piece.tile if by_rows else piece.width // LANES
            each = piece.rows // BLOCKS

            @pl.when((step >= start) & (step < start + number))
            def _(start=start, piece=piece, by_rows=by_rows, each=each, offset=offset):
                total = None
                for (left, left_at), (right, right_at) in piece.terms:
                    term = dot_lt(given[left][left_at], given[right][right_at])
                    total = term if total is None else total + term
                natural[: piece.tile, :] = total.astype(BF16)
                at = step - start
                for sub in range(piece.tile // each):
                    block = (at * (piece.tile // each) + sub if by_rows else sub) ^ me
                    place = place_of(block, order)
                    base = offset if by_rows else offset + at * each
                    rows = pl.ds(base, each)
                    values = natural[sub * each : (sub + 1) * each, :]

                    @pl.when(place < BLOCKS // 2)
                    def _():
                        keep[place, rows, :] = values

                    @pl.when(place >= BLOCKS // 2)
                    def _():
                        send[place - BLOCKS // 2, rows, :] = values

            offset += each * (piece.width // LANES)

    def spec(array, axis, start, number, block):
        if axis is None:
            return whole(array.shape)
        shape = list(array.shape)
        shape[axis] = block
        first, at = start

        def index(i):
            place = [0] * len(shape)
            place[axis] = first + jnp.clip(i - at, 0, number - 1)
            return tuple(place)

        return pl.BlockSpec(tuple(shape), index)

    half_shape = (BLOCKS // 2, rows_each, LANES)
    return call(
        body,
        (steps,),
        [SMEM_SPEC] + [spec(*operand) for operand in operands],
        [whole(half_shape)] * 2,
        [shape_of(half_shape, BF16)] * 2,
        (block_index, *(operand[0] for operand in operands)),
        scratch=[pltpu.VMEM((max(piece.tile for piece in pieces), LANES), BF16)],
    )


def open_packet(block_index, pieces, order, kept, received, before):
    steps = 4
    group = BLOCKS // steps
    previous = [x for x in before if x is not None]

    def body(*refs):
        me = refs[0][0]
        low, high = refs[1], refs[2]
        outs = refs[3 + len(previous) :]
        for step in range(group):
            place = place_of((pl.program_id(0) * group + step) ^ me, order)
            inner = place & (BLOCKS // 2 - 1)
            upper = place >= BLOCKS // 2
            offset = 0
            for out, piece in zip(outs, pieces):
                each = piece.rows // BLOCKS
                for column in range(piece.width // LANES):
                    part = slice(offset, offset + each)
                    values = jnp.where(upper, high[inner, part, :], low[inner, part, :])
                    lanes = slice(column * LANES, (column + 1) * LANES)
                    out[step * each : (step + 1) * each, lanes] = values.astype(F32)
                    offset += each

    out_specs, out_shape, aliases = [], [], {}
    for number, (piece, old) in enumerate(zip(pieces, before)):
        at = piece.first // piece.width
        out_specs.append(
            pl.BlockSpec((piece.rows // steps, piece.width), lambda i, at=at: (i, at))
        )
        out_shape.append(shape_of((piece.rows, piece.full), F32))
        if old is not None:
            aliases[3 + len(aliases)] = number
    return pl.pallas_call(
        body,
        grid=(steps,),
        in_specs=[SMEM_SPEC, whole(kept.shape), whole(kept.shape)]
        + [pl.BlockSpec(memory_space=pl.ANY)] * len(previous),
        out_specs=out_specs,
        out_shape=out_shape,
        input_output_aliases=aliases,
        compiler_params=pltpu.CompilerParams(vmem_limit_bytes=3 * SLACK_BYTES),
        cost_estimate=pl.CostEstimate(flops=0, bytes_accessed=1024, transcendentals=0),
    )(block_index, kept, received, *previous)


def main_bits():
    bits = lax.axis_size("dp").bit_length() - 1
    along_x = (bits - 2) // 2
    main = [0, along_x, bits - 2, bits - 1]
    return main, [bit for bit in range(bits) if bit not in main]


def exchange(values, bit):
    pairs = [(d, d ^ (1 << bit)) for d in range(lax.axis_size("dp"))]
    return lax.ppermute(values, "dp", pairs)


def add_rounded(one, two):
    return (one.astype(F32) + two.astype(F32)).astype(BF16)


SWAP = [(0, 1), (1, 0)]


def swap_cores(values):
    return lax.ppermute(values, "mp", SWAP)


class Program:
    def __init__(self, given):
        self.v = given
        self.out = {}
        self.token = jnp.zeros((8, 128), F32)
        self.packets = {}

    def tie(self, values):
        values, self.token = lax.optimization_barrier((values, self.token))
        return values

    def start(self, name):
        packet = self.packets[name]
        order, step = packet.order, packet.step
        bit = (order + order[::-1])[step]
        if step < LEVELS:
            values = self.tie(packet.send)
        else:
            values = packet.keep = self.tie(packet.keep)
        packet.arrived = exchange(values, self.main[bit])

    def finish(self, name):
        packet = self.packets[name]
        step, keep = packet.step, packet.keep
        arrived = self.tie(packet.arrived)
        packet.arrived = None
        packet.step = step + 1
        if step < LEVELS - 1:
            half = keep.shape[0] // 2
            packet.send = add_rounded(keep[half:], arrived[half:])
            packet.keep = add_rounded(keep[:half], arrived[:half])
            packet.send = self.tie(packet.send)
        elif step == LEVELS - 1:
            keep = add_rounded(keep, arrived)
            for bit in self.extra:
                keep = add_rounded(keep, exchange(keep, bit))
            packet.keep = self.tie(keep)
        elif step < 2 * LEVELS - 1:
            packet.keep = self.tie(jnp.concatenate([keep, arrived], 0))
        else:
            outs = open_packet(
                self.block,
                packet.pieces,
                packet.order,
                keep,
                arrived,
                [self.out.get(out) for out in packet.outs],
            )
            for out, values in zip(packet.outs, outs):
                self.out[out] = values
            self.out[packet.outs[0]] = self.tie(outs[0])

    def packet(self, name, outs, pieces, operands):
        order = ORDERS[name]
        operands = [
            x if isinstance(x, tuple) else (x, None, None, None, None) for x in operands
        ]
        operands[0] = (self.tie(operands[0][0]), *operands[0][1:])
        self.add(name, gradient_packet(self.block, pieces, order, operands), pieces, outs)

    def add(self, name, halves_of, pieces, outs):
        keep, send = halves_of
        self.packets[name] = SimpleNamespace(
            order=ORDERS[name], step=0, keep=keep, send=self.tie(send), pieces=pieces,
            outs=outs, arrived=None,
        )


def stage_text(p):
    v = p.v
    v.text_own = p.tie(v.text_own)
    v.k_cross, v.v_cross = project_text(
        v.text_own, v.text_other, v.c_key, v.c_value
    )
    v.k_cross = p.tie(v.k_cross)


def stage_tokens(p):
    v = p.v
    v.tokens = p.tie(v.tokens)
    items, frames, width = v.tokens.shape
    normed, *heads = project_tokens(
        v.tokens.reshape(items * frames, width),
        v.gain_one,
        v.bias_one,
        v.w_query,
        v.w_key,
        v.w_value,
    )
    v.normed_one = normed
    v.q_self, v.k_self, v.v_self = [x.reshape(items, frames, -1) for x in heads]
    v.q_self = p.tie(v.q_self)


def stage_self(p):
    v = p.v
    v.q_self = p.tie(v.q_self)
    v.mix_self, v.lse_self, v.attn_own, send = self_forward(
        p.rank, v.frame_valid, v.q_self, v.k_self, v.v_self, v.w_out
    )
    v.attn_other = swap_cores(send)
    v.attn_own = p.tie(v.attn_own)


def stage_norm_two(p):
    v = p.v
    v.attn_own = p.tie(v.attn_own)
    v.hidden_one, v.n2_own, v.square_attn = residual_norm(
        p.rank, v.frame_valid, v.tokens, v.attn_own, v.attn_other,
        v.gain_two, v.bias_two,
    )
    v.n2_other = swap_cores(v.n2_own)
    v.n2_own = p.tie(v.n2_own)


def stage_cross(p):
    v = p.v
    v.n2_own = p.tie(v.n2_own)
    v.q_cross, v.mix_cross, v.lse_cross, v.cross_own, send = cross_forward(
        p.rank, v.text_len, v.n2_own, v.n2_other, v.c_query,
        v.k_cross, v.v_cross, v.c_out,
    )
    v.cross_other = swap_cores(send)
    v.cross_own = p.tie(v.cross_own)


def stage_norm_three(p):
    v = p.v
    v.cross_own = p.tie(v.cross_own)
    v.hidden_two, v.n3_own, v.square_cross = residual_norm(
        p.rank, v.frame_valid, v.hidden_one, v.cross_own, v.cross_other,
        v.gain_three, v.bias_three,
    )
    v.n3_other = swap_cores(v.n3_own)
    v.n3_own = p.tie(v.n3_own)


def flat(values):
    return values.reshape(-1, values.shape[-1])


def stage_units(p):
    v = p.v
    v.n3_own = p.tie(v.n3_own)
    units, width = v.w_down.shape
    v.activated, v.grad_up, pairs = feed_forward(
        p.block, ORDERS, flat(v.n3_own), flat(v.n3_other), flat(v.grad_own),
        flat(v.grad_other), v.w_up, v.w_down,
    )
    down = [Piece(None, units, at, LANES, None, width) for at in (0, LANES)]
    up = [
        Piece(None, width, 0, units - LANES, None, units),
        Piece(None, width, units - LANES, LANES, None, units),
    ]
    p.add(DOWN, pairs[DOWN], down[:1], [D_W_DOWN])
    p.add(UP, pairs[UP], up[:1], [D_W_UP])
    p.add(REST, pairs[REST], [down[1], up[1]], [D_W_DOWN, D_W_UP])
    v.grad_up = p.tie(v.grad_up)


HALF_TERMS = [((0, (0,)), (1, ())), ((0, (1,)), (2, ()))]


def stage_back_units(p):
    v = p.v
    v.grad_up = p.tie(v.grad_up)
    own, send = project_halves(v.grad_up, v.w_up, True)
    shape = v.hidden_two.shape
    v.gn3_own, v.gn3_other = own.reshape(shape), swap_cores(send).reshape(shape)
    v.gn3_own = p.tie(v.gn3_own)


def stage_back_three(p):
    v = p.v
    v.gn3_own = p.tie(v.gn3_own)
    v.g_h2, v.d_gain_three, v.d_bias_three, v.g_cross_own = norm_backward(
        p.rank, v.hidden_two, v.gain_three, v.gn3_own, v.gn3_other,
        v.grad_own, False,
    )
    v.g_cross_other = swap_cores(v.g_cross_own)
    v.g_cross_own = p.tie(v.g_cross_own)


def stage_out(p):
    v = p.v
    v.activated = p.tie(v.activated)
    own, send = project_halves(v.activated, v.w_down, False)
    shape = v.hidden_two.shape
    v.ff_own, v.ff_other = own.reshape(shape), swap_cores(send).reshape(shape)
    v.ff_own = p.tie(v.ff_own)


def stage_result(p):
    v = p.v
    v.ff_own = p.tie(v.ff_own)
    v.out, v.square_out, v.square_ff = finish_output(
        p.rank, v.frame_valid, v.hidden_two, v.ff_own, v.ff_other
    )
    v.out = p.tie(v.out)


def stage_back_cross(p):
    v = p.v
    v.g_cross_own = p.tie(v.g_cross_own)
    (
        v.dq_cross, v.dk_cross, v.dv_cross, v.gn2_own, send,
        v.text_grad_own, text_send,
    ) = cross_backward(
        p.rank, v.text_len, v.g_cross_own, v.g_cross_other, v.c_out,
        v.q_cross, v.k_cross, v.v_cross, v.lse_cross,
        v.c_query, v.c_key, v.c_value,
    )
    v.gn2_other = swap_cores(send)
    v.text_grad_other = swap_cores(text_send)
    v.gn2_own = p.tie(v.gn2_own)


def halves(values):
    return values.reshape(2, -1, values.shape[-1])


def stage_cross_packet(p):
    v = p.v
    items, _, _, local = v.dk_cross.shape
    depth = v.c_key.shape[0]
    width = v.c_query.shape[0]
    query_terms = [((1, ()), (0, (0,))), ((2, ()), (0, (1,)))]

    def text_terms(place):
        return [
            ((3 + half, (item,)), (place, (item, half))) for item in range(items) for half in (0, 1)
        ]

    p.packet(
        CROSS, [D_C_QUERY, D_C_KEY, D_C_VALUE],
        [
            Piece(query_terms, width, 0, local, width, local),
            Piece(text_terms(5), depth, 0, local, depth, local),
            Piece(text_terms(6), depth, 0, local, depth, local),
        ],
        [
            halves(v.dq_cross), flat(v.n2_own), flat(v.n2_other),
            v.text_own, v.text_other, v.dk_cross, v.dv_cross,
        ],
    )


def stage_back_two(p):
    v = p.v
    v.gn2_own = p.tie(v.gn2_own)
    v.g_h1, v.d_gain_two, v.d_bias_two, v.g_attn_own = norm_backward(
        p.rank, v.hidden_one, v.gain_two, v.gn2_own, v.gn2_other, v.g_h2, False
    )
    v.g_attn_other = swap_cores(v.g_attn_own)
    v.g_attn_own = p.tie(v.g_attn_own)


def stage_back_self(p):
    v = p.v
    v.g_attn_own = p.tie(v.g_attn_own)
    v.dq_self, v.dk_self, v.dv_self, v.gn1_own, send = self_backward(
        p.rank, v.frame_valid, v.g_attn_own, v.g_attn_other, v.w_out,
        v.q_self, v.k_self, v.v_self, v.lse_self,
        v.w_query, v.w_key, v.w_value,
    )
    v.gn1_other = swap_cores(send)
    v.gn1_own = p.tie(v.gn1_own)


def stage_proj_packet(p):
    v = p.v
    local, width = v.w_out.shape
    terms = [((3, (0,)), (4, ())), ((3, (1,)), (5, ()))]
    steps = width // LANES

    def streamed(name, first):
        return (flat(name), 1, (0, first), steps, LANES)

    p.packet(
        PROJ, [D_C_OUT, D_W_OUT],
        [
            Piece(HALF_TERMS, local, 0, width, local, width),
            Piece(terms, local, 0, width, local, width),
        ],
        [
            halves(v.mix_cross), streamed(v.g_cross_own, 0), streamed(v.g_cross_other, 0),
            halves(v.mix_self), streamed(v.g_attn_own, steps),
            streamed(v.g_attn_other, steps),
        ],
    )


def self_packet(p, name, grad, out):
    v = p.v
    width, local = v.w_query.shape
    piece = Piece([((0, ()), (1, ()))], width, 0, local, width, local)
    p.packet(name, [out], [piece], [v.normed_one, flat(grad)])


def stage_query_packet(p):
    self_packet(p, QUERY, p.v.dq_self, D_W_QUERY)


def stage_key_packet(p):
    self_packet(p, KEY, p.v.dk_self, D_W_KEY)


def stage_value_packet(p):
    self_packet(p, VALUE, p.v.dv_self, D_W_VALUE)


def stage_back_one(p):
    v = p.v
    v.gn1_own = p.tie(v.gn1_own)
    v.d_tokens, v.d_gain_one, v.d_bias_one = norm_backward(
        p.rank, v.tokens, v.gain_one, v.gn1_own, v.gn1_other, v.g_h1, True
    )
    v.d_tokens = p.tie(v.d_tokens)


def stage_text_grad(p):
    v = p.v
    v.text_grad_own = p.tie(v.text_grad_own)
    v.d_text = v.text_grad_own + v.text_grad_other.astype(F32)
    v.d_text = p.tie(v.d_text)


def stage_small(p):
    v = p.v
    half = v.hidden_one.shape[1]
    width = v.hidden_one.shape[2]
    own = jnp.clip(v.frame_valid - p.rank * half, 0, half).sum().astype(F32)
    rows = [
        v.d_gain_one, v.d_bias_one, v.d_gain_two, v.d_bias_two,
        v.d_gain_three, v.d_bias_three, v.square_out, v.square_attn,
        v.square_cross, v.square_ff, jnp.full((1, width), own / width, F32),
    ]
    rows.append(jnp.zeros((16 - len(rows), width), F32))
    total = p.tie(jnp.concatenate(rows, 0))
    v.small = total
    v.small_other = swap_cores(total)
    p.hops = list(range(lax.axis_size("dp").bit_length() - 1))


def stage_hop(p):
    v = p.v
    total = v.small = p.tie(v.small + v.small_other)
    if p.hops:
        v.small_other = exchange(total, p.hops.pop(0))


def stage_rms(p):
    v = p.v
    while p.hops:
        stage_hop(p)
    total = v.small + v.small_other
    width = total.shape[1]
    v.small = total[:6]
    sums = jnp.sum(total[6:11], -1)
    v.rms = jnp.sqrt(sums[:4] / (sums[4] * width))


def stage_end(p):
    p.v.rms = p.v.rms + p.token[0, :4] * 0.0


ORDERS = {
    DOWN: [2, 0, 1, 3],
    UP: [0, 1, 2, 3],
    REST: [1, 0, 2, 3],
    CROSS: [2, 1, 0, 3],
    PROJ: [1, 0, 3, 2],
    QUERY: [0, 1, 2, 3],
    KEY: [1, 0, 3, 2],
    VALUE: [0, 1, 2, 3],
}


PLAN = [
    stage_tokens, stage_self, stage_text, stage_norm_two, stage_cross, stage_norm_three,
    stage_units, REST, UP, DOWN, stage_back_units, stage_back_three, stage_back_cross, REST,
    stage_cross_packet, DOWN, UP, stage_back_two, REST, UP, CROSS, DOWN, stage_back_self, REST,
    UP, DOWN, stage_proj_packet, stage_value_packet, REST, CROSS, stage_key_packet, UP, PROJ,
    stage_query_packet, CROSS, KEY, QUERY, VALUE, DOWN, REST, REST, stage_back_one, UP,
    stage_out, UP, QUERY, REST, REST, PROJ, PROJ, QUERY, VALUE, UP, UP, stage_result, CROSS,
    DOWN, CROSS, REST, KEY, VALUE, REST, PROJ, PROJ, KEY, UP, UP, CROSS, CROSS, REST, REST,
    QUERY, DOWN, PROJ, PROJ, KEY, UP, UP, KEY, VALUE, CROSS, REST, CROSS, DOWN, QUERY, PROJ,
    REST, PROJ, KEY, KEY, QUERY, VALUE, CROSS, CROSS, QUERY, PROJ, PROJ, UP, UP, KEY, KEY, VALUE,
    VALUE, QUERY, QUERY, CROSS, CROSS, KEY, KEY, QUERY, PROJ, PROJ, DOWN, VALUE, VALUE, QUERY,
    KEY, KEY, REST, DOWN, DOWN, VALUE, VALUE, QUERY, QUERY, CROSS, CROSS, UP, VALUE, VALUE, DOWN,
    DOWN, PROJ, PROJ, QUERY, QUERY, KEY, KEY, VALUE, stage_text_grad, DOWN, DOWN, stage_small,
    stage_hop, VALUE, CROSS, stage_hop, QUERY, stage_hop, stage_hop, VALUE, DOWN, PROJ, KEY,
    stage_rms, stage_end,
]

def per_device(
    tokens,
    text_own,
    text_len,
    frame_valid,
    gain_one,
    bias_one,
    gain_two,
    bias_two,
    gain_three,
    bias_three,
    w_query,
    w_key,
    w_value,
    w_out,
    c_query,
    c_key,
    c_value,
    c_out,
    w_up,
    w_down,
    grad_own,
):
    v = SimpleNamespace()
    v.tokens = tokens
    v.text_own = text_own
    v.text_len = text_len
    v.frame_valid = frame_valid
    v.gain_one = gain_one.reshape(1, -1)
    v.bias_one = bias_one.reshape(1, -1)
    v.gain_two = gain_two.reshape(1, -1)
    v.bias_two = bias_two.reshape(1, -1)
    v.gain_three = gain_three.reshape(1, -1)
    v.bias_three = bias_three.reshape(1, -1)
    v.w_query = w_query
    v.w_key = w_key
    v.w_value = w_value
    v.w_out = w_out
    v.c_query = c_query
    v.c_key = c_key
    v.c_value = c_value
    v.c_out = c_out
    v.w_up = w_up
    v.w_down = w_down
    v.grad_own = grad_own
    p = Program(v)
    p.rank = lax.axis_index("mp").astype(jnp.int32).reshape(1)
    p.main, p.extra = main_bits()
    place = lax.axis_index("dp")
    p.block = sum(((place >> bit) & 1) << k for k, bit in enumerate(p.main))
    p.block = p.block.astype(jnp.int32).reshape(1)
    v.text_other = swap_cores(v.text_own)
    v.grad_other = swap_cores(v.grad_own)
    for action in PLAN:
        if callable(action):
            action(p)
        elif p.packets[action].arrived is None:
            p.start(action)
        else:
            p.finish(action)
    return (
        v.out,
        v.d_tokens,
        v.d_text,
        *(v.small[n] for n in range(6)),
        *(p.out[name] for name in range(10)),
        v.rms,
    )


def solution(mesh):
    split = P("dp", "mp", None)
    columns, rows = P(None, "mp"), P("mp", None)
    weights = (columns,) * 3 + (rows,) + (columns,) * 3 + (rows, columns, rows)
    return jax.shard_map(
        per_device,
        mesh=mesh,
        in_specs=(P("dp", None, None), split, P("dp"), P("dp"))
        + (P(),) * 6
        + weights
        + (split,),
        out_specs=(split,) * 3 + (P(),) * 6 + weights + (P(),),
        check_vma=False,
    )
```

```python
import math
from types import SimpleNamespace

import jax
import jax.numpy as jnp
from jax import lax
from jax.experimental import pallas as pl
from jax.experimental.pallas import tpu as pltpu
from jax.sharding import PartitionSpec as P

HD = 64
PAIR = 2 * HD
norm_eps = 1e-05
score_scale = 0.125
masked_fill = -1e30
F32 = jnp.float32
BF16 = jnp.bfloat16
SLACK_BYTES = 6 * 1024 * 1024
SMEM_SPEC = pl.BlockSpec(memory_space=pltpu.SMEM)


def dot(a, b):
    return lax.dot_general(a, b, (((1,), (0,)), ((), ())), preferred_element_type=F32)


def dot_rt(a, b):
    return lax.dot_general(a, b, (((1,), (1,)), ((), ())), preferred_element_type=F32)


def dot_lt(a, b):
    return lax.dot_general(a, b, (((0,), (0,)), ((), ())), preferred_element_type=F32)


def whole(shape):
    zeros = (0,) * len(shape)
    return pl.BlockSpec(tuple(shape), lambda *_: zeros)


def shape_of(shape, kind):
    return jax.ShapeDtypeStruct(tuple(shape), kind)


def vmem_bytes(specs, arrays, scratch=()):
    total = SLACK_BYTES
    for spec, array in zip(specs, arrays):
        if spec.block_shape is not None:
            total += 2 * math.prod(spec.block_shape) * jnp.dtype(array.dtype).itemsize
    for buffer in scratch:
        total += math.prod(buffer.shape) * jnp.dtype(buffer.dtype).itemsize
    return min(total, 60 * 1024 * 1024)


def call(body, grid, in_specs, out_specs, out_shape, args, scratch=(), flops=0):
    return pl.pallas_call(
        body,
        grid=grid,
        in_specs=in_specs,
        out_specs=out_specs,
        out_shape=out_shape,
        scratch_shapes=list(scratch),
        compiler_params=pltpu.CompilerParams(
            vmem_limit_bytes=vmem_bytes(
                [*in_specs, *out_specs], [*args, *out_shape], scratch
            )
        ),
        cost_estimate=pl.CostEstimate(flops=flops, bytes_accessed=1024, transcendentals=0),
    )(*args)


def norm_parts(values):
    average = jnp.mean(values, -1, keepdims=True)
    centered = values - average
    variance = jnp.mean(centered * centered, -1, keepdims=True)
    scale = lax.rsqrt(variance + norm_eps)
    return centered * scale, scale


def layer_norm(values, gain_ref, bias_ref):
    normed, _ = norm_parts(values)
    return normed * gain_ref[...].astype(F32) + bias_ref[...].astype(F32)


ROW_BLOCK = 256


def add_row(ref, row):
    first = (pl.program_id(0) == 0) & (pl.program_id(1) == 0)

    @pl.when(first)
    def _():
        ref[...] = row

    @pl.when(jnp.logical_not(first))
    def _():
        ref[...] += row


def column_sum(values):
    return jnp.sum(values, 0, keepdims=True)


def row_mask(rank_ref, half, count):
    first_row = rank_ref[0] * half + pl.program_id(1) * ROW_BLOCK
    place = first_row + lax.broadcasted_iota(jnp.int32, (ROW_BLOCK, 1), 0)
    return (place < count).astype(F32)


def project_tokens(tokens, gain, bias, w_query, w_key, w_value):
    rows, width = tokens.shape
    local = w_query.shape[1]
    block = 256

    def body(x, g, b, wq, wk, wv, n, q, k, v):
        normed = layer_norm(x[...].astype(F32), g, b).astype(BF16)
        n[...] = normed
        q[...] = dot(normed, wq[...]).astype(BF16)
        k[...] = dot(normed, wk[...]).astype(BF16)
        v[...] = dot(normed, wv[...]).astype(BF16)

    wide = pl.BlockSpec((block, width), lambda i: (i, 0))
    slim = pl.BlockSpec((block, local), lambda i: (i, 0))
    return call(
        body,
        (rows // block,),
        [wide, whole((1, width)), whole((1, width))] + [whole(w_query.shape)] * 3,
        [wide, slim, slim, slim],
        [shape_of((rows, width), BF16)] + [shape_of((rows, local), BF16)] * 3,
        (tokens, gain, bias, w_query, w_key, w_value),
    )


def project_text(text_own, text_other, c_key, c_value):
    items, text_half, depth = text_own.shape
    local = c_key.shape[1]

    def body(own, other, wk, wv, k, v):
        for half, rows in enumerate((own, other)):
            for item in range(items):
                k[item, half] = dot(rows[item], wk[...]).astype(BF16)
                v[item, half] = dot(rows[item], wv[...]).astype(BF16)

    shape = (items, 2, text_half, local)
    return call(
        body,
        (1,),
        [whole(text_own.shape)] * 2 + [whole(c_key.shape)] * 2,
        [whole(shape)] * 2,
        [shape_of(shape, BF16)] * 2,
        (text_own, text_other, c_key, c_value),
    )


def head_mask(rows, head):
    lane = lax.broadcasted_iota(jnp.int32, (rows, PAIR), 1)
    return lane < HD if head == 0 else lane >= HD


def pick(first, second):
    return jnp.where(head_mask(first.shape[0], 0), first, second)


def only(values, head):
    return jnp.where(head_mask(values.shape[0], head), values, jnp.zeros_like(values))


def scores_t(query_pair, key_pair, head, masked):
    return dot_rt(key_pair, only(query_pair, head) * jnp.asarray(score_scale, BF16)) + masked


def attend_pair(query_pair, key_pair, value_pair, allowed, lse_ref, lse_at):
    mixed = []
    for head in range(2):
        scores = scores_t(query_pair, key_pair, head, allowed)
        highest = jnp.max(scores, 0, keepdims=True)
        powers = jnp.exp(scores - highest)
        total = jnp.sum(powers, 0, keepdims=True)
        probs = (powers * (1.0 / total)).astype(BF16)
        mixed.append(dot_lt(probs, value_pair))
        row, columns = lse_at(head)
        lse_ref[0, row : row + 1, columns] = highest + jnp.log(total)
    return pick(mixed[0], mixed[1]).astype(BF16)


def attend_pair_back(query_pair, key_pair, value_pair, allowed, lse_rows, grad_pair):
    grads = []
    for head in range(2):
        probs = jnp.exp(scores_t(query_pair, key_pair, head, allowed) - lse_rows[head])
        grad_probs = dot_rt(value_pair, only(grad_pair, head))
        inner = jnp.sum(grad_probs * probs, 0, keepdims=True)
        grad_scores = (probs * (grad_probs - inner)).astype(BF16)
        grads.append(
            (
                dot_lt(grad_scores, key_pair),
                dot(grad_scores, query_pair),
                dot(probs.astype(BF16), grad_pair),
            )
        )
    return [pick(one, two) for one, two in zip(grads[0], grads[1])]


def causal_mask(keys, queries, first_query, count):
    key_at = lax.broadcasted_iota(jnp.int32, (keys, queries), 0)
    query_at = first_query + lax.broadcasted_iota(jnp.int32, (keys, queries), 1)
    return jnp.where((key_at <= query_at) & (key_at < count), 0.0, masked_fill)


def text_mask(text_half, queries, rank, count):
    key_at = lax.broadcasted_iota(jnp.int32, (2 * text_half, queries), 0)
    swapped = jnp.where(key_at < text_half, key_at + text_half, key_at - text_half)
    return jnp.where(jnp.where(rank == 0, key_at, swapped) < count, 0.0, masked_fill)


def self_forward(rank, valid, query, key, value, w_out):
    items, frames, local = query.shape
    width = w_out.shape[1]
    half = frames // 2
    heads = local // HD

    def body(rank_ref, valid_ref, q, k, v, w, mix, lse, own, send):
        me = rank_ref[0]
        count = valid_ref[pl.program_id(0)]
        for part in range(2):
            keys = (part + 1) * half
            allowed = causal_mask(keys, half, part * half, count)
            rows = slice(part * half, (part + 1) * half)
            for pair in range(local // PAIR):
                columns = slice(pair * PAIR, (pair + 1) * PAIR)
                mix[part ^ me, 0, :, columns] = attend_pair(
                    q[0, rows, columns],
                    k[0, :keys, columns],
                    v[0, :keys, columns],
                    allowed,
                    lse,
                    lambda head: (2 * pair + head, rows),
                )
        send[0] = dot(mix[1, 0], w[...]).astype(BF16)
        own[0] = dot(mix[0, 0], w[...])

    tall = pl.BlockSpec((1, frames, local), lambda i: (i, 0, 0))
    out = pl.BlockSpec((1, half, width), lambda i: (i, 0, 0))
    return call(
        body,
        (items,),
        [SMEM_SPEC, SMEM_SPEC, tall, tall, tall, whole(w_out.shape)],
        [
            pl.BlockSpec((2, 1, half, local), lambda i: (0, i, 0, 0)),
            pl.BlockSpec((1, heads, frames), lambda i: (i, 0, 0)),
            out,
            out,
        ],
        [
            shape_of((2, items, half, local), BF16),
            shape_of((items, heads, frames), F32),
            shape_of((items, half, width), F32),
            shape_of((items, half, width), BF16),
        ],
        (rank, valid, query, key, value, w_out),
    )


def cross_forward(rank, text_len, normed_own, normed_other, c_query, key, value, c_out):
    items, half, width = normed_own.shape
    text_half = key.shape[2]
    local = c_query.shape[1]
    heads = local // HD

    def body(rank_ref, len_ref, own_n, other_n, wq, k, v, w, q, mix, lse, own, send):
        allowed = text_mask(text_half, half, rank_ref[0], len_ref[pl.program_id(0)])
        for part, normed in enumerate((own_n, other_n)):
            q[part, 0] = dot(normed[0], wq[...]).astype(BF16)
            for pair in range(local // PAIR):
                columns = slice(pair * PAIR, (pair + 1) * PAIR)
                mix[part, 0, :, columns] = attend_pair(
                    q[part, 0, :, columns],
                    k[0, :, :, columns].reshape(2 * text_half, PAIR),
                    v[0, :, :, columns].reshape(2 * text_half, PAIR),
                    allowed,
                    lse,
                    lambda head: (2 * pair + head, slice(part * half, (part + 1) * half)),
                )
        send[0] = dot(mix[1, 0], w[...]).astype(BF16)
        own[0] = dot(mix[0, 0], w[...])

    out = pl.BlockSpec((1, half, width), lambda i: (i, 0, 0))
    text = pl.BlockSpec((1, 2, text_half, local), lambda i: (i, 0, 0, 0))
    both = pl.BlockSpec((2, 1, half, local), lambda i: (0, i, 0, 0))
    return call(
        body,
        (items,),
        [SMEM_SPEC, SMEM_SPEC, out, out, whole(c_query.shape), text, text, whole(c_out.shape)],
        [both, both, pl.BlockSpec((1, heads, 2 * half), lambda i: (i, 0, 0)), out, out],
        [
            shape_of((2, items, half, local), BF16),
            shape_of((2, items, half, local), BF16),
            shape_of((items, heads, 2 * half), F32),
            shape_of((items, half, width), F32),
            shape_of((items, half, width), BF16),
        ],
        (rank, text_len, normed_own, normed_other, c_query, key, value, c_out),
    )


def residual_norm(rank, valid, base, own, received, gain, bias):
    items, half, width = own.shape

    def body(rank_ref, valid_ref, x, part, other, g, b, hidden, normed, square):
        item = pl.program_id(0)
        branch = part[0] + other[0].astype(F32)
        total = x[0].astype(F32) + branch
        hidden[0] = total
        normed[0] = layer_norm(total, g, b).astype(BF16)
        mask = row_mask(rank_ref, half, valid_ref[item])
        add_row(square, column_sum(mask * branch * branch))

    steps = half // ROW_BLOCK
    block = pl.BlockSpec((1, ROW_BLOCK, width), lambda i, r, *_: (i, r, 0))
    row = whole((1, width))
    if base.shape[1] == half:
        base_spec = block
    else:
        base_spec = pl.BlockSpec(
            (1, ROW_BLOCK, width), lambda i, r, me, _: (i, me[0] * steps + r, 0)
        )
    return pl.pallas_call(
        body,
        grid_spec=pltpu.PrefetchScalarGridSpec(
            num_scalar_prefetch=2,
            grid=(items, steps),
            in_specs=[base_spec, block, block, row, row],
            out_specs=[block, block, row],
        ),
        out_shape=[
            shape_of(own.shape, F32),
            shape_of(own.shape, BF16),
            shape_of((1, width), F32),
        ],
        compiler_params=pltpu.CompilerParams(vmem_limit_bytes=3 * SLACK_BYTES),
        cost_estimate=pl.CostEstimate(flops=0, bytes_accessed=1024, transcendentals=0),
    )(rank, valid, base, own, received, gain, bias)


def gelu_parts(values):
    normal = 0.5 * (1.0 + lax.erf(values * (0.5**0.5)))
    density = jnp.exp(-0.5 * values * values) * 0.3989422804014327
    return values * normal, normal + values * density


def feed_forward(
    block_index, orders, normed_own, normed_other, grad_own, grad_other, w_up, w_down
):
    rows, width = normed_own.shape
    units = w_up.shape[1]
    steps = units // LANES
    down_each, up_each = units // BLOCKS, width // BLOCKS
    sizes = {DOWN: down_each, UP: up_each * (steps - 1), REST: down_each + up_each}

    def body(me_ref, n_own, n_other, g_own, g_other, up_w, down_w, act, grad, *rest):
        me = me_ref[0]
        packets = {name: rest[2 * k : 2 * k + 2] for k, name in enumerate(sizes)}
        down_part, up_part = rest[2 * len(sizes) :]
        step = pl.program_id(0)
        down_sum, up_sum = 0.0, 0.0
        for half, (n, g) in enumerate(((n_own, g_own), (n_other, g_other))):
            value, slope = gelu_parts(dot(n[...], up_w[...]))
            act[half] = value.astype(BF16)
            grad[half] = (dot_rt(g[...], down_w[...]) * slope).astype(BF16)
            down_sum = down_sum + dot_lt(act[half], g[...])
            up_sum = up_sum + dot_lt(n[...], grad[half])
        down_part[...] = down_sum.astype(BF16)
        up_part[...] = up_sum.astype(BF16)

        def put(name, block, first, values):
            place = place_of(block ^ me, orders[name])
            keep, send = packets[name]
            where = pl.ds(first, values.shape[0])

            @pl.when(place < BLOCKS // 2)
            def _():
                keep[place, where, :] = values

            @pl.when(place >= BLOCKS // 2)
            def _():
                send[place - BLOCKS // 2, where, :] = values

        for sub in range(LANES // down_each):
            part = slice(sub * down_each, (sub + 1) * down_each)
            block = step * (LANES // down_each) + sub
            put(DOWN, block, 0, down_part[part, :LANES])
            put(REST, block, 0, down_part[part, LANES:])

        @pl.when(step < steps - 1)
        def _():
            for block in range(BLOCKS):
                part = slice(block * up_each, (block + 1) * up_each)
                put(UP, block, step * up_each, up_part[part, :])

        @pl.when(step == steps - 1)
        def _():
            for block in range(BLOCKS):
                part = slice(block * up_each, (block + 1) * up_each)
                put(REST, block, down_each, up_part[part, :])

    out = pl.BlockSpec((2, rows, LANES), lambda j: (0, 0, j))
    shapes = [(BLOCKS // 2, sizes[name], LANES) for name in sizes for _ in range(2)]
    results = call(
        body,
        (steps,),
        [SMEM_SPEC]
        + [whole(normed_own.shape)] * 4
        + [
            pl.BlockSpec((width, LANES), lambda j: (0, j)),
            pl.BlockSpec((LANES, width), lambda j: (j, 0)),
        ],
        [out, out] + [whole(shape) for shape in shapes],
        [shape_of((2, rows, units), BF16)] * 2 + [shape_of(shape, BF16) for shape in shapes],
        (block_index, normed_own, normed_other, grad_own, grad_other, w_up, w_down),
        scratch=[pltpu.VMEM((LANES, width), BF16), pltpu.VMEM((width, LANES), BF16)],
    )
    pairs = {name: results[2 + 2 * k : 4 + 2 * k] for k, name in enumerate(sizes)}
    return results[0], results[1], pairs


def project_halves(values, weight, transposed):
    _, rows, depth = values.shape
    width = weight.shape[0] if transposed else weight.shape[1]

    def body(a, w, own, send):
        multiply = dot_rt if transposed else dot
        product = multiply(a[0], w[...])

        @pl.when(pl.program_id(0) == 0)
        def _():
            send[...] = product.astype(BF16)

        @pl.when(pl.program_id(0) == 1)
        def _():
            own[...] = product

    return call(
        body,
        (2,),
        [pl.BlockSpec((1, rows, depth), lambda j: (1 - j, 0, 0)), whole(weight.shape)],
        [whole((rows, width))] * 2,
        [shape_of((rows, width), F32), shape_of((rows, width), BF16)],
        (values, weight),
    )


def finish_output(rank, valid, hidden, own, received):
    items, half, width = hidden.shape

    def body(rank_ref, valid_ref, x, part, other, out, square, branch_square):
        branch = part[0] + other[0].astype(F32)
        total = x[0] + branch
        out[0] = total.astype(BF16)
        mask = row_mask(rank_ref, half, valid_ref[pl.program_id(0)])
        add_row(square, column_sum(mask * total * total))
        add_row(branch_square, column_sum(mask * branch * branch))

    steps = half // ROW_BLOCK
    block = pl.BlockSpec((1, ROW_BLOCK, width), lambda i, r: (i, r, 0))
    return call(
        body,
        (items, steps),
        [SMEM_SPEC, SMEM_SPEC, block, block, block],
        [block, whole((1, width)), whole((1, width))],
        [shape_of(hidden.shape, BF16)] + [shape_of((1, width), F32)] * 2,
        (rank, valid, hidden, own, received),
    )


def norm_backward(rank, values, gain, own, received, grad_base, last):
    items, half, width = own.shape

    def body(rank_ref, x, g, part, other, base, *outs):
        normed, scale = norm_parts(x[0].astype(F32))
        grad = part[0] + other[0].astype(F32)
        add_row(outs[1], column_sum(grad * normed))
        add_row(outs[2], column_sum(grad))
        scaled = grad * g[...].astype(F32)
        first = jnp.mean(scaled, -1, keepdims=True)
        second = jnp.mean(scaled * normed, -1, keepdims=True)
        total = base[0].astype(F32) + scale * (scaled - first - normed * second)
        outs[0][0] = total
        if not last:
            outs[3][0] = total.astype(BF16)

    steps = half // ROW_BLOCK
    block = pl.BlockSpec((1, ROW_BLOCK, width), lambda i, r, *_: (i, r, 0))
    row = whole((1, width))
    if values.shape[1] == half:
        values_spec = block
    else:
        values_spec = pl.BlockSpec(
            (1, ROW_BLOCK, width), lambda i, r, me: (i, me[0] * steps + r, 0)
        )
    out_specs = [block, row, row]
    out_shape = [
        shape_of(own.shape, F32),
        shape_of((1, width), F32),
        shape_of((1, width), F32),
    ]
    if not last:
        out_specs.append(block)
        out_shape.append(shape_of(own.shape, BF16))
    return pl.pallas_call(
        body,
        grid_spec=pltpu.PrefetchScalarGridSpec(
            num_scalar_prefetch=1,
            grid=(items, steps),
            in_specs=[values_spec, row, block, block, block],
            out_specs=out_specs,
        ),
        out_shape=out_shape,
        compiler_params=pltpu.CompilerParams(vmem_limit_bytes=3 * SLACK_BYTES),
        cost_estimate=pl.CostEstimate(flops=0, bytes_accessed=1024, transcendentals=0),
    )(rank, values, gain, own, received, grad_base)


def cross_backward(
    rank, text_len, grad_own, grad_other, c_out, query, key, value, lse, c_query, c_key, c_value
):
    items, half, width = grad_own.shape
    text_half = key.shape[2]
    depth, local = c_key.shape
    heads = local // HD

    def body(
        rank_ref, len_ref, g_own, g_other, w, q, k, v, stats, wq, wk, wv,
        dq, dk, dv, own, send, text_own, text_send, grad_mix,
    ):
        allowed = text_mask(text_half, half, rank_ref[0], len_ref[pl.program_id(0)])
        for part, grad in enumerate((g_own, g_other)):
            grad_mix[part] = dot_rt(grad[0], w[...]).astype(BF16)
        for pair in range(local // PAIR):
            columns = slice(pair * PAIR, (pair + 1) * PAIR)
            key_sum, value_sum = 0.0, 0.0
            for part in range(2):
                rows = slice(part * half, (part + 1) * half)
                one, two, three = attend_pair_back(
                    q[part, 0, :, columns],
                    k[0, :, :, columns].reshape(2 * text_half, PAIR),
                    v[0, :, :, columns].reshape(2 * text_half, PAIR),
                    allowed,
                    [stats[0, 2 * pair + head : 2 * pair + head + 1, rows] for head in range(2)],
                    grad_mix[part, :, columns],
                )
                dq[part, 0, :, columns] = (one * score_scale).astype(BF16)
                key_sum, value_sum = key_sum + two, value_sum + three
            key_sum = (key_sum * score_scale).astype(BF16)
            value_sum = value_sum.astype(BF16)
            for part in range(2):
                rows = slice(part * text_half, (part + 1) * text_half)
                dk[0, part, :, columns] = key_sum[rows]
                dv[0, part, :, columns] = value_sum[rows]
        send[0] = dot_rt(dq[1, 0], wq[...]).astype(BF16)
        own[0] = dot_rt(dq[0, 0], wq[...])
        text_send[0] = (dot_rt(dk[0, 1], wk[...]) + dot_rt(dv[0, 1], wv[...])).astype(BF16)
        text_own[0] = dot_rt(dk[0, 0], wk[...]) + dot_rt(dv[0, 0], wv[...])

    out = pl.BlockSpec((1, half, width), lambda i: (i, 0, 0))
    text = pl.BlockSpec((1, 2, text_half, local), lambda i: (i, 0, 0, 0))
    both = pl.BlockSpec((2, 1, half, local), lambda i: (0, i, 0, 0))
    deep = pl.BlockSpec((1, text_half, depth), lambda i: (i, 0, 0))
    return call(
        body,
        (items,),
        [
            SMEM_SPEC, SMEM_SPEC, out, out, whole(c_out.shape), both, text, text,
            pl.BlockSpec((1, heads, 2 * half), lambda i: (i, 0, 0)),
            whole(c_query.shape), whole(c_key.shape), whole(c_value.shape),
        ],
        [both, text, text, out, out, deep, deep],
        [
            shape_of(query.shape, BF16),
            shape_of(key.shape, BF16),
            shape_of(key.shape, BF16),
            shape_of(grad_own.shape, F32),
            shape_of(grad_own.shape, BF16),
            shape_of((items, text_half, depth), F32),
            shape_of((items, text_half, depth), BF16),
        ],
        (
            rank, text_len, grad_own, grad_other, c_out, query, key, value, lse,
            c_query, c_key, c_value,
        ),
        scratch=[pltpu.VMEM((2, half, local), BF16)],
    )


def self_backward(
    rank, valid, grad_own, grad_other, w_out, query, key, value, lse, w_query, w_key, w_value
):
    items, half, width = grad_own.shape
    frames, local = query.shape[1:]
    heads = local // HD

    def body(
        rank_ref, valid_ref, g_own, g_other, w, q, k, v, stats, wq, wk, wv,
        dq, dk, dv, own, send, grad_mix,
    ):
        me = rank_ref[0]
        count = valid_ref[pl.program_id(0)]
        grad_mix[me] = dot_rt(g_own[0], w[...]).astype(BF16)
        grad_mix[1 - me] = dot_rt(g_other[0], w[...]).astype(BF16)
        masks = [causal_mask((part + 1) * half, half, part * half, count) for part in range(2)]
        for pair in range(local // PAIR):
            columns = slice(pair * PAIR, (pair + 1) * PAIR)
            sums = []
            for part in range(2):
                keys = (part + 1) * half
                rows = slice(part * half, keys)
                one, two, three = attend_pair_back(
                    q[0, rows, columns],
                    k[0, :keys, columns],
                    v[0, :keys, columns],
                    masks[part],
                    [stats[0, 2 * pair + head : 2 * pair + head + 1, rows] for head in range(2)],
                    grad_mix[part, :, columns],
                )
                dq[0, rows, columns] = (one * score_scale).astype(BF16)
                sums.append((two, three))
            (key_a, value_a), (key_b, value_b) = sums
            dk[0, :half, columns] = ((key_a + key_b[:half]) * score_scale).astype(BF16)
            dk[0, half:, columns] = (key_b[half:] * score_scale).astype(BF16)
            dv[0, :half, columns] = (value_a + value_b[:half]).astype(BF16)
            dv[0, half:, columns] = value_b[half:].astype(BF16)

        def back(part):
            rows = pl.ds(pl.multiple_of(part * half, half), half)
            return (
                dot_rt(dq[0, rows, :], wq[...])
                + dot_rt(dk[0, rows, :], wk[...])
                + dot_rt(dv[0, rows, :], wv[...])
            )

        send[0] = back(1 - me).astype(BF16)
        own[0] = back(me)

    out = pl.BlockSpec((1, half, width), lambda i: (i, 0, 0))
    tall = pl.BlockSpec((1, frames, local), lambda i: (i, 0, 0))
    return call(
        body,
        (items,),
        [
            SMEM_SPEC, SMEM_SPEC, out, out, whole(w_out.shape), tall, tall, tall,
            pl.BlockSpec((1, heads, frames), lambda i: (i, 0, 0)),
            whole(w_query.shape), whole(w_key.shape), whole(w_value.shape),
        ],
        [tall, tall, tall, out, out],
        [shape_of(query.shape, BF16)] * 3
        + [shape_of(grad_own.shape, F32), shape_of(grad_own.shape, BF16)],
        (
            rank, valid, grad_own, grad_other, w_out, query, key, value, lse,
            w_query, w_key, w_value,
        ),
        scratch=[pltpu.VMEM((2, half, local), BF16)],
    )


DOWN, UP, REST, CROSS, PROJ, QUERY, KEY, VALUE = range(8)
(
    D_W_QUERY,
    D_W_KEY,
    D_W_VALUE,
    D_W_OUT,
    D_C_QUERY,
    D_C_KEY,
    D_C_VALUE,
    D_C_OUT,
    D_W_UP,
    D_W_DOWN,
) = range(10)
BLOCKS = 16
LEVELS = 4
LANES = 512


class Piece:
    def __init__(self, terms, rows, first, width, tile, full):
        self.terms, self.rows, self.first = terms, rows, first
        self.width, self.tile, self.full = width, tile, full


def place_of(block, order):
    place = 0
    for k, bit in enumerate(order):
        place = place + (((block >> bit) & 1) << (LEVELS - 1 - k))
    return place


def block_at(place, order):
    return sum(((place >> (LEVELS - 1 - k)) & 1) << bit for k, bit in enumerate(order))


def gradient_packet(block_index, pieces, order, operands):
    rows_each = sum(piece.rows // BLOCKS * (piece.width // LANES) for piece in pieces)
    count = len(operands)
    starts = []
    steps = 0
    for piece in pieces:
        starts.append(steps)
        steps += piece.rows // piece.tile if piece.tile < piece.rows else piece.width // LANES

    def body(*refs):
        me = refs[0][0]
        given = refs[1 : 1 + count]
        keep, send, natural = refs[1 + count :]
        step = pl.program_id(0)
        offset = 0
        for start, piece in zip(starts, pieces):
            by_rows = piece.tile < piece.rows
            number = piece.rows // piece.tile if by_rows else piece.width // LANES
            each = piece.rows // BLOCKS

            @pl.when((step >= start) & (step < start + number))
            def _(start=start, piece=piece, by_rows=by_rows, each=each, offset=offset):
                total = None
                for (left, left_at), (right, right_at) in piece.terms:
                    term = dot_lt(given[left][left_at], given[right][right_at])
                    total = term if total is None else total + term
                natural[: piece.tile, :] = total.astype(BF16)
                at = step - start
                for sub in range(piece.tile // each):
                    block = (at * (piece.tile // each) + sub if by_rows else sub) ^ me
                    place = place_of(block, order)
                    base = offset if by_rows else offset + at * each
                    rows = pl.ds(base, each)
                    values = natural[sub * each : (sub + 1) * each, :]

                    @pl.when(place < BLOCKS // 2)
                    def _():
                        keep[place, rows, :] = values

                    @pl.when(place >= BLOCKS // 2)
                    def _():
                        send[place - BLOCKS // 2, rows, :] = values

            offset += each * (piece.width // LANES)

    def spec(array, axis, start, number, block):
        if axis is None:
            return whole(array.shape)
        shape = list(array.shape)
        shape[axis] = block
        first, at = start

        def index(i):
            place = [0] * len(shape)
            place[axis] = first + jnp.clip(i - at, 0, number - 1)
            return tuple(place)

        return pl.BlockSpec(tuple(shape), index)

    half_shape = (BLOCKS // 2, rows_each, LANES)
    return call(
        body,
        (steps,),
        [SMEM_SPEC] + [spec(*operand) for operand in operands],
        [whole(half_shape)] * 2,
        [shape_of(half_shape, BF16)] * 2,
        (block_index, *(operand[0] for operand in operands)),
        scratch=[pltpu.VMEM((max(piece.tile for piece in pieces), LANES), BF16)],
    )


def open_packet(block_index, pieces, order, kept, received, before):
    steps = 4
    group = BLOCKS // steps
    previous = [x for x in before if x is not None]

    def body(*refs):
        me = refs[0][0]
        low, high = refs[1], refs[2]
        outs = refs[3 + len(previous) :]
        for step in range(group):
            place = place_of((pl.program_id(0) * group + step) ^ me, order)
            inner = place & (BLOCKS // 2 - 1)
            upper = place >= BLOCKS // 2
            offset = 0
            for out, piece in zip(outs, pieces):
                each = piece.rows // BLOCKS
                for column in range(piece.width // LANES):
                    part = slice(offset, offset + each)
                    values = jnp.where(upper, high[inner, part, :], low[inner, part, :])
                    lanes = slice(column * LANES, (column + 1) * LANES)
                    out[step * each : (step + 1) * each, lanes] = values.astype(F32)
                    offset += each

    out_specs, out_shape, aliases = [], [], {}
    for number, (piece, old) in enumerate(zip(pieces, before)):
        at = piece.first // piece.width
        out_specs.append(
            pl.BlockSpec((piece.rows // steps, piece.width), lambda i, at=at: (i, at))
        )
        out_shape.append(shape_of((piece.rows, piece.full), F32))
        if old is not None:
            aliases[3 + len(aliases)] = number
    return pl.pallas_call(
        body,
        grid=(steps,),
        in_specs=[SMEM_SPEC, whole(kept.shape), whole(kept.shape)]
        + [pl.BlockSpec(memory_space=pl.ANY)] * len(previous),
        out_specs=out_specs,
        out_shape=out_shape,
        input_output_aliases=aliases,
        compiler_params=pltpu.CompilerParams(vmem_limit_bytes=3 * SLACK_BYTES),
        cost_estimate=pl.CostEstimate(flops=0, bytes_accessed=1024, transcendentals=0),
    )(block_index, kept, received, *previous)


def main_bits():
    bits = lax.axis_size("dp").bit_length() - 1
    along_x = (bits - 2) // 2
    main = [0, along_x, bits - 2, bits - 1]
    return main, [bit for bit in range(bits) if bit not in main]


def exchange(values, bit):
    pairs = [(d, d ^ (1 << bit)) for d in range(lax.axis_size("dp"))]
    return lax.ppermute(values, "dp", pairs)


def add_rounded(one, two):
    return (one.astype(F32) + two.astype(F32)).astype(BF16)


SWAP = [(0, 1), (1, 0)]


def swap_cores(values):
    return lax.ppermute(values, "mp", SWAP)


class Program:
    def __init__(self, given):
        self.v = given
        self.out = {}
        self.token = jnp.zeros((8, 128), F32)
        self.packets = {}

    def tie(self, values):
        values, self.token = lax.optimization_barrier((values, self.token))
        return values

    def start(self, name):
        packet = self.packets[name]
        order, step = packet.order, packet.step
        bit = (order + order[::-1])[step]
        if step < LEVELS:
            values = self.tie(packet.send)
        else:
            values = packet.keep = self.tie(packet.keep)
        packet.arrived = exchange(values, self.main[bit])

    def finish(self, name):
        packet = self.packets[name]
        step, keep = packet.step, packet.keep
        arrived = self.tie(packet.arrived)
        packet.arrived = None
        packet.step = step + 1
        if step < LEVELS - 1:
            half = keep.shape[0] // 2
            packet.send = add_rounded(keep[half:], arrived[half:])
            packet.keep = add_rounded(keep[:half], arrived[:half])
            packet.send = self.tie(packet.send)
        elif step == LEVELS - 1:
            keep = add_rounded(keep, arrived)
            for bit in self.extra:
                keep = add_rounded(keep, exchange(keep, bit))
            packet.keep = self.tie(keep)
        elif step < 2 * LEVELS - 1:
            packet.keep = self.tie(jnp.concatenate([keep, arrived], 0))
        else:
            outs = open_packet(
                self.block,
                packet.pieces,
                packet.order,
                keep,
                arrived,
                [self.out.get(out) for out in packet.outs],
            )
            for out, values in zip(packet.outs, outs):
                self.out[out] = values
            self.out[packet.outs[0]] = self.tie(outs[0])

    def packet(self, name, outs, pieces, operands):
        order = ORDERS[name]
        operands = [
            x if isinstance(x, tuple) else (x, None, None, None, None) for x in operands
        ]
        operands[0] = (self.tie(operands[0][0]), *operands[0][1:])
        self.add(name, gradient_packet(self.block, pieces, order, operands), pieces, outs)

    def add(self, name, halves_of, pieces, outs):
        keep, send = halves_of
        self.packets[name] = SimpleNamespace(
            order=ORDERS[name], step=0, keep=keep, send=self.tie(send), pieces=pieces,
            outs=outs, arrived=None,
        )


def stage_text(p):
    v = p.v
    v.text_own = p.tie(v.text_own)
    v.k_cross, v.v_cross = project_text(
        v.text_own, v.text_other, v.c_key, v.c_value
    )
    v.k_cross = p.tie(v.k_cross)


def stage_tokens(p):
    v = p.v
    v.tokens = p.tie(v.tokens)
    items, frames, width = v.tokens.shape
    normed, *heads = project_tokens(
        v.tokens.reshape(items * frames, width),
        v.gain_one,
        v.bias_one,
        v.w_query,
        v.w_key,
        v.w_value,
    )
    v.normed_one = normed
    v.q_self, v.k_self, v.v_self = [x.reshape(items, frames, -1) for x in heads]
    v.q_self = p.tie(v.q_self)


def stage_self(p):
    v = p.v
    v.q_self = p.tie(v.q_self)
    v.mix_self, v.lse_self, v.attn_own, send = self_forward(
        p.rank, v.frame_valid, v.q_self, v.k_self, v.v_self, v.w_out
    )
    v.attn_other = swap_cores(send)
    v.attn_own = p.tie(v.attn_own)


def stage_norm_two(p):
    v = p.v
    v.attn_own = p.tie(v.attn_own)
    v.hidden_one, v.n2_own, v.square_attn = residual_norm(
        p.rank, v.frame_valid, v.tokens, v.attn_own, v.attn_other,
        v.gain_two, v.bias_two,
    )
    v.n2_other = swap_cores(v.n2_own)
    v.n2_own = p.tie(v.n2_own)


def stage_cross(p):
    v = p.v
    v.n2_own = p.tie(v.n2_own)
    v.q_cross, v.mix_cross, v.lse_cross, v.cross_own, send = cross_forward(
        p.rank, v.text_len, v.n2_own, v.n2_other, v.c_query,
        v.k_cross, v.v_cross, v.c_out,
    )
    v.cross_other = swap_cores(send)
    v.cross_own = p.tie(v.cross_own)


def stage_norm_three(p):
    v = p.v
    v.cross_own = p.tie(v.cross_own)
    v.hidden_two, v.n3_own, v.square_cross = residual_norm(
        p.rank, v.frame_valid, v.hidden_one, v.cross_own, v.cross_other,
        v.gain_three, v.bias_three,
    )
    v.n3_other = swap_cores(v.n3_own)
    v.n3_own = p.tie(v.n3_own)


def flat(values):
    return values.reshape(-1, values.shape[-1])


def stage_units(p):
    v = p.v
    v.n3_own = p.tie(v.n3_own)
    units, width = v.w_down.shape
    v.activated, v.grad_up, pairs = feed_forward(
        p.block, ORDERS, flat(v.n3_own), flat(v.n3_other), flat(v.grad_own),
        flat(v.grad_other), v.w_up, v.w_down,
    )
    down = [Piece(None, units, at, LANES, None, width) for at in (0, LANES)]
    up = [
        Piece(None, width, 0, units - LANES, None, units),
        Piece(None, width, units - LANES, LANES, None, units),
    ]
    p.add(DOWN, pairs[DOWN], down[:1], [D_W_DOWN])
    p.add(UP, pairs[UP], up[:1], [D_W_UP])
    p.add(REST, pairs[REST], [down[1], up[1]], [D_W_DOWN, D_W_UP])
    v.grad_up = p.tie(v.grad_up)


HALF_TERMS = [((0, (0,)), (1, ())), ((0, (1,)), (2, ()))]


def stage_back_units(p):
    v = p.v
    v.grad_up = p.tie(v.grad_up)
    own, send = project_halves(v.grad_up, v.w_up, True)
    shape = v.hidden_two.shape
    v.gn3_own, v.gn3_other = own.reshape(shape), swap_cores(send).reshape(shape)
    v.gn3_own = p.tie(v.gn3_own)


def stage_back_three(p):
    v = p.v
    v.gn3_own = p.tie(v.gn3_own)
    v.g_h2, v.d_gain_three, v.d_bias_three, v.g_cross_own = norm_backward(
        p.rank, v.hidden_two, v.gain_three, v.gn3_own, v.gn3_other,
        v.grad_own, False,
    )
    v.g_cross_other = swap_cores(v.g_cross_own)
    v.g_cross_own = p.tie(v.g_cross_own)


def stage_out(p):
    v = p.v
    v.activated = p.tie(v.activated)
    own, send = project_halves(v.activated, v.w_down, False)
    shape = v.hidden_two.shape
    v.ff_own, v.ff_other = own.reshape(shape), swap_cores(send).reshape(shape)
    v.ff_own = p.tie(v.ff_own)


def stage_result(p):
    v = p.v
    v.ff_own = p.tie(v.ff_own)
    v.out, v.square_out, v.square_ff = finish_output(
        p.rank, v.frame_valid, v.hidden_two, v.ff_own, v.ff_other
    )
    v.out = p.tie(v.out)


def stage_back_cross(p):
    v = p.v
    v.g_cross_own = p.tie(v.g_cross_own)
    (
        v.dq_cross, v.dk_cross, v.dv_cross, v.gn2_own, send,
        v.text_grad_own, text_send,
    ) = cross_backward(
        p.rank, v.text_len, v.g_cross_own, v.g_cross_other, v.c_out,
        v.q_cross, v.k_cross, v.v_cross, v.lse_cross,
        v.c_query, v.c_key, v.c_value,
    )
    v.gn2_other = swap_cores(send)
    v.text_grad_other = swap_cores(text_send)
    v.gn2_own = p.tie(v.gn2_own)


def halves(values):
    return values.reshape(2, -1, values.shape[-1])


def stage_cross_packet(p):
    v = p.v
    items, _, _, local = v.dk_cross.shape
    depth = v.c_key.shape[0]
    width = v.c_query.shape[0]
    query_terms = [((1, ()), (0, (0,))), ((2, ()), (0, (1,)))]

    def text_terms(place):
        return [
            ((3 + half, (item,)), (place, (item, half))) for item in range(items) for half in (0, 1)
        ]

    p.packet(
        CROSS, [D_C_QUERY, D_C_KEY, D_C_VALUE],
        [
            Piece(query_terms, width, 0, local, width, local),
            Piece(text_terms(5), depth, 0, local, depth, local),
            Piece(text_terms(6), depth, 0, local, depth, local),
        ],
        [
            halves(v.dq_cross), flat(v.n2_own), flat(v.n2_other),
            v.text_own, v.text_other, v.dk_cross, v.dv_cross,
        ],
    )


def stage_back_two(p):
    v = p.v
    v.gn2_own = p.tie(v.gn2_own)
    v.g_h1, v.d_gain_two, v.d_bias_two, v.g_attn_own = norm_backward(
        p.rank, v.hidden_one, v.gain_two, v.gn2_own, v.gn2_other, v.g_h2, False
    )
    v.g_attn_other = swap_cores(v.g_attn_own)
    v.g_attn_own = p.tie(v.g_attn_own)


def stage_back_self(p):
    v = p.v
    v.g_attn_own = p.tie(v.g_attn_own)
    v.dq_self, v.dk_self, v.dv_self, v.gn1_own, send = self_backward(
        p.rank, v.frame_valid, v.g_attn_own, v.g_attn_other, v.w_out,
        v.q_self, v.k_self, v.v_self, v.lse_self,
        v.w_query, v.w_key, v.w_value,
    )
    v.gn1_other = swap_cores(send)
    v.gn1_own = p.tie(v.gn1_own)


def stage_proj_packet(p):
    v = p.v
    local, width = v.w_out.shape
    terms = [((3, (0,)), (4, ())), ((3, (1,)), (5, ()))]
    steps = width // LANES

    def streamed(name, first):
        return (flat(name), 1, (0, first), steps, LANES)

    p.packet(
        PROJ, [D_C_OUT, D_W_OUT],
        [
            Piece(HALF_TERMS, local, 0, width, local, width),
            Piece(terms, local, 0, width, local, width),
        ],
        [
            halves(v.mix_cross), streamed(v.g_cross_own, 0), streamed(v.g_cross_other, 0),
            halves(v.mix_self), streamed(v.g_attn_own, steps),
            streamed(v.g_attn_other, steps),
        ],
    )


def self_packet(p, name, grad, out):
    v = p.v
    width, local = v.w_query.shape
    piece = Piece([((0, ()), (1, ()))], width, 0, local, width, local)
    p.packet(name, [out], [piece], [v.normed_one, flat(grad)])


def stage_query_packet(p):
    self_packet(p, QUERY, p.v.dq_self, D_W_QUERY)


def stage_key_packet(p):
    self_packet(p, KEY, p.v.dk_self, D_W_KEY)


def stage_value_packet(p):
    self_packet(p, VALUE, p.v.dv_self, D_W_VALUE)


def stage_back_one(p):
    v = p.v
    v.gn1_own = p.tie(v.gn1_own)
    v.d_tokens, v.d_gain_one, v.d_bias_one = norm_backward(
        p.rank, v.tokens, v.gain_one, v.gn1_own, v.gn1_other, v.g_h1, True
    )
    v.d_tokens = p.tie(v.d_tokens)


def stage_text_grad(p):
    v = p.v
    v.text_grad_own = p.tie(v.text_grad_own)
    v.d_text = v.text_grad_own + v.text_grad_other.astype(F32)
    v.d_text = p.tie(v.d_text)


def stage_small(p):
    v = p.v
    half = v.hidden_one.shape[1]
    width = v.hidden_one.shape[2]
    own = jnp.clip(v.frame_valid - p.rank * half, 0, half).sum().astype(F32)
    rows = [
        v.d_gain_one, v.d_bias_one, v.d_gain_two, v.d_bias_two,
        v.d_gain_three, v.d_bias_three, v.square_out, v.square_attn,
        v.square_cross, v.square_ff, jnp.full((1, width), own / width, F32),
    ]
    rows.append(jnp.zeros((16 - len(rows), width), F32))
    total = p.tie(jnp.concatenate(rows, 0))
    v.small = total
    v.small_other = swap_cores(total)
    p.hops = list(range(lax.axis_size("dp").bit_length() - 1))


def stage_hop(p):
    v = p.v
    total = v.small = p.tie(v.small + v.small_other)
    if p.hops:
        v.small_other = exchange(total, p.hops.pop(0))


def stage_rms(p):
    v = p.v
    while p.hops:
        stage_hop(p)
    total = v.small + v.small_other
    width = total.shape[1]
    v.small = total[:6]
    sums = jnp.sum(total[6:11], -1)
    v.rms = jnp.sqrt(sums[:4] / (sums[4] * width))


def stage_end(p):
    p.v.rms = p.v.rms + p.token[0, :4] * 0.0


ORDERS = {
    DOWN: [2, 0, 1, 3],
    UP: [0, 1, 2, 3],
    REST: [1, 0, 2, 3],
    CROSS: [2, 1, 0, 3],
    PROJ: [1, 0, 3, 2],
    QUERY: [0, 1, 2, 3],
    KEY: [1, 0, 3, 2],
    VALUE: [0, 1, 2, 3],
}


PLAN = [
    stage_tokens, stage_self, stage_text, stage_norm_two, stage_cross, stage_norm_three,
    stage_units, REST, UP, DOWN, stage_back_units, stage_back_three, stage_back_cross, REST,
    stage_cross_packet, DOWN, UP, stage_back_two, REST, UP, CROSS, DOWN, stage_back_self, REST,
    UP, DOWN, stage_proj_packet, stage_value_packet, REST, CROSS, stage_key_packet, UP, PROJ,
    stage_query_packet, CROSS, KEY, QUERY, VALUE, DOWN, REST, REST, stage_back_one, UP,
    stage_out, UP, QUERY, REST, REST, PROJ, PROJ, QUERY, VALUE, UP, UP, stage_result, CROSS,
    DOWN, CROSS, REST, KEY, VALUE, REST, PROJ, PROJ, KEY, UP, UP, CROSS, CROSS, REST, REST,
    QUERY, DOWN, PROJ, PROJ, KEY, UP, UP, KEY, VALUE, CROSS, REST, CROSS, DOWN, QUERY, PROJ,
    REST, PROJ, KEY, KEY, QUERY, VALUE, CROSS, CROSS, QUERY, PROJ, PROJ, UP, UP, KEY, KEY, VALUE,
    VALUE, QUERY, QUERY, CROSS, CROSS, KEY, KEY, QUERY, PROJ, PROJ, DOWN, VALUE, VALUE, QUERY,
    KEY, KEY, REST, DOWN, DOWN, VALUE, VALUE, QUERY, QUERY, CROSS, CROSS, UP, VALUE, VALUE, DOWN,
    DOWN, PROJ, PROJ, QUERY, QUERY, KEY, KEY, VALUE, stage_text_grad, DOWN, DOWN, stage_small,
    stage_hop, VALUE, CROSS, stage_hop, QUERY, stage_hop, stage_hop, VALUE, DOWN, PROJ, KEY,
    stage_rms, stage_end,
]

def per_device(
    tokens,
    text_own,
    text_len,
    frame_valid,
    gain_one,
    bias_one,
    gain_two,
    bias_two,
    gain_three,
    bias_three,
    w_query,
    w_key,
    w_value,
    w_out,
    c_query,
    c_key,
    c_value,
    c_out,
    w_up,
    w_down,
    grad_own,
):
    v = SimpleNamespace()
    v.tokens = tokens
    v.text_own = text_own
    v.text_len = text_len
    v.frame_valid = frame_valid
    v.gain_one = gain_one.reshape(1, -1)
    v.bias_one = bias_one.reshape(1, -1)
    v.gain_two = gain_two.reshape(1, -1)
    v.bias_two = bias_two.reshape(1, -1)
    v.gain_three = gain_three.reshape(1, -1)
    v.bias_three = bias_three.reshape(1, -1)
    v.w_query = w_query
    v.w_key = w_key
    v.w_value = w_value
    v.w_out = w_out
    v.c_query = c_query
    v.c_key = c_key
    v.c_value = c_value
    v.c_out = c_out
    v.w_up = w_up
    v.w_down = w_down
    v.grad_own = grad_own
    p = Program(v)
    p.rank = lax.axis_index("mp").astype(jnp.int32).reshape(1)
    p.main, p.extra = main_bits()
    place = lax.axis_index("dp")
    p.block = sum(((place >> bit) & 1) << k for k, bit in enumerate(p.main))
    p.block = p.block.astype(jnp.int32).reshape(1)
    v.text_other = swap_cores(v.text_own)
    v.grad_other = swap_cores(v.grad_own)
    for action in PLAN:
        if callable(action):
            action(p)
        elif p.packets[action].arrived is None:
            p.start(action)
        else:
            p.finish(action)
    return (
        v.out,
        v.d_tokens,
        v.d_text,
        *(v.small[n] for n in range(6)),
        *(p.out[name] for name in range(10)),
        v.rms,
    )


def solution(mesh):
    split = P("dp", "mp", None)
    columns, rows = P(None, "mp"), P("mp", None)
    weights = (columns,) * 3 + (rows,) + (columns,) * 3 + (rows, columns, rows)
    return jax.shard_map(
        per_device,
        mesh=mesh,
        in_specs=(P("dp", None, None), split, P("dp"), P("dp"))
        + (P(),) * 6
        + weights
        + (split,),
        out_specs=(split,) * 3 + (P(),) * 6 + weights + (P(),),
        check_vma=False,
    )
```
